32 devices in a mesh: ha: 4 (over x, core), wa: 8 (over z, y).
Axes of the slice: x: 2, y: 2, z: 4, core: 2. Of those that a mesh axis runs over, the one named last changes fastest.
Arguments:
- tokens: bfloat16 [1, 8, 32, 16, 1152], P(None, None, 'ha', 'wa'), may hold values from -36 to 36
- cotangent: bfloat16 [1, 8, 32, 16, 1152], P(None, None, 'ha', 'wa'), may hold values from -6 to 6
- w_qkv: bfloat16 [3, 1152, 1728], P(None, 'wa'), may hold values from -0.1875 to 0.1875
- w_out: bfloat16 [3, 576, 1152], P(None, 'wa'), may hold values from -0.25 to 0.25
- gains: float32 [3, 1152], replicated, may hold values from 0.1 to 1.9
- gates: float32 [3, 8], replicated, may hold values from 0.5 to 2
Outputs:
- token_grad: bfloat16 [1, 8, 32, 16, 1152], P(None, None, 'ha', 'wa')
- head_sens: bfloat16 [1, 3, 8, 32, 16, 8], P(None, None, None, 'ha', 'wa')
The draws below stay inside these ranges and needn't reach their ends.
All inputs are finite; a program needn't handle non-finite values.
Results may differ from the reference program's by a relative error of at most 0.02.
Values may be sent and summed in bfloat16 or wider, within the bound.
No kernel may reach another device: no remote copies, remote signals or barrier semaphores. Data moves between devices by JAX's collectives and lax.ppermute only.
A program may use at most 128 MiB of HBM per device.

```python
import math
import jax
import jax.numpy as jnp
from jax import lax

D = 1152
HEADS = 8
F = 8
B = 1
H = 32
W = 16
HD = 576


def draw_tokens(key, part):
    pieces = jax.random.split(jax.random.fold_in(key, 11), 3)
    full_shape = (B, F, H, W, D)
    row_scale = jnp.exp(jax.random.uniform(pieces[0], (B, F, H, W, 1), minval=math.log(0.3), maxval=math.log(3.0)))
    column_scale = jnp.exp(jax.random.uniform(pieces[1], (D,), minval=math.log(0.3), maxval=math.log(3.0)))
    base_draw = jnp.clip(jax.random.normal(pieces[2], full_shape), -4.0, 4.0)
    return (base_draw * row_scale * column_scale).astype(jnp.bfloat16)


def shard_levels(own_key, dims, cuts, low, top_value):
    level, own = 1.0, jax.random.fold_in(own_key, 6)
    for dim, shards_of in cuts:
        steps = jnp.exp(jax.random.uniform(jax.random.fold_in(own, dim), (shards_of,), jnp.float32, low / len(cuts), top_value / len(cuts)))
        level = level * jnp.repeat(steps, dims[dim] // shards_of).reshape([-1 if axis == dim else 1 for axis in range(len(dims))])
    return level


def noise(own_key, shape, width, reach, cuts=(), dtype=jnp.bfloat16):
    drawn = jax.random.normal(own_key, shape, jnp.float32) * width
    if len(cuts) > 0:
        drawn = shard_levels(own_key, shape, cuts, -0.22, 0.18) * drawn
    return jnp.clip(drawn, min=-reach, max=reach).astype(dtype)


def setup_inputs(seed: int = 0) -> dict:
    keys = jax.random.split(jax.random.key(seed), 7)
    tokens = draw_tokens(jax.random.fold_in(keys[6], 71), 0)
    cotangent = noise(keys[1], (B, F, H, W, D), 1.0, 6.0, ((2, 4), (3, 8)))
    w_qkv = noise(keys[2], (3, D, 3 * HD), D ** -0.5, 0.1875, ((1, 8),))
    w_out = noise(keys[3], (3, HD, D), HD ** -0.5, 0.25, ((1, 8),))
    gains = jnp.clip(1.0 + 0.18 * jax.random.normal(keys[4], (3, D), jnp.float32), 0.1, 1.9)
    gates = jnp.clip(jnp.exp(jax.random.uniform(keys[5], (3, HEADS), jnp.float32, math.log(0.5), math.log(2.0))), 0.5, 2.0)
    return dict(tokens=tokens, cotangent=cotangent, w_qkv=w_qkv, w_out=w_out, gains=gains, gates=gates)


def letter_forms(attend_axis):
    letters = 'bfhw'
    query_side = letters + 'nc'
    key_side = letters[:attend_axis] + 'g' + letters[attend_axis + 1:] + 'nc'
    score_side = letters[:attend_axis] + letters[attend_axis + 1:] + 'n' + letters[attend_axis] + 'g'
    return (query_side + ',' + key_side + '->' + score_side, score_side + ',' + key_side + '->' + query_side, score_side + ',' + query_side + '->' + key_side)

def product(form, left, right):
    return jnp.einsum(form, left.astype(jnp.float32), right.astype(jnp.float32))

def forward_sublayer(inputs, w_qkv, w_out, gain, gate, attend_axis):
    scores_form, mixing_form, keyward_form = letter_forms(attend_axis)
    heads = gate.shape[0]
    hidden = w_out.shape[0]
    head_dim = hidden // heads
    leading = inputs.shape[:4]
    inputs_f = inputs.astype(jnp.float32)
    inverse = lax.rsqrt(lax.optimization_barrier(jnp.mean(inputs_f * inputs_f, axis=-1, keepdims=True)) + 1e-06)
    normed = (inputs_f * inverse * gain).astype(jnp.bfloat16)
    projected = jnp.dot(normed, w_qkv, preferred_element_type=jnp.float32).astype(jnp.bfloat16)
    split = projected.reshape(leading + (3, heads, head_dim))
    queries = split[..., 0, :, :]
    keys_all = split[..., 1, :, :]
    values = split[..., 2, :, :]
    scores = product(scores_form, queries, keys_all) * head_dim ** (-0.5)
    raised = jnp.exp(scores)
    probs = raised / lax.optimization_barrier(jnp.sum(raised, axis=-1, keepdims=True))
    probs_half = probs.astype(jnp.bfloat16)
    attended = product(mixing_form, probs_half, values).astype(jnp.bfloat16)
    gated = (attended.astype(jnp.float32) * gate[:, None]).astype(jnp.bfloat16).reshape(leading + (hidden,))
    outputs = (inputs_f + jnp.dot(gated, w_out, preferred_element_type=jnp.float32)).astype(jnp.bfloat16)
    return (outputs, (inverse, queries, keys_all, values, probs, probs_half, attended))

def backward_sublayer(outgrad, inputs, saved, w_qkv, w_out, gain, gate, attend_axis):
    scores_form, mixing_form, keyward_form = letter_forms(attend_axis)
    inverse, queries, keys_all, values, probs, probs_half, attended = saved
    heads = gate.shape[0]
    hidden = w_out.shape[0]
    head_dim = hidden // heads
    leading = inputs.shape[:4]
    d_gated = jnp.dot(outgrad, w_out.T, preferred_element_type=jnp.float32).astype(jnp.bfloat16)
    d_gated = d_gated.reshape(leading + (heads, head_dim))
    sens = lax.optimization_barrier(jnp.sum(d_gated.astype(jnp.float32) * attended.astype(jnp.float32), axis=-1)).astype(jnp.bfloat16)
    d_attended = (d_gated.astype(jnp.float32) * gate[:, None]).astype(jnp.bfloat16)
    d_probs = product(scores_form, d_attended, values)
    d_values = product(keyward_form, probs_half, d_attended)
    d_scores = (probs * (d_probs - lax.optimization_barrier(jnp.sum(d_probs * probs, axis=-1, keepdims=True))) * head_dim ** (-0.5)).astype(jnp.bfloat16)
    d_queries = product(mixing_form, d_scores, keys_all)
    d_keys = product(keyward_form, d_scores, queries)
    d_proj = jnp.stack([d_queries, d_keys, d_values], axis=4).reshape(leading + (3 * hidden,)).astype(jnp.bfloat16)
    d_normed = jnp.dot(d_proj, w_qkv.T, preferred_element_type=jnp.float32) * gain
    inputs_f = inputs.astype(jnp.float32)
    ingrad = outgrad.astype(jnp.float32) + inverse * d_normed - inputs_f * inverse * inverse * inverse * lax.optimization_barrier(jnp.mean(inputs_f * d_normed, axis=-1, keepdims=True))
    return (ingrad.astype(jnp.bfloat16), sens)

def reference(tokens, cotangent, w_qkv, w_out, gains, gates):

    def one_video(pair):
        video = pair[0][None]
        video_cot = pair[1][None]
        after_time, saved_time = forward_sublayer(video, w_qkv[0], w_out[0], gains[0], gates[0], 1)
        after_height, saved_height = forward_sublayer(after_time, w_qkv[1], w_out[1], gains[1], gates[1], 2)
        unused_out, saved_width = forward_sublayer(after_height, w_qkv[2], w_out[2], gains[2], gates[2], 3)
        grad_width, sens_width = backward_sublayer(video_cot, after_height, saved_width, w_qkv[2], w_out[2], gains[2], gates[2], 3)
        grad_height, sens_height = backward_sublayer(grad_width, after_time, saved_height, w_qkv[1], w_out[1], gains[1], gates[1], 2)
        grad_time, sens_time = backward_sublayer(grad_height, video, saved_time, w_qkv[0], w_out[0], gains[0], gates[0], 1)
        return (grad_time[0], jnp.stack([sens_time[0], sens_height[0], sens_width[0]], axis=0))
    token_grad, head_sens = lax.map(one_video, (tokens, cotangent))
    return (token_grad, head_sens)
```

```python
import functools

import jax
import jax.numpy as jnp
from jax import lax
from jax.experimental import pallas as pl
from jax.experimental.pallas import tpu as pltpu
from jax.sharding import PartitionSpec as P

LANES = 128
ROWS = 16
AXES = ("ha", "wa")
NT = (((1,), (1,)), ((), ()))
TN = (((0,), (0,)), ((), ()))


def ceil_to(value, unit):
    return -(-value // unit) * unit


def tile_qkv(w):
    lead, (rows, cols) = w.shape[:-2], w.shape[-2:]
    wide = ceil_to(cols, LANES)
    w = jnp.pad(w, [(0, 0)] * (len(lead) + 1) + [(0, wide - cols)])
    w = w.reshape(lead + (rows // ROWS, ROWS, wide // LANES, LANES))
    return jnp.moveaxis(w, -2, -4)


def tile_out(w):
    lead, (rows, cols) = w.shape[:-2], w.shape[-2:]
    tall = ceil_to(rows, ROWS)
    w = jnp.pad(w, [(0, 0)] * len(lead) + [(0, tall - rows), (0, 0)])
    w = w.reshape(lead + (tall // ROWS, ROWS, cols // LANES, LANES))
    return jnp.swapaxes(w, -3, -2)


class Routes:
    def __init__(self, n_ha, n_wa):
        self.n_ha, self.n_wa = n_ha, n_wa

    def send(self, value, ha_bits=0, wa_bits=0, only_core=None):
        pairs = []
        for a in range(self.n_ha):
            for b in range(self.n_wa):
                if only_core is None or a % 2 == only_core:
                    source = a * self.n_wa + b
                    target = (a ^ ha_bits) * self.n_wa + (b ^ wa_bits)
                    pairs.append((source, target))
        return lax.ppermute(value, AXES, pairs)

    def y(self, value):
        return self.send(value, wa_bits=1)

    def z(self, value, k):
        return self.send(value, wa_bits=2 * k)

    def x(self, value, core):
        return self.send(value, ha_bits=2, only_core=core)

    def core(self, value):
        return self.send(value, ha_bits=1)

    def core_from(self, value, core):
        return self.send(value, ha_bits=1, only_core=core)


def spread(routes, groups, part, core_of):
    out = []
    for (buffer, offsets), home in zip(groups, core_of):
        other = routes.core(buffer)
        out.append((buffer, None, offsets, 0, 0))
        out.append((other, None, offsets, 1, 0))
        across = routes.x(buffer if home == 1 else other, home)
        copied = routes.core_from(across, home)
        out.append((across, copied, offsets, 2, home))
    return out


def gather_early(routes, own):
    r1 = routes.z(own, 1)
    ry = routes.y(own)
    far = [routes.z(own, k) for k in range(2, routes.n_wa // 2)]
    ry1 = routes.y(r1)
    near = jnp.stack([r1, ry, ry1])
    far_own = jnp.stack(far)
    far_y = routes.y(far_own)
    ks = range(2, routes.n_wa // 2)
    groups = [
        (near, [2, 1, 3]),
        (far_own, [2 * k for k in ks]),
        (far_y, [2 * k + 1 for k in ks]),
    ]
    return spread(routes, groups, None, (1, 0, 1))


def gather_late(routes, own):
    stack = own[None]
    k = 1
    while 2 * k < routes.n_wa:
        stack = jnp.concatenate([stack, routes.z(stack, k)])
        k *= 2
    across = routes.y(stack)
    n = stack.shape[0]
    groups = [
        (stack, [2 * k for k in range(n)]),
        (across, [2 * k + 1 for k in range(n)]),
    ]
    return spread(routes, groups, None, (1, 0))


def load_weights(plan, place_ref, refs, sems, w_scr, o_scr, start):
    count = [0]

    def move(src, dst):
        copy = pltpu.make_async_copy(src, dst, sems.at[count[0]])
        count[0] += 1
        if start:
            copy.start()
        else:
            copy.wait()

    if plan["full"]:
        move(refs[0], w_scr)
        move(refs[1], o_scr)
        return
    tiles, rg, og, ot = plan["tiles"], plan["rg"], plan["og"], plan["ot"]

    def put(src, slot, part):
        move(src.at[pl.ds(0, tiles)], w_scr.at[:, pl.ds(slot * 3 * rg + part * rg, rg)])
        move(src.at[pl.ds(tiles, og)], o_scr.at[slot, :, pl.ds(part * ot, ot)])

    own_ref = refs[0]
    for part in range(3):
        put(own_ref.at[part], place_ref[0], part)
    at = 1
    for offsets, kind, home, double in plan["groups"]:
        if not double:
            for i, offset in enumerate(offsets):
                if offset != 0:
                    put(refs[at].at[i], place_ref[offset], place_ref[plan["n_wa"] + kind])
            at += 1
        else:
            here, there = refs[at], refs[at + 1]
            base = count[0]
            for ref, cond in ((here, True), (there, False)):
                count[0] = base
                at_home = place_ref[plan["n_wa"] + 3] == home

                @pl.when(at_home if cond else jnp.logical_not(at_home))
                def _():
                    for i, offset in enumerate(offsets):
                        if offset != 0:
                            put(ref.at[i], place_ref[offset], place_ref[plan["n_wa"] + kind])

            at += 2


def dims_of(plan):
    return plan["T"], plan["D"], plan["heads"], plan["hd"], plan["tiles"] * LANES


def project(plan, x, gain, w_scr, proj_scr):
    T, D, heads, hd, wide = dims_of(plan)
    xf = x.astype(jnp.float32)
    inverse = lax.rsqrt(jnp.mean(xf * xf, axis=-1, keepdims=True) + 1e-06)
    normed = (xf * inverse * gain).astype(jnp.bfloat16)
    for j in range(0, plan["tiles"], 2):
        js = range(j, min(j + 2, plan["tiles"]))
        w = jnp.concatenate([w_scr[i].reshape(D, LANES) for i in js], axis=1)
        proj_scr[:, j * LANES : j * LANES + LANES * len(js)] = jnp.dot(
            normed, w, preferred_element_type=jnp.float32
        ).astype(jnp.bfloat16)
    return inverse


def qkv_of(plan, proj_ref, h):
    hd, hidden = plan["hd"], plan["heads"] * plan["hd"]
    return [proj_ref[:, m * hidden + h * hd : m * hidden + (h + 1) * hd] for m in range(3)]


def attend(plan, h, proj_ref, bias):
    q, k, v = qkv_of(plan, proj_ref, h)
    scores = lax.dot_general(q, k, NT, preferred_element_type=jnp.float32)
    raised = jnp.exp(scores * plan["hd"] ** (-0.5) + bias)
    probs = raised / jnp.sum(raised, axis=-1, keepdims=True)
    attended = jnp.dot(probs.astype(jnp.bfloat16), v, preferred_element_type=jnp.float32)
    return probs, attended.astype(jnp.bfloat16)


def fwd_kernel(plan, place_ref, gates_ref, x_ref, gain_ref, bias_ref, *rest):
    n = plan["n_refs"]
    refs, rest = rest[:n], rest[n:]
    y_ref, proj_ref, probs_ref, att_ref, inv_ref, w_scr, o_scr, gated_scr, sems = rest
    T, D, heads, hd, wide = dims_of(plan)
    layer, stride = plan["layer"], plan["og"] * ROWS
    load_weights(plan, place_ref, refs, sems, w_scr, o_scr, True)
    load_weights(plan, place_ref, refs, sems, w_scr, o_scr, False)
    x = x_ref[...]
    inv_ref[...] = project(plan, x, gain_ref[layer : layer + 1, :], w_scr, proj_ref)
    bias = bias_ref[...]
    gated_scr[...] = jnp.zeros_like(gated_scr)
    for h in range(heads):
        probs, attended = attend(plan, h, proj_ref, bias)
        probs_ref[h] = probs
        att_ref[:, h * hd : (h + 1) * hd] = attended
        gated = (attended.astype(jnp.float32) * gates_ref[layer, h]).astype(jnp.bfloat16)
        gated_scr[:, h * stride : h * stride + hd] = gated
    gated = gated_scr[...]
    lane_tiles = D // LANES
    for j in range(0, lane_tiles, 2):
        js = range(j, min(j + 2, lane_tiles))
        w = jnp.concatenate([o_scr[:, :, i].reshape(heads * stride, LANES) for i in js], axis=1)
        cols = slice(j * LANES, j * LANES + LANES * len(js))
        y_ref[:, cols] = (
            x_ref[:, cols].astype(jnp.float32)
            + jnp.dot(gated, w, preferred_element_type=jnp.float32)
        ).astype(jnp.bfloat16)


def backward(plan, gates_ref, outgrad_ref, x_ref, gain, inverse, proj_ref, probs_of, att_of,
             w_scr, o_scr, dgated_scr, dproj_scr, g_ref):
    T, D, heads, hd, wide = dims_of(plan)
    layer, stride, hidden = plan["layer"], plan["og"] * ROWS, heads * hd
    lane_tiles = D // LANES
    outgrad = outgrad_ref[:, :D]
    rows = heads * stride
    for r in range(0, heads, 2):
        hs = min(2, heads - r)
        w = jnp.concatenate(
            [o_scr[r : r + hs, :, i].reshape(hs * stride, LANES) for i in range(lane_tiles)],
            axis=1,
        )
        out = lax.dot_general(outgrad, w, NT, preferred_element_type=jnp.float32)
        dgated_scr[:, r * stride : (r + hs) * stride] = out.astype(jnp.bfloat16)
    if wide > 3 * hidden:
        dproj_scr[:, wide - LANES :] = jnp.zeros((T, LANES), jnp.bfloat16)
    lane = lax.broadcasted_iota(jnp.int32, (T, LANES), 1)
    sens = jnp.zeros((T, LANES), jnp.float32)
    if plan["carry"]:
        sens = outgrad_ref[:, D : D + LANES].astype(jnp.float32)
    for h in range(heads):
        q, k, v = qkv_of(plan, proj_ref, h)
        probs = probs_of(h)
        dgated = dgated_scr[:, h * stride : h * stride + hd].astype(jnp.float32)
        own = jnp.sum(dgated * att_of(h).astype(jnp.float32), axis=-1, keepdims=True)
        sens = jnp.where(lane == layer * heads + h, own, sens)
        datt = (dgated * gates_ref[layer, h]).astype(jnp.bfloat16)
        dprobs = lax.dot_general(datt, v, NT, preferred_element_type=jnp.float32)
        dvalues = lax.dot_general(
            probs.astype(jnp.bfloat16), datt, TN, preferred_element_type=jnp.float32
        )
        inner = jnp.sum(dprobs * probs, axis=-1, keepdims=True)
        dscores = (probs * (dprobs - inner) * hd ** (-0.5)).astype(jnp.bfloat16)
        dqueries = jnp.dot(dscores, k, preferred_element_type=jnp.float32)
        dkeys = lax.dot_general(dscores, q, TN, preferred_element_type=jnp.float32)
        for m, d in enumerate((dqueries, dkeys, dvalues)):
            at = m * hidden + h * hd
            dproj_scr[:, at : at + hd] = d.astype(jnp.bfloat16)
    g_ref[:, D : D + LANES] = sens.astype(jnp.bfloat16)
    dproj = dproj_scr[...]
    step = 2 * LANES
    groups = w_scr.shape[1]
    parts = []
    for r in range(0, D, step):
        rr = min(step, D - r)
        w = jnp.concatenate(
            [
                w_scr[i, r // ROWS : (r + rr) // ROWS].reshape(rr, LANES)
                for i in range(plan["tiles"])
            ],
            axis=1,
        )
        parts.append(lax.dot_general(dproj, w, NT, preferred_element_type=jnp.float32))
    dnormed = jnp.concatenate(parts, axis=1) * gain
    xf = x_ref[...].astype(jnp.float32)
    mean = jnp.mean(xf * dnormed, axis=-1, keepdims=True)
    ingrad = (
        outgrad.astype(jnp.float32)
        + inverse * dnormed
        - xf * (inverse * inverse * inverse) * mean
    )
    g_ref[:, :D] = ingrad.astype(jnp.bfloat16)


def both_kernel(plan, place_ref, gates_ref, x_ref, gain_ref, bias_ref, outgrad_ref, *rest):
    n = plan["n_refs"]
    refs, rest = rest[:n], rest[n:]
    g_ref, w_scr, o_scr, proj_scr, probs_scr, att_scr, dgated_scr, dproj_scr, sems = rest
    T, D, heads, hd, wide = dims_of(plan)
    layer = plan["layer"]
    load_weights(plan, place_ref, refs, sems, w_scr, o_scr, True)
    load_weights(plan, place_ref, refs, sems, w_scr, o_scr, False)
    gain = gain_ref[layer : layer + 1, :]
    inverse = project(plan, x_ref[...], gain, w_scr, proj_scr)
    bias = bias_ref[...]
    for h in range(heads):
        probs, attended = attend(plan, h, proj_scr, bias)
        probs_scr[h] = probs
        att_scr[:, h * hd : (h + 1) * hd] = attended
    backward(
        plan, gates_ref, outgrad_ref, x_ref, gain, inverse, proj_scr,
        lambda h: probs_scr[h], lambda h: att_scr[:, h * hd : (h + 1) * hd],
        w_scr, o_scr, dgated_scr, dproj_scr, g_ref,
    )


def bwd_kernel(plan, place_ref, gates_ref, x_ref, gain_ref, outgrad_ref, proj_ref, probs_ref,
               att_ref, inv_ref, *rest):
    n = plan["n_refs"]
    refs, rest = rest[:n], rest[n:]
    g_ref, w_scr, o_scr, dgated_scr, dproj_scr, sems = rest
    layer, hd = plan["layer"], plan["hd"]
    load_weights(plan, place_ref, refs, sems, w_scr, o_scr, True)
    load_weights(plan, place_ref, refs, sems, w_scr, o_scr, False)
    backward(
        plan, gates_ref, outgrad_ref, x_ref, gain_ref[layer : layer + 1, :], inv_ref[...],
        proj_ref, lambda h: probs_ref[h], lambda h: att_ref[:, h * hd : (h + 1) * hd],
        w_scr, o_scr, dgated_scr, dproj_scr, g_ref,
    )


def call(kernel, plan, place, gates, arrays, weights, outs, scratch, flops):
    vmem = pl.BlockSpec(memory_space=pltpu.VMEM)
    smem = pl.BlockSpec(memory_space=pltpu.SMEM)
    plan = dict(plan, n_refs=len(weights))
    D, heads = plan["D"], plan["heads"]
    w_shape = (plan["tiles"], D // ROWS, ROWS, LANES)
    o_shape = (heads, plan["og"], D // LANES, ROWS, LANES)
    n_sems = 2 * 3 * plan["n_wa"] + 2
    return pl.pallas_call(
        functools.partial(kernel, plan),
        out_shape=outs,
        in_specs=[smem, smem] + [vmem] * len(arrays) + [pl.BlockSpec(memory_space=pl.ANY)] * len(weights),
        out_specs=jax.tree.map(lambda _: vmem, outs),
        scratch_shapes=[pltpu.VMEM(w_shape, jnp.bfloat16), pltpu.VMEM(o_shape, jnp.bfloat16)]
        + scratch
        + [pltpu.SemaphoreType.DMA((n_sems,))],
        compiler_params=pltpu.CompilerParams(vmem_limit_bytes=40 * 1024 * 1024),
        cost_estimate=pl.CostEstimate(flops=flops, bytes_accessed=6 * 1024 * 1024, transcendentals=0),
    )(place, gates, *arrays, *weights)


def per_device(n_ha, n_wa, tokens, cotangent, w_qkv, w_out, gains, gates):
    videos, frames, rows, cols, D = tokens.shape
    layers, heads = gates.shape
    T = videos * frames * rows * cols
    width = w_qkv.shape[2]
    hidden = width // 3
    hd = hidden // heads
    tiles = ceil_to(width, LANES) // LANES
    og = ceil_to(hd, ROWS) // ROWS
    lane_tiles = D // LANES
    wide = tiles * LANES

    def flat(value):
        return jnp.swapaxes(value, 0, 1).reshape(T, D)

    idx = jnp.arange(T)
    fl = frames // n_ha * videos
    lines = [
        idx % (videos * rows * cols),
        (idx // (rows * cols)) % fl * cols + idx % cols,
        (idx // cols) % (T // (n_wa * cols)),
    ]
    biases = [jnp.where(line[:, None] == line[None, :], 0.0, -1e30).astype(jnp.float32) for line in lines]

    shard = w_qkv.shape[1]
    fast = (
        n_ha % 4 == 0
        and n_wa % 4 == 0
        and n_wa & (n_wa - 1) == 0
        and shard % (3 * ROWS) == 0
        and w_out.shape[1] == hd
        and lane_tiles % 3 == 0
    )
    ha, wa = lax.axis_index("ha"), lax.axis_index("wa")
    base = dict(T=T, D=D, heads=heads, hd=hd, tiles=tiles, og=og, n_wa=n_wa, carry=False)
    weights, plans = [], []
    if fast:
        rg, ot = shard // (3 * ROWS), lane_tiles // 3
        core, xbit = ha % 2, (ha // 2) % 2
        part = jnp.where(core == 0, 0, 1 + xbit)
        part_core = jnp.where(core == 0, 1 + xbit, 0)
        place = jnp.stack(
            [wa ^ offset for offset in range(n_wa)] + [part, part_core, 2 - xbit, core]
        ).astype(jnp.int32)
        routes = Routes(n_ha, n_wa)
        for layer in range(layers):
            thirds_q = tile_qkv(w_qkv[layer].reshape(3, shard // 3, width))
            thirds_o = tile_out(w_out[layer]).reshape(og, 3, ot, ROWS, LANES)
            thirds_o = jnp.swapaxes(thirds_o, 0, 1)
            own = jnp.concatenate([thirds_q, thirds_o], axis=1)
            mine = lax.dynamic_index_in_dim(own, part, 0, keepdims=False)
            groups = (gather_early if layer == 0 else gather_late)(routes, mine)
            arrays, meta = [own], []
            for here, there, offsets, kind, home in groups:
                arrays += [here] if there is None else [here, there]
                meta.append((offsets, kind, home, there is not None))
            weights.append(arrays)
            plans.append(dict(base, full=False, layer=layer, rg=rg, ot=ot, groups=meta))
    else:
        place = jnp.zeros((1,), jnp.int32)
        full_qkv = lax.all_gather(w_qkv, "wa", axis=1, tiled=True)
        full_out = lax.all_gather(w_out, "wa", axis=1, tiled=True)
        for layer in range(layers):
            weights.append([tile_qkv(full_qkv[layer]), tile_out(full_out[layer].reshape(heads, hd, D))])
            plans.append(dict(base, full=True, layer=layer))

    def swap(value, axis):
        return lax.all_to_all(value, axis, split_axis=0, concat_axis=0, tiled=True)

    bf16, f32 = jnp.bfloat16, jnp.float32
    act = jax.ShapeDtypeStruct((T, D), bf16)
    loaded = jax.ShapeDtypeStruct((T, D + LANES), bf16)
    dense = 2 * T * D * (width + hidden)

    def forward(layer, x):
        return call(
            fwd_kernel, plans[layer], place, gates, [x, gains, biases[layer]], weights[layer],
            [
                act,
                jax.ShapeDtypeStruct((T, wide), bf16),
                jax.ShapeDtypeStruct((heads, T, T), f32),
                jax.ShapeDtypeStruct((T, hidden), bf16),
                jax.ShapeDtypeStruct((T, 1), f32),
            ],
            [pltpu.VMEM((T, heads * og * ROWS), bf16)],
            dense,
        )

    grads = [pltpu.VMEM((T, heads * og * ROWS), bf16), pltpu.VMEM((T, wide), bf16)]

    def back(layer, x, outgrad, saved):
        return call(
            bwd_kernel, dict(plans[layer], carry=True), place, gates, [x, gains, outgrad] + list(saved),
            weights[layer], loaded, grads, dense,
        )

    home = flat(tokens)
    cot = swap(swap(flat(cotangent), "ha"), "wa")
    after_time, *saved_time = forward(0, home)
    tall = swap(after_time, "ha")
    after_height, *saved_height = forward(1, tall)
    across = swap(after_height, "wa")
    grad = call(
        both_kernel, plans[2], place, gates, [across, gains, biases[2], cot], weights[2], loaded,
        [
            pltpu.VMEM((T, wide), bf16),
            pltpu.VMEM((heads, T, T), f32),
            pltpu.VMEM((T, hidden), bf16),
        ]
        + grads,
        2 * dense,
    )
    grad = back(1, tall, swap(grad, "wa"), saved_height)
    grad = back(0, home, swap(grad, "ha"), saved_time)

    def unflat(value):
        value = value.reshape(frames, videos, rows, cols, value.shape[-1])
        return jnp.swapaxes(value, 0, 1)

    token_grad = unflat(grad[:, :D])
    sens = unflat(grad[:, D : D + layers * heads]).reshape(videos, frames, rows, cols, layers, heads)
    return (token_grad, jnp.moveaxis(sens, 4, 1))


def solution(mesh):
    spec = P(None, None, "ha", "wa", None)
    in_specs = (spec, spec, P(None, "wa", None), P(None, "wa", None), P(), P())
    out_specs = (spec, P(None, None, None, "ha", "wa", None))
    n_ha, n_wa = mesh.shape["ha"], mesh.shape["wa"]
    return jax.shard_map(
        functools.partial(per_device, n_ha, n_wa),
        mesh=mesh, in_specs=in_specs, out_specs=out_specs, check_vma=False,
    )
```

```python
import functools

import jax
import jax.numpy as jnp
from jax import lax
from jax.experimental import pallas as pl
from jax.experimental.pallas import tpu as pltpu
from jax.sharding import PartitionSpec as P

LANES = 128
ROWS = 16
AXES = ("ha", "wa")
NT = (((1,), (1,)), ((), ()))
TN = (((0,), (0,)), ((), ()))


def ceil_to(value, unit):
    return -(-value // unit) * unit


def blocks_of(w):
    rows, cols = w.shape
    tall, wide = ceil_to(rows, ROWS), ceil_to(cols, LANES)
    w = jnp.pad(w, [(0, tall - rows), (0, wide - cols)])
    return jnp.moveaxis(w.reshape(tall // ROWS, ROWS, wide // LANES, LANES), 2, 0)


def flat_blocks(*arrays):
    return jnp.concatenate([a.reshape(-1, ROWS, LANES) for a in arrays])


HBM = pl.BlockSpec(memory_space=pltpu.HBM)


def hand_on(value, *after):
    def nothing(*refs):
        del refs

    return pl.pallas_call(
        nothing,
        out_shape=jax.ShapeDtypeStruct(value.shape, value.dtype),
        in_specs=[HBM] * (1 + len(after)),
        out_specs=HBM,
        input_output_aliases={0: 0},
        compiler_params=pltpu.CompilerParams(vmem_limit_bytes=60 * 2**20),
    )(value, *after)


class Routes:
    def __init__(self, n_ha, n_wa):
        self.n_ha, self.n_wa = n_ha, n_wa

    def send(self, value, ha_bits=0, wa_bits=0):
        pairs = [
            (a * self.n_wa + b, (a ^ ha_bits) * self.n_wa + (b ^ wa_bits))
            for a in range(self.n_ha)
            for b in range(self.n_wa)
        ]
        return lax.ppermute(value, AXES, pairs)

    def core(self, value):
        return self.send(value, ha_bits=1)

    def x(self, value):
        return self.send(value, ha_bits=2)

    def y(self, value):
        return self.send(value, wa_bits=1)

    def line(self, value):
        groups = [
            [a * self.n_wa + 2 * z + y for z in range(self.n_wa // 2)]
            for a in range(self.n_ha)
            for y in range(2)
        ]
        return lax.all_gather(value, AXES, axis=0, tiled=True, axis_index_groups=groups)


def over_square(routes, line, before, between):
    half = line.shape[0] // 2
    over_y, over_x = routes.y(line), routes.x(line)
    over_y, over_x = hand_on(over_y, *before), hand_on(over_x, *before)
    low, high = routes.y(over_x[:half]), routes.x(over_y[half:])
    there = between(over_y, over_x)
    low, high = hand_on(low, *there), hand_on(high, *there)
    mine = [hand_on(line, over_y, over_x), over_y, over_x, low, high]
    return mine + [routes.core(piece) for piece in mine]


def stack_kernel(n, slot_ref, *refs):
    ins, outs, held, sems = refs[:n], refs[n:-2], refs[-2], refs[-1]
    rows = held.shape[2]
    reads, writes = [], []
    for j, out in enumerate(outs):
        for i in range(n):
            slot = pl.ds(slot_ref[i] * rows, rows)
            piece = ins[i].at[pl.ds(j * rows, rows)]
            reads.append(pltpu.make_async_copy(piece, held.at[j, i], sems.at[0, j, i]))
            writes.append(pltpu.make_async_copy(held.at[j, i], out.at[slot], sems.at[1, j, i]))
    for read in reads:
        read.start()
    for read, write in zip(reads, writes):
        read.wait()
        write.start()
    for write in writes:
        write.wait()


def stacked(slots, arrays, outs, after):
    n, rows = len(arrays), arrays[0].shape[0] // outs
    anywhere = pl.BlockSpec(memory_space=pl.ANY)
    line = jax.ShapeDtypeStruct((n * rows, ROWS, LANES), jnp.bfloat16)
    return pl.pallas_call(
        lambda *refs: stack_kernel(n, *refs[: n + 1], *refs[n + 1 + len(after) :]),
        out_shape=[line] * outs,
        in_specs=[pl.BlockSpec(memory_space=pltpu.SMEM)] + [anywhere] * (n + len(after)),
        out_specs=[anywhere] * outs,
        scratch_shapes=[
            pltpu.VMEM((outs, n, rows, ROWS, LANES), jnp.bfloat16),
            pltpu.SemaphoreType.DMA((2, outs, n)),
        ],
        compiler_params=pltpu.CompilerParams(vmem_limit_bytes=60 * 2**20),
    )(slots, *arrays, *after)


def w_tile(plan, ref, tile, first=0, count=None):
    count = plan["D"] // ROWS - first if count is None else count
    return jnp.concatenate([ref[plan["w_at"](g, tile)] for g in range(first, first + count)], axis=0)


def o_tile(plan, ref, tile, heads):
    return jnp.concatenate(
        [ref[plan["o_at"](h, g, tile)] for h in heads for g in range(plan["og"])], axis=0
    )


class Weights:
    def __init__(self, plan, place_ref, refs, w_scr, sems, order):
        self.plan, self.w_scr, self.sems, self.here = plan, w_scr, sems, set()
        n_parts = plan["n_parts"]
        self.rows = w_scr.shape[0] // n_parts
        if not plan["square"]:
            for part in order if n_parts > 1 else [0]:
                self.copy(refs[0].at[pl.ds(part * self.rows, self.rows)], part * self.rows, part)
            return
        pieces = []
        for c in range(2):
            for which, ref in enumerate(refs[5 * c : 5 * c + 5]):
                spot = place_ref[4 * c + min(which, 3)]
                to = spot * plan["n_line"] + (ref.shape[0] if which == 4 else 0)
                pieces.append((ref, to, spot // 2))
        for wanted in order:
            for ref, to, part in pieces:

                @pl.when(part == wanted)
                def _():
                    self.copy(ref, to, part)

    def copy(self, ref, to, part):
        dst = self.w_scr.at[pl.ds(to, ref.shape[0])]
        pltpu.make_async_copy(ref, dst, self.sems.at[part]).start()

    def need(self, kind, tiles):
        per_tile, first = self.plan[kind]
        quarter = self.plan["quarter"]
        for part in range(self.plan["n_parts"]):
            used = any(
                first + t * per_tile < (part + 1) * quarter and first + (t + 1) * per_tile > part * quarter
                for t in tiles
            )
            if used and part not in self.here:
                self.here.add(part)
                rows = self.w_scr.at[pl.ds(part * self.rows, self.rows)]
                pltpu.make_async_copy(rows, rows, self.sems.at[part]).wait()


def dims_of(plan):
    return plan["T"], plan["D"], plan["heads"], plan["hd"], plan["tiles"] * LANES


def norm(x, gain):
    xf = x.astype(jnp.float32)
    inverse = lax.rsqrt(jnp.mean(xf * xf, axis=-1, keepdims=True) + 1e-06)
    return inverse, (xf * inverse * gain).astype(jnp.bfloat16)


def project(plan, normed, weights, w_ref, proj_scr):
    for j in range(0, plan["tiles"], 2):
        js = range(j, min(j + 2, plan["tiles"]))
        weights.need("w_tiles", js)
        w = jnp.concatenate([w_tile(plan, w_ref, i) for i in js], axis=1)
        proj_scr[:, j * LANES : j * LANES + LANES * len(js)] = jnp.dot(
            normed, w, preferred_element_type=jnp.float32
        ).astype(jnp.bfloat16)


def qkv_of(plan, proj_ref, h):
    hd, hidden = plan["hd"], plan["heads"] * plan["hd"]
    return [proj_ref[:, m * hidden + h * hd : m * hidden + (h + 1) * hd] for m in range(3)]


def attend(plan, h, proj_ref, bias):
    q, k, v = qkv_of(plan, proj_ref, h)
    scores = lax.dot_general(q, k, NT, preferred_element_type=jnp.float32)
    raised = jnp.exp(scores * plan["hd"] ** (-0.5) + bias)
    probs = raised / jnp.sum(raised, axis=-1, keepdims=True)
    attended = jnp.dot(probs.astype(jnp.bfloat16), v, preferred_element_type=jnp.float32)
    return probs, attended.astype(jnp.bfloat16)


def rows_of(plan, ref, second=False):
    if not plan["pairs"]:
        return ref[...]
    n = plan["T"] // plan["pairs"]
    at = n if second else 0
    return jnp.concatenate([ref[2 * n * i + at : 2 * n * i + at + n, :] for i in range(plan["pairs"])], axis=0)


def fwd_kernel(plan, place_ref, gates_ref, x_ref, gain_ref, bias_ref, cot_ref, *rest):
    n = plan["n_refs"]
    refs, rest = rest[:n], rest[n:]
    y_ref, proj_out, probs_out, att_out, w_ref, sems, proj_ref, probs_ref, att_ref, gated_scr = rest
    T, D, heads, hd, wide = dims_of(plan)
    layer, stride = plan["layer"], plan["og"] * ROWS
    weights = Weights(plan, place_ref, refs, w_ref, sems, (0, 1, 2, 3))
    x = rows_of(plan, x_ref)
    inverse, normed = norm(x, gain_ref[layer : layer + 1, :])
    project(plan, normed, weights, w_ref, proj_ref)
    free = 4
    saves = [pltpu.make_async_copy(proj_ref, proj_out, sems.at[free])]
    saves[0].start()
    bias = bias_ref[...]
    gated_scr[...] = jnp.zeros_like(gated_scr)
    for h in range(heads):
        probs, attended = attend(plan, h, proj_ref, bias)
        probs_ref[h] = probs
        saves.append(pltpu.make_async_copy(probs_ref.at[h], probs_out.at[h], sems.at[free + 2 + h]))
        saves[-1].start()
        att_ref[:, h * hd : (h + 1) * hd] = attended
        gated = (attended.astype(jnp.float32) * gates_ref[layer, h]).astype(jnp.bfloat16)
        gated_scr[:, h * stride : h * stride + hd] = gated
    saves.append(pltpu.make_async_copy(att_ref, att_out, sems.at[free + 1]))
    saves[-1].start()
    gated = gated_scr[...]
    lane_tiles = D // LANES
    for j in range(0, lane_tiles, 2):
        js = range(j, min(j + 2, lane_tiles))
        weights.need("o_tiles", js)
        w = jnp.concatenate([o_tile(plan, w_ref, i, range(heads)) for i in js], axis=1)
        cols = slice(j * LANES, j * LANES + LANES * len(js))
        y = (
            x[:, cols].astype(jnp.float32) + jnp.dot(gated, w, preferred_element_type=jnp.float32)
        ).astype(jnp.bfloat16)
        n = T // plan["to"]
        for i in range(plan["to"]):
            y_ref[2 * n * i : 2 * n * i + n, cols] = y[n * i : n * i + n]
    cot = rows_of(plan, cot_ref, True)
    for i in range(plan["to"]):
        y_ref[2 * n * i + n : 2 * n * i + 2 * n, :] = cot[n * i : n * i + n]
    for copy in saves:
        copy.wait()


def backward(plan, gates_ref, outgrad, x, gain, inverse, proj_ref, probs_of, att_of, sens,
             weights, w_ref, dgated_scr, dproj_scr, g_ref, sens_ref):
    T, D, heads, hd, wide = dims_of(plan)
    layer, stride, hidden = plan["layer"], plan["og"] * ROWS, heads * hd
    lane_tiles = D // LANES
    weights.need("o_tiles", range(lane_tiles))
    for r in range(0, heads, 2):
        hs = min(2, heads - r)
        w = jnp.concatenate(
            [o_tile(plan, w_ref, i, range(r, r + hs)) for i in range(lane_tiles)],
            axis=1,
        )
        out = lax.dot_general(outgrad, w, NT, preferred_element_type=jnp.float32)
        dgated_scr[:, r * stride : (r + hs) * stride] = out.astype(jnp.bfloat16)
    if wide > 3 * hidden:
        dproj_scr[:, wide - LANES :] = jnp.zeros((T, LANES), jnp.bfloat16)
    lane = lax.broadcasted_iota(jnp.int32, (T, LANES), 1)
    for h in range(heads):
        q, k, v = qkv_of(plan, proj_ref, h)
        probs = probs_of(h)
        dgated = dgated_scr[:, h * stride : h * stride + hd].astype(jnp.float32)
        own = jnp.sum(dgated * att_of(h).astype(jnp.float32), axis=-1, keepdims=True)
        sens = jnp.where(lane == layer * heads + h, own, sens)
        datt = (dgated * gates_ref[layer, h]).astype(jnp.bfloat16)
        dprobs = lax.dot_general(datt, v, NT, preferred_element_type=jnp.float32)
        dvalues = lax.dot_general(
            probs.astype(jnp.bfloat16), datt, TN, preferred_element_type=jnp.float32
        )
        inner = jnp.sum(dprobs * probs, axis=-1, keepdims=True)
        dscores = (probs * (dprobs - inner) * hd ** (-0.5)).astype(jnp.bfloat16)
        dqueries = jnp.dot(dscores, k, preferred_element_type=jnp.float32)
        dkeys = lax.dot_general(dscores, q, TN, preferred_element_type=jnp.float32)
        for m, d in enumerate((dqueries, dkeys, dvalues)):
            at = m * hidden + h * hd
            dproj_scr[:, at : at + hd] = d.astype(jnp.bfloat16)
    sens_ref[...] = sens.astype(jnp.bfloat16)
    weights.need("w_tiles", range(plan["tiles"]))
    dproj = dproj_scr[...]
    step = 2 * LANES
    parts = []
    for r in range(0, D, step):
        rr = min(step, D - r)
        w = jnp.concatenate(
            [
                w_tile(plan, w_ref, i, r // ROWS, rr // ROWS)
                for i in range(plan["tiles"])
            ],
            axis=1,
        )
        parts.append(lax.dot_general(dproj, w, NT, preferred_element_type=jnp.float32))
    dnormed = jnp.concatenate(parts, axis=1) * gain
    xf = x.astype(jnp.float32)
    mean = jnp.mean(xf * dnormed, axis=-1, keepdims=True)
    ingrad = (
        outgrad.astype(jnp.float32)
        + inverse * dnormed
        - xf * (inverse * inverse * inverse) * mean
    )
    g_ref[...] = ingrad.astype(jnp.bfloat16)


def both_kernel(plan, place_ref, gates_ref, x_ref, gain_ref, bias_ref, *rest):
    n = plan["n_refs"]
    refs, rest = rest[:n], rest[n:]
    g_ref, w_ref, sems, proj_scr, probs_scr, att_scr, dgated_scr, dproj_scr = rest
    T, D, heads, hd, wide = dims_of(plan)
    layer = plan["layer"]
    weights = Weights(plan, place_ref, refs, w_ref, sems, (0, 1, 2, 3))
    gain = gain_ref[layer : layer + 1, :]
    x = rows_of(plan, x_ref)
    inverse, normed = norm(x, gain)
    project(plan, normed, weights, w_ref, proj_scr)
    bias = bias_ref[...]
    for h in range(heads):
        probs, attended = attend(plan, h, proj_scr, bias)
        probs_scr[h] = probs
        att_scr[:, h * hd : (h + 1) * hd] = attended
    backward(
        plan, gates_ref, rows_of(plan, x_ref, True), x, gain, inverse, proj_scr,
        lambda h: probs_scr[h], lambda h: att_scr[:, h * hd : (h + 1) * hd],
        jnp.zeros((T, LANES), jnp.float32), weights, w_ref, dgated_scr, dproj_scr,
        g_ref.at[:, :D], g_ref.at[:, D : D + LANES],
    )


def bwd_kernel(plan, place_ref, gates_ref, x_ref, gain_ref, outgrad_ref, proj_in, probs_in, att_in,
               *rest):
    n = plan["n_refs"]
    refs, rest = rest[:n], rest[n:]
    if plan["apart"]:
        g_ref, sens_ref, *rest = rest
    else:
        g_ref, *rest = rest
    w_ref, sems, proj_ref, probs_ref, att_ref, dgated_scr, dproj_scr = rest
    T, D, heads, hd, wide = dims_of(plan)
    layer = plan["layer"]
    loads = []
    for src, dst in ((att_in, att_ref), (proj_in, proj_ref), (probs_in, probs_ref)):
        loads.append(pltpu.make_async_copy(src, dst, sems.at[4 + len(loads)]))
    for copy in loads:
        copy.start()
    weights = Weights(plan, place_ref, refs, w_ref, sems, (3, 2, 1, 0))
    gain = gain_ref[layer : layer + 1, :]
    x = rows_of(plan, x_ref)
    inverse, _ = norm(x, gain)
    for copy in loads:
        copy.wait()
    if not plan["apart"]:
        g_ref, sens_ref = g_ref.at[:, :D], g_ref.at[:, D : D + LANES]
    backward(
        plan, gates_ref, outgrad_ref[:, :D], x, gain, inverse,
        proj_ref, lambda h: probs_ref[h], lambda h: att_ref[:, h * hd : (h + 1) * hd],
        outgrad_ref[:, D : D + LANES].astype(jnp.float32),
        weights, w_ref, dgated_scr, dproj_scr, g_ref, sens_ref,
    )


def call(kernel, plan, place, gates, weights, arrays, saved, outs, saves, scratch, flops):
    vmem = pl.BlockSpec(memory_space=pltpu.VMEM)
    smem = pl.BlockSpec(memory_space=pltpu.SMEM)
    plan = dict(plan, n_refs=len(weights))
    n_sems = 4 + 2 + plan["heads"]
    return pl.pallas_call(
        functools.partial(kernel, plan),
        out_shape=list(outs) + list(saves),
        in_specs=[smem, smem]
        + [vmem] * len(arrays)
        + [pl.BlockSpec(memory_space=pl.ANY)] * (len(saved) + len(weights)),
        out_specs=[vmem] * len(outs) + [HBM] * len(saves),
        scratch_shapes=[
            pltpu.VMEM((plan["n_blocks"], ROWS, LANES), jnp.bfloat16),
            pltpu.SemaphoreType.DMA((n_sems,)),
        ]
        + scratch,
        compiler_params=pltpu.CompilerParams(vmem_limit_bytes=60 * 2**20),
        cost_estimate=pl.CostEstimate(flops=flops, bytes_accessed=12 * 2**20, transcendentals=0),
    )(place, gates, *arrays, *saved, *weights)


def per_device(n_ha, n_wa, tokens, cotangent, w_qkv, w_out, gains, gates):
    videos, frames, rows, cols, D = tokens.shape
    layers, heads = gates.shape
    T = videos * frames * rows * cols
    width = w_qkv.shape[2]
    hidden = width // 3
    hd = hidden // heads
    tiles = ceil_to(width, LANES) // LANES
    og = ceil_to(hd, ROWS) // ROWS
    lane_tiles = D // LANES
    wide = tiles * LANES

    def flat(value):
        return jnp.swapaxes(value, 0, 1).reshape(T, D)

    idx = jnp.arange(T)
    fl = frames // n_ha * videos
    lines = [
        idx % (videos * rows * cols),
        (idx // (rows * cols)) % fl * cols + idx % cols,
        (idx // cols) % (T // (n_wa * cols)),
    ]
    biases = [jnp.where(line[:, None] == line[None, :], 0.0, -1e30).astype(jnp.float32) for line in lines]

    def swap(value, axis):
        return lax.all_to_all(value, axis, split_axis=0, concat_axis=0, tiled=True)

    home, teacher = flat(tokens), flat(cotangent)

    shard = w_qkv.shape[1]
    base = dict(T=T, D=D, heads=heads, hd=hd, tiles=tiles, og=og, square=False, apart=False, pairs=0,
                w_tiles=(shard // ROWS, 0), o_tiles=(og, shard // ROWS * tiles))
    weights = []
    fast = n_ha == 4 and n_wa % 4 == 0 and shard % ROWS == 0 and w_out.shape[1] == hd
    if fast:
        routes = Routes(n_ha, n_wa)
        ha, wa = lax.axis_index("ha"), lax.axis_index("wa")
        n_z = n_wa // 2
        spot = ha * 2 + wa % 2
        spots = [spot ^ k for k in (0, 1, 4, 5, 2, 3, 6, 7)]
        place = jnp.stack(spots).astype(jnp.int32)
        rg = shard // ROWS
        quarter = -(-(rg * tiles + og * lane_tiles) // 4)

        def own_quarter(layer):
            own = flat_blocks(blocks_of(w_qkv[layer]), blocks_of(w_out[layer]))
            own = jnp.pad(own, [(0, 4 * quarter - own.shape[0]), (0, 0), (0, 0)])
            return lax.dynamic_slice_in_dim(own, ha * quarter, quarter, 0)

        def addresses(at):
            return dict(
                w_at=lambda g, t: at(g // rg, *divmod(t * rg + g % rg, quarter)),
                o_at=lambda h, g, t: at(h, *divmod(rg * tiles + t * og + g, quarter)),
            )

        squarewise = addresses(
            lambda slot, part, inner: ((part * 2 + slot % 2) * n_z + slot // 2) * quarter + inner
        )
        slots = jnp.stack([(wa // 2) ^ k for k in range(n_z)]).astype(jnp.int32)
        base.update(n_line=n_z * quarter, n_blocks=4 * quarter * n_wa, quarter=quarter, n_parts=4)
        plans = [dict(base, layer=layer, square=True, **squarewise) for layer in range(layers)]

        line = routes.line(own_quarter(0))
        later = hand_on(jnp.concatenate([own_quarter(1), own_quarter(2)]), line)
        far = [routes.send(later, wa_bits=2 * k) for k in range(1, n_z)]
        lines = []

        def stack_later(*squares):
            lines.extend(stacked(slots, [later] + far, 2, squares))
            return lines

        weights = [over_square(routes, line, [home, teacher] + biases, stack_later)]

        def gather(which, before, there):
            line = hand_on(lines[which], *weights[which][3:5])
            weights.append(over_square(routes, line, before, lambda *squares: there))

    else:
        full_qkv = lax.all_gather(w_qkv, "wa", axis=1, tiled=True)
        full_out = lax.all_gather(w_out, "wa", axis=1, tiled=True)
        n_rows = D // ROWS
        n_w = n_rows * tiles
        base["w_at"] = lambda g, t: t * n_rows + g
        base["o_at"] = lambda h, g, t: n_w + (h * lane_tiles + t) * og + g
        for layer in range(layers):
            by_head = full_out[layer].reshape(heads, hd, D)
            weights.append(
                [flat_blocks(blocks_of(full_qkv[layer]), *[blocks_of(by_head[h]) for h in range(heads)])]
            )
        n_blocks = weights[0][0].shape[0]
        base.update(n_blocks=n_blocks, quarter=n_blocks, n_parts=1)
        place = jnp.zeros((1,), jnp.int32)
        plans = [dict(base, layer=layer) for layer in range(layers)]

    bf16, f32 = jnp.bfloat16, jnp.float32
    act = jax.ShapeDtypeStruct((T, D), bf16)
    loaded = jax.ShapeDtypeStruct((T, D + LANES), bf16)
    dense = 2 * T * D * (width + hidden)

    keep = [
        jax.ShapeDtypeStruct((T, wide), bf16),
        jax.ShapeDtypeStruct((heads, T, T), f32),
        jax.ShapeDtypeStruct((T, hidden), bf16),
    ]
    kept = [pltpu.VMEM(array.shape, array.dtype) for array in keep]
    grads = [pltpu.VMEM((T, heads * og * ROWS), bf16), pltpu.VMEM((T, wide), bf16)]

    def forward(layer, x, cot, pairs, to):
        return call(
            fwd_kernel, dict(plans[layer], pairs=pairs, to=to), place, gates, weights[layer],
            [x, gains, biases[layer], cot], [], [jax.ShapeDtypeStruct((2 * T, D), bf16)], keep,
            kept + grads[:1], dense,
        )

    def back(layer, x, outgrad, saved, pairs, outs):
        plan = dict(plans[layer], pairs=pairs, apart=len(outs) > 1)
        return call(
            bwd_kernel, plan, place, gates, weights[layer], [x, gains, outgrad], saved, outs, [],
            kept + grads, dense,
        )

    after_time, *saved_time = forward(0, home, teacher, 0, n_ha)
    tall = swap(after_time, "ha")
    if fast:
        gather(0, [after_time], [tall])
    after_height, *saved_height = forward(1, tall, tall, n_ha, n_wa)
    if fast:
        gather(1, [after_height], [after_height])
    across = swap(after_height, "wa")
    (grad,) = call(
        both_kernel, dict(plans[2], pairs=n_wa), place, gates, weights[2],
        [across, gains, biases[2]], [], [loaded], [], kept + grads, 2 * dense,
    )
    (grad,) = back(1, tall, swap(grad, "wa"), saved_height, n_ha, [loaded])
    apart = [act, jax.ShapeDtypeStruct((T, LANES), bf16)]
    grad, sens = back(0, home, swap(grad, "ha"), saved_time, 0, apart)

    def unflat(value):
        value = value.reshape(frames, videos, rows, cols, value.shape[-1])
        return jnp.swapaxes(value, 0, 1)

    token_grad = unflat(grad)
    sens = unflat(sens[:, : layers * heads]).reshape(videos, frames, rows, cols, layers, heads)
    return (token_grad, jnp.moveaxis(sens, 4, 1))


def solution(mesh):
    spec = P(None, None, "ha", "wa", None)
    in_specs = (spec, spec, P(None, "wa", None), P(None, "wa", None), P(), P())
    out_specs = (spec, P(None, None, None, "ha", "wa", None))
    n_ha, n_wa = mesh.shape["ha"], mesh.shape["wa"]
    return jax.shard_map(
        functools.partial(per_device, n_ha, n_wa),
        mesh=mesh, in_specs=in_specs, out_specs=out_specs, check_vma=False,
    )
```

```python
import functools

import jax
import jax.numpy as jnp
from jax import lax
from jax.experimental import pallas as pl
from jax.experimental.pallas import tpu as pltpu
from jax.sharding import PartitionSpec as P

LANES = 128
ROWS = 16
AXES = ("ha", "wa")
NT = (((1,), (1,)), ((), ()))
TN = (((0,), (0,)), ((), ()))


def ceil_to(value, unit):
    return -(-value // unit) * unit


def blocks_of(w):
    rows, cols = w.shape
    tall, wide = ceil_to(rows, ROWS), ceil_to(cols, LANES)
    w = jnp.pad(w, [(0, tall - rows), (0, wide - cols)])
    return jnp.moveaxis(w.reshape(tall // ROWS, ROWS, wide // LANES, LANES), 2, 0)


def flat_blocks(*arrays):
    return jnp.concatenate([a.reshape(-1, ROWS, LANES) for a in arrays])


HBM = pl.BlockSpec(memory_space=pltpu.HBM)


def hand_on(value, *after):
    def nothing(*refs):
        del refs

    return pl.pallas_call(
        nothing,
        out_shape=jax.ShapeDtypeStruct(value.shape, value.dtype),
        in_specs=[HBM] * (1 + len(after)),
        out_specs=HBM,
        input_output_aliases={0: 0},
        compiler_params=pltpu.CompilerParams(vmem_limit_bytes=60 * 2**20),
    )(value, *after)


def pack_kernel(part_ref, q_ref, o_ref, *rest):
    *outs, q_scr, o_scr = rest
    layers, rows, width = q_ref.shape
    hd = o_ref.shape[1]
    q_scr[:, :, :width] = q_ref[...]
    if q_scr.shape[2] > width:
        q_scr[:, :, width:] = jnp.zeros((layers, rows, q_scr.shape[2] - width), q_scr.dtype)
    o_scr[:, :hd, :] = o_ref[...]
    if o_scr.shape[1] > hd:
        o_scr[:, hd:, :] = jnp.zeros((layers, o_scr.shape[1] - hd, o_scr.shape[2]), o_scr.dtype)
    rg, og = rows // ROWS, o_scr.shape[1] // ROWS
    n_q, n_o = rg * (q_scr.shape[2] // LANES), og * (o_scr.shape[2] // LANES)
    quarter = outs[0].shape[0]

    def block(scr, layer, index, groups):
        row = pl.multiple_of(lax.rem(index, groups) * ROWS, ROWS)
        lane = pl.multiple_of(lax.div(index, groups) * LANES, LANES)
        return scr[layer, pl.ds(row, ROWS), pl.ds(lane, LANES)]

    def body(i, carry):
        index = part_ref[0] * quarter + i
        in_q = jnp.minimum(index, n_q - 1)
        in_o = jnp.clip(index - n_q, 0, n_o - 1)
        for layer in range(layers):
            out = outs[min(layer, 1)]
            out[i + max(layer - 1, 0) * quarter] = jnp.where(index < n_q, block(q_scr, layer, in_q, rg), block(o_scr, layer, in_o, og))
        return carry

    lax.fori_loop(0, quarter, body, 0)


def own_quarters(part, w_qkv, w_out, quarter):
    layers, rows, width = w_qkv.shape
    vmem = pl.BlockSpec(memory_space=pltpu.VMEM)
    return pl.pallas_call(
        pack_kernel,
        out_shape=[
            jax.ShapeDtypeStruct((n * quarter, ROWS, LANES), w_qkv.dtype) for n in (1, layers - 1)
        ],
        in_specs=[pl.BlockSpec(memory_space=pltpu.SMEM), vmem, vmem],
        out_specs=[vmem] * 2,
        scratch_shapes=[
            pltpu.VMEM((layers, rows, ceil_to(width, LANES)), w_qkv.dtype),
            pltpu.VMEM((layers, ceil_to(w_out.shape[1], ROWS), w_out.shape[2]), w_out.dtype),
        ],
        compiler_params=pltpu.CompilerParams(vmem_limit_bytes=60 * 2**20),
    )(part, w_qkv, w_out)


class Routes:
    def __init__(self, n_ha, n_wa):
        self.n_ha, self.n_wa = n_ha, n_wa

    def send(self, value, ha_bits=0, wa_bits=0):
        pairs = [
            (a * self.n_wa + b, (a ^ ha_bits) * self.n_wa + (b ^ wa_bits))
            for a in range(self.n_ha)
            for b in range(self.n_wa)
        ]
        return lax.ppermute(value, AXES, pairs)

    def core(self, value):
        return self.send(value, ha_bits=1)

    def x(self, value):
        return self.send(value, ha_bits=2)

    def y(self, value):
        return self.send(value, wa_bits=1)

    def line(self, value):
        groups = [
            [a * self.n_wa + 2 * z + y for z in range(self.n_wa // 2)]
            for a in range(self.n_ha)
            for y in range(2)
        ]
        return lax.all_gather(value, AXES, axis=0, tiled=True, axis_index_groups=groups)


def over_square(routes, line, before, between):
    half = line.shape[0] // 2
    over_y, over_x = routes.y(line), routes.x(line)
    over_y, over_x = hand_on(over_y, *before), hand_on(over_x, *before)
    low, high = routes.y(over_x[:half]), routes.x(over_y[half:])
    there = between(over_y, over_x)
    low, high = hand_on(low, *there), hand_on(high, *there)
    mine = [hand_on(line, over_y, over_x), over_y, over_x, low, high]
    return mine + [routes.core(piece) for piece in mine]


def stack_kernel(n, slot_ref, *refs):
    ins, outs, held, sems = refs[:n], refs[n:-2], refs[-2], refs[-1]
    rows = held.shape[2]
    reads, writes = [], []
    for j, out in enumerate(outs):
        for i in range(n):
            slot = pl.ds(slot_ref[i] * rows, rows)
            piece = ins[i].at[pl.ds(j * rows, rows)]
            reads.append(pltpu.make_async_copy(piece, held.at[j, i], sems.at[0, j, i]))
            writes.append(pltpu.make_async_copy(held.at[j, i], out.at[slot], sems.at[1, j, i]))
    for read in reads:
        read.start()
    for read, write in zip(reads, writes):
        read.wait()
        write.start()
    for write in writes:
        write.wait()


def stacked(slots, arrays, outs, after):
    n, rows = len(arrays), arrays[0].shape[0] // outs
    anywhere = pl.BlockSpec(memory_space=pl.ANY)
    line = jax.ShapeDtypeStruct((n * rows, ROWS, LANES), jnp.bfloat16)
    return pl.pallas_call(
        lambda *refs: stack_kernel(n, *refs[: n + 1], *refs[n + 1 + len(after) :]),
        out_shape=[line] * outs,
        in_specs=[pl.BlockSpec(memory_space=pltpu.SMEM)] + [anywhere] * (n + len(after)),
        out_specs=[anywhere] * outs,
        scratch_shapes=[
            pltpu.VMEM((outs, n, rows, ROWS, LANES), jnp.bfloat16),
            pltpu.SemaphoreType.DMA((2, outs, n)),
        ],
        compiler_params=pltpu.CompilerParams(vmem_limit_bytes=60 * 2**20),
    )(slots, *arrays, *after)


def w_tile(plan, ref, tile, first=0, count=None):
    count = plan["D"] // ROWS - first if count is None else count
    return jnp.concatenate([ref[plan["w_at"](g, tile)] for g in range(first, first + count)], axis=0)


def o_tile(plan, ref, tile, heads):
    return jnp.concatenate(
        [ref[plan["o_at"](h, g, tile)] for h in heads for g in range(plan["og"])], axis=0
    )


class Weights:
    def __init__(self, plan, place_ref, refs, w_scr, sems, order):
        self.plan, self.w_scr, self.sems, self.here = plan, w_scr, sems, set()
        n_parts = plan["n_parts"]
        self.rows = w_scr.shape[0] // n_parts
        if not plan["square"]:
            for part in order if n_parts > 1 else [0]:
                self.copy(refs[0].at[pl.ds(part * self.rows, self.rows)], part * self.rows, part)
            return
        pieces = []
        for c in range(2):
            for which, ref in enumerate(refs[5 * c : 5 * c + 5]):
                spot = place_ref[4 * c + min(which, 3)]
                to = spot * plan["n_line"] + (ref.shape[0] if which == 4 else 0)
                pieces.append((ref, to, spot // 2))
        for wanted in order:
            for ref, to, part in pieces:

                @pl.when(part == wanted)
                def _():
                    self.copy(ref, to, part)

    def copy(self, ref, to, part):
        dst = self.w_scr.at[pl.ds(to, ref.shape[0])]
        pltpu.make_async_copy(ref, dst, self.sems.at[part]).start()

    def need(self, kind, tiles):
        per_tile, first = self.plan[kind]
        quarter = self.plan["quarter"]
        for part in range(self.plan["n_parts"]):
            used = any(
                first + t * per_tile < (part + 1) * quarter and first + (t + 1) * per_tile > part * quarter
                for t in tiles
            )
            if used and part not in self.here:
                self.here.add(part)
                rows = self.w_scr.at[pl.ds(part * self.rows, self.rows)]
                pltpu.make_async_copy(rows, rows, self.sems.at[part]).wait()


def dims_of(plan):
    return plan["T"], plan["D"], plan["heads"], plan["hd"], plan["tiles"] * LANES


def norm(x, gain):
    xf = x.astype(jnp.float32)
    inverse = lax.rsqrt(jnp.mean(xf * xf, axis=-1, keepdims=True) + 1e-06)
    return inverse, (xf * inverse * gain).astype(jnp.bfloat16)


def project(plan, normed, weights, w_ref, proj_scr):
    for j in range(0, plan["tiles"], 2):
        js = range(j, min(j + 2, plan["tiles"]))
        weights.need("w_tiles", js)
        w = jnp.concatenate([w_tile(plan, w_ref, i) for i in js], axis=1)
        proj_scr[:, j * LANES : j * LANES + LANES * len(js)] = jnp.dot(
            normed, w, preferred_element_type=jnp.float32
        ).astype(jnp.bfloat16)


def qkv_of(plan, proj_ref, h):
    hd, hidden = plan["hd"], plan["heads"] * plan["hd"]
    return [proj_ref[:, m * hidden + h * hd : m * hidden + (h + 1) * hd] for m in range(3)]


def attend(plan, h, proj_ref, bias):
    q, k, v = qkv_of(plan, proj_ref, h)
    scores = lax.dot_general(q, k, NT, preferred_element_type=jnp.float32)
    raised = jnp.exp(scores * plan["hd"] ** (-0.5) + bias)
    probs = raised / jnp.sum(raised, axis=-1, keepdims=True)
    attended = jnp.dot(probs.astype(jnp.bfloat16), v, preferred_element_type=jnp.float32)
    return probs, attended.astype(jnp.bfloat16)


def rows_of(plan, ref, second=False):
    if not plan["pairs"]:
        return ref[...]
    n = plan["T"] // plan["pairs"]
    at = n if second else 0
    return jnp.concatenate([ref[2 * n * i + at : 2 * n * i + at + n, :] for i in range(plan["pairs"])], axis=0)


def fwd_kernel(plan, place_ref, gates_ref, x_ref, gain_ref, bias_ref, cot_ref, *rest):
    n = plan["n_refs"]
    refs, rest = rest[:n], rest[n:]
    y_ref, proj_out, probs_out, att_out, w_ref, sems, proj_ref, probs_ref, att_ref, gated_scr = rest
    T, D, heads, hd, wide = dims_of(plan)
    layer, stride = plan["layer"], plan["og"] * ROWS
    weights = Weights(plan, place_ref, refs, w_ref, sems, (0, 1, 2, 3))
    x = rows_of(plan, x_ref)
    inverse, normed = norm(x, gain_ref[layer : layer + 1, :])
    project(plan, normed, weights, w_ref, proj_ref)
    free = 4
    saves = [pltpu.make_async_copy(proj_ref, proj_out, sems.at[free])]
    saves[0].start()
    bias = bias_ref[...]
    gated_scr[...] = jnp.zeros_like(gated_scr)
    for h in range(heads):
        probs, attended = attend(plan, h, proj_ref, bias)
        probs_ref[h] = probs
        saves.append(pltpu.make_async_copy(probs_ref.at[h], probs_out.at[h], sems.at[free + 2 + h]))
        saves[-1].start()
        att_ref[:, h * hd : (h + 1) * hd] = attended
        gated = (attended.astype(jnp.float32) * gates_ref[layer, h]).astype(jnp.bfloat16)
        gated_scr[:, h * stride : h * stride + hd] = gated
    saves.append(pltpu.make_async_copy(att_ref, att_out, sems.at[free + 1]))
    saves[-1].start()
    gated = gated_scr[...]
    lane_tiles = D // LANES
    for j in range(0, lane_tiles, 2):
        js = range(j, min(j + 2, lane_tiles))
        weights.need("o_tiles", js)
        w = jnp.concatenate([o_tile(plan, w_ref, i, range(heads)) for i in js], axis=1)
        cols = slice(j * LANES, j * LANES + LANES * len(js))
        y = (
            x[:, cols].astype(jnp.float32) + jnp.dot(gated, w, preferred_element_type=jnp.float32)
        ).astype(jnp.bfloat16)
        n = T // plan["to"]
        for i in range(plan["to"]):
            y_ref[2 * n * i : 2 * n * i + n, cols] = y[n * i : n * i + n]
    cot = rows_of(plan, cot_ref, True)
    for i in range(plan["to"]):
        y_ref[2 * n * i + n : 2 * n * i + 2 * n, :] = cot[n * i : n * i + n]
    for copy in saves:
        copy.wait()


def backward(plan, gates_ref, outgrad, x, gain, inverse, proj_ref, probs_of, att_of, sens,
             weights, w_ref, dgated_scr, dproj_scr):
    T, D, heads, hd, wide = dims_of(plan)
    layer, stride, hidden = plan["layer"], plan["og"] * ROWS, heads * hd
    lane_tiles = D // LANES
    weights.need("o_tiles", range(lane_tiles))
    for r in range(0, heads, 2):
        hs = min(2, heads - r)
        w = jnp.concatenate(
            [o_tile(plan, w_ref, i, range(r, r + hs)) for i in range(lane_tiles)],
            axis=1,
        )
        out = lax.dot_general(outgrad, w, NT, preferred_element_type=jnp.float32)
        dgated_scr[:, r * stride : (r + hs) * stride] = out.astype(jnp.bfloat16)
    if wide > 3 * hidden:
        dproj_scr[:, wide - LANES :] = jnp.zeros((T, LANES), jnp.bfloat16)
    lane = lax.broadcasted_iota(jnp.int32, (T, LANES), 1)
    for h in range(heads):
        q, k, v = qkv_of(plan, proj_ref, h)
        probs = probs_of(h)
        dgated = dgated_scr[:, h * stride : h * stride + hd].astype(jnp.float32)
        own = jnp.sum(dgated * att_of(h).astype(jnp.float32), axis=-1, keepdims=True)
        sens = jnp.where(lane == layer * heads + h, own, sens)
        datt = (dgated * gates_ref[layer, h]).astype(jnp.bfloat16)
        dprobs = lax.dot_general(datt, v, NT, preferred_element_type=jnp.float32)
        dvalues = lax.dot_general(
            probs.astype(jnp.bfloat16), datt, TN, preferred_element_type=jnp.float32
        )
        inner = jnp.sum(dprobs * probs, axis=-1, keepdims=True)
        dscores = (probs * (dprobs - inner) * hd ** (-0.5)).astype(jnp.bfloat16)
        dqueries = jnp.dot(dscores, k, preferred_element_type=jnp.float32)
        dkeys = lax.dot_general(dscores, q, TN, preferred_element_type=jnp.float32)
        for m, d in enumerate((dqueries, dkeys, dvalues)):
            at = m * hidden + h * hd
            dproj_scr[:, at : at + hd] = d.astype(jnp.bfloat16)
    weights.need("w_tiles", range(plan["tiles"]))
    dproj = dproj_scr[...]
    step = 2 * LANES
    parts = []
    for r in range(0, D, step):
        rr = min(step, D - r)
        w = jnp.concatenate(
            [
                w_tile(plan, w_ref, i, r // ROWS, rr // ROWS)
                for i in range(plan["tiles"])
            ],
            axis=1,
        )
        parts.append(lax.dot_general(dproj, w, NT, preferred_element_type=jnp.float32))
    dnormed = jnp.concatenate(parts, axis=1) * gain
    xf = x.astype(jnp.float32)
    mean = jnp.mean(xf * dnormed, axis=-1, keepdims=True)
    ingrad = (
        outgrad.astype(jnp.float32)
        + inverse * dnormed
        - xf * (inverse * inverse * inverse) * mean
    )
    return ingrad, sens


def both_kernel(plan, place_ref, gates_ref, x_ref, gain_ref, bias_ref, *rest):
    n = plan["n_refs"]
    refs, rest = rest[:n], rest[n:]
    g_ref, w_ref, sems, proj_scr, probs_scr, att_scr, dgated_scr, dproj_scr = rest
    T, D, heads, hd, wide = dims_of(plan)
    layer = plan["layer"]
    weights = Weights(plan, place_ref, refs, w_ref, sems, (0, 1, 2, 3))
    gain = gain_ref[layer : layer + 1, :]
    x = rows_of(plan, x_ref)
    inverse, normed = norm(x, gain)
    project(plan, normed, weights, w_ref, proj_scr)
    bias = bias_ref[...]
    for h in range(heads):
        probs, attended = attend(plan, h, proj_scr, bias)
        probs_scr[h] = probs
        att_scr[:, h * hd : (h + 1) * hd] = attended
    ingrad, sens = backward(
        plan, gates_ref, rows_of(plan, x_ref, True), x, gain, inverse, proj_scr,
        lambda h: probs_scr[h], lambda h: att_scr[:, h * hd : (h + 1) * hd],
        jnp.zeros((T, LANES), jnp.float32), weights, w_ref, dgated_scr, dproj_scr,
    )
    g_ref[:, :D] = ingrad.astype(jnp.bfloat16)
    g_ref[:, D:] = sens.astype(jnp.bfloat16)


def bwd_kernel(plan, place_ref, gates_ref, x_ref, gain_ref, *rest):
    T, D, heads, hd, wide = dims_of(plan)
    n_in, n_out = plan["n_in"], plan["n_out"]
    outgrad_refs, rest = rest[:n_in], rest[n_in:]
    proj_in, probs_in, att_in, *rest = rest
    n = plan["n_refs"]
    refs, outs, rest = rest[:n], rest[n : n + n_out], rest[n + n_out :]
    w_ref, sems, proj_ref, probs_ref, att_ref, dgated_scr, dproj_scr, flow_scr = rest
    layer = plan["layer"]
    loads = []
    for src, dst in ((att_in, att_ref), (proj_in, proj_ref), (probs_in, probs_ref)):
        loads.append(pltpu.make_async_copy(src, dst, sems.at[4 + len(loads)]))
    for copy in loads:
        copy.start()
    weights = Weights(plan, place_ref, refs, w_ref, sems, (3, 2, 1, 0))
    gain = gain_ref[layer : layer + 1, :]
    x = rows_of(plan, x_ref)
    inverse, _ = norm(x, gain)

    def block(count, k):
        rows = T // count
        return pl.ds(pl.multiple_of(place_ref[8 + k] * rows, rows), rows)

    outgrad_ref = outgrad_refs[0]
    if n_in > 1:
        outgrad_ref = dproj_scr.at[:, : D + LANES]
        for k, ref in enumerate(outgrad_refs):
            outgrad_ref[block(n_in, k), :] = ref[...]
    outgrad, sens = outgrad_ref[:, :D], outgrad_ref[:, D : D + LANES].astype(jnp.float32)
    for copy in loads:
        copy.wait()
    ingrad, sens = backward(
        plan, gates_ref, outgrad, x, gain, inverse,
        proj_ref, lambda h: probs_ref[h], lambda h: att_ref[:, h * hd : (h + 1) * hd],
        sens, weights, w_ref, dgated_scr, dproj_scr,
    )
    if plan["last"]:
        g_ref, sens_ref = outs
        cols, n_tiles = g_ref.shape[1], D // LANES
        for t in range(n_tiles):
            flow_scr[t] = ingrad[:, t * LANES : (t + 1) * LANES]
        flow_scr[n_tiles] = sens
        for j in range(cols):
            rows = pl.ds(j, T // cols, stride=cols)
            for t in range(n_tiles):
                g_ref[:, j, t * LANES : (t + 1) * LANES] = flow_scr[t, rows, :].astype(jnp.bfloat16)
            own = flow_scr[n_tiles, rows, :].astype(jnp.bfloat16)
            for m in range(sens_ref.shape[0]):
                sens_ref[m, :, j, :] = own[:, m * heads : (m + 1) * heads]
    elif n_out > 1:
        flow_scr[:, :D] = ingrad
        flow_scr[:, D:] = sens
        for k, out in enumerate(outs):
            out[...] = flow_scr[block(n_out, k), :].astype(jnp.bfloat16)
    else:
        outs[0][:, :D] = ingrad.astype(jnp.bfloat16)
        outs[0][:, D:] = sens.astype(jnp.bfloat16)


def call(kernel, plan, place, gates, weights, arrays, saved, outs, saves, scratch, flops):
    vmem = pl.BlockSpec(memory_space=pltpu.VMEM)
    smem = pl.BlockSpec(memory_space=pltpu.SMEM)
    plan = dict(plan, n_refs=len(weights))
    n_sems = 4 + 2 + plan["heads"]
    return pl.pallas_call(
        functools.partial(kernel, plan),
        out_shape=list(outs) + list(saves),
        in_specs=[smem, smem]
        + [vmem] * len(arrays)
        + [pl.BlockSpec(memory_space=pl.ANY)] * (len(saved) + len(weights)),
        out_specs=[vmem] * len(outs) + [HBM] * len(saves),
        scratch_shapes=[
            pltpu.VMEM((plan["n_blocks"], ROWS, LANES), jnp.bfloat16),
            pltpu.SemaphoreType.DMA((n_sems,)),
        ]
        + scratch,
        compiler_params=pltpu.CompilerParams(vmem_limit_bytes=60 * 2**20),
        cost_estimate=pl.CostEstimate(flops=flops, bytes_accessed=12 * 2**20, transcendentals=0),
    )(place, gates, *arrays, *saved, *weights)


def per_device(n_ha, n_wa, tokens, cotangent, w_qkv, w_out, gains, gates):
    videos, frames, rows, cols, D = tokens.shape
    layers, heads = gates.shape
    T = videos * frames * rows * cols
    width = w_qkv.shape[2]
    hidden = width // 3
    hd = hidden // heads
    tiles = ceil_to(width, LANES) // LANES
    og = ceil_to(hd, ROWS) // ROWS
    lane_tiles = D // LANES
    wide = tiles * LANES

    def flat(value):
        return jnp.swapaxes(value, 0, 1).reshape(T, D)

    idx = jnp.arange(T)
    fl = frames // n_ha * videos
    lines = [
        idx % (videos * rows * cols),
        (idx // (rows * cols)) % fl * cols + idx % cols,
        (idx // cols) % (T // (n_wa * cols)),
    ]
    biases = [jnp.where(line[:, None] == line[None, :], 0.0, -1e30).astype(jnp.float32) for line in lines]

    def swap(value, axis):
        return lax.all_to_all(value, axis, split_axis=0, concat_axis=0, tiled=True)

    home, teacher = flat(tokens), flat(cotangent)

    shard = w_qkv.shape[1]
    base = dict(T=T, D=D, heads=heads, hd=hd, tiles=tiles, og=og, square=False, pairs=0,
                w_tiles=(shard // ROWS, 0), o_tiles=(og, shard // ROWS * tiles))
    weights = []
    fast = n_ha == 4 and n_wa % 4 == 0 and shard % ROWS == 0 and w_out.shape[1] == hd
    if fast:
        routes = Routes(n_ha, n_wa)
        ha, wa = lax.axis_index("ha"), lax.axis_index("wa")
        n_z = n_wa // 2
        spot = ha * 2 + wa % 2
        spots = [spot ^ k for k in (0, 1, 4, 5, 2, 3, 6, 7)]
        place = jnp.stack(spots + [ha ^ k for k in range(n_ha)]).astype(jnp.int32)
        rg = shard // ROWS
        quarter = -(-(rg * tiles + og * lane_tiles) // 4)

        def addresses(at):
            return dict(
                w_at=lambda g, t: at(g // rg, *divmod(t * rg + g % rg, quarter)),
                o_at=lambda h, g, t: at(h, *divmod(rg * tiles + t * og + g, quarter)),
            )

        squarewise = addresses(
            lambda slot, part, inner: ((part * 2 + slot % 2) * n_z + slot // 2) * quarter + inner
        )
        slots = jnp.stack([(wa // 2) ^ k for k in range(n_z)]).astype(jnp.int32)
        base.update(n_line=n_z * quarter, n_blocks=4 * quarter * n_wa, quarter=quarter, n_parts=4)
        plans = [dict(base, layer=layer, square=True, **squarewise) for layer in range(layers)]

        own, later = own_quarters(ha.astype(jnp.int32)[None], w_qkv, w_out, quarter)
        line = routes.line(own)
        later = hand_on(later, line)
        far = [routes.send(later, wa_bits=2 * k) for k in range(1, n_z)]
        lines = []

        def stack_later(*squares):
            lines.extend(stacked(slots, [later] + far, 2, squares))
            return lines

        weights = [over_square(routes, line, [home, teacher] + biases, stack_later)]

        def gather(which, before, there):
            line = hand_on(lines[which], *weights[which][3:5])
            weights.append(over_square(routes, line, before, lambda *squares: there))

    else:
        full_qkv = lax.all_gather(w_qkv, "wa", axis=1, tiled=True)
        full_out = lax.all_gather(w_out, "wa", axis=1, tiled=True)
        n_rows = D // ROWS
        n_w = n_rows * tiles
        base["w_at"] = lambda g, t: t * n_rows + g
        base["o_at"] = lambda h, g, t: n_w + (h * lane_tiles + t) * og + g
        for layer in range(layers):
            by_head = full_out[layer].reshape(heads, hd, D)
            weights.append(
                [flat_blocks(blocks_of(full_qkv[layer]), *[blocks_of(by_head[h]) for h in range(heads)])]
            )
        n_blocks = weights[0][0].shape[0]
        base.update(n_blocks=n_blocks, quarter=n_blocks, n_parts=1)
        place = jnp.zeros((1,), jnp.int32)
        plans = [dict(base, layer=layer) for layer in range(layers)]

    bf16, f32 = jnp.bfloat16, jnp.float32
    act = jax.ShapeDtypeStruct((T, D), bf16)
    loaded = jax.ShapeDtypeStruct((T, D + LANES), bf16)
    dense = 2 * T * D * (width + hidden)

    keep = [
        jax.ShapeDtypeStruct((T, wide), bf16),
        jax.ShapeDtypeStruct((heads, T, T), f32),
        jax.ShapeDtypeStruct((T, hidden), bf16),
    ]
    kept = [pltpu.VMEM(array.shape, array.dtype) for array in keep]
    grads = [pltpu.VMEM((T, heads * og * ROWS), bf16), pltpu.VMEM((T, wide), bf16)]

    def forward(layer, x, cot, pairs, to):
        return call(
            fwd_kernel, dict(plans[layer], pairs=pairs, to=to), place, gates, weights[layer],
            [x, gains, biases[layer], cot], [], [jax.ShapeDtypeStruct((2 * T, D), bf16)], keep,
            kept + grads[:1], dense,
        )

    def back(layer, x, outgrads, saved, pairs, outs, last=False):
        plan = dict(plans[layer], pairs=pairs, n_in=len(outgrads), n_out=len(outs), last=last)
        flow = pltpu.VMEM((D // LANES + 1, T, LANES) if last else (T, D + LANES), f32)
        return call(
            bwd_kernel, plan, place, gates, weights[layer], [x, gains] + outgrads, saved, outs, [],
            kept + grads + [flow], dense,
        )

    after_time, *saved_time = forward(0, home, teacher, 0, n_ha)
    tall = swap(after_time, "ha")
    if fast:
        gather(0, [after_time], [tall])
    after_height, *saved_height = forward(1, tall, tall, n_ha, n_wa)
    if fast:
        gather(1, [after_height], [after_height])
    across = swap(after_height, "wa")
    (grad,) = call(
        both_kernel, dict(plans[2], pairs=n_wa), place, gates, weights[2],
        [across, gains, biases[2]], [], [loaded], [], kept + grads, 2 * dense,
    )
    grad = swap(grad, "wa")
    if fast:
        block = jax.ShapeDtypeStruct((T // n_ha, D + LANES), bf16)
        blocks = back(1, tall, [grad], saved_height, n_ha, [block] * n_ha)
        outgrads = [blocks[0]] + [routes.send(blocks[k], ha_bits=k) for k in range(1, n_ha)]
    else:
        (grad,) = back(1, tall, [grad], saved_height, n_ha, [loaded])
        outgrads = [swap(grad, "ha")]
    ends = [
        jax.ShapeDtypeStruct((T // cols, cols, D), bf16),
        jax.ShapeDtypeStruct((layers, T // cols, cols, heads), bf16),
    ]
    grad, sens = back(0, home, outgrads, saved_time, 0, ends, True)
    token_grad = jnp.swapaxes(grad.reshape(frames, videos, rows, cols, D), 0, 1)
    sens = sens.reshape(layers, frames, videos, rows, cols, heads)
    return (token_grad, jnp.moveaxis(sens, 2, 0))


def solution(mesh):
    spec = P(None, None, "ha", "wa", None)
    in_specs = (spec, spec, P(None, "wa", None), P(None, "wa", None), P(), P())
    out_specs = (spec, P(None, None, None, "ha", "wa", None))
    n_ha, n_wa = mesh.shape["ha"], mesh.shape["wa"]
    return jax.shard_map(
        functools.partial(per_device, n_ha, n_wa),
        mesh=mesh, in_specs=in_specs, out_specs=out_specs, check_vma=False,
    )
```

```python
import functools

import jax
import jax.numpy as jnp
from jax import lax
from jax.experimental import pallas as pl
from jax.experimental.pallas import tpu as pltpu
from jax.sharding import PartitionSpec as P

LANES = 128
ROWS = 16
AXES = ("ha", "wa")
NT = (((1,), (1,)), ((), ()))
TN = (((0,), (0,)), ((), ()))


def ceil_to(value, unit):
    return -(-value // unit) * unit


def blocks_of(w):
    rows, cols = w.shape
    tall, wide = ceil_to(rows, ROWS), ceil_to(cols, LANES)
    w = jnp.pad(w, [(0, tall - rows), (0, wide - cols)])
    return jnp.moveaxis(w.reshape(tall // ROWS, ROWS, wide // LANES, LANES), 2, 0)


def flat_blocks(*arrays):
    return jnp.concatenate([a.reshape(-1, ROWS, LANES) for a in arrays])


HBM = pl.BlockSpec(memory_space=pl.ANY)


def hand_on(value, *after):
    def nothing(*refs):
        del refs

    return pl.pallas_call(
        nothing,
        out_shape=jax.ShapeDtypeStruct(value.shape, value.dtype),
        in_specs=[HBM] * (1 + len(after)),
        out_specs=HBM,
        input_output_aliases={0: 0},
        compiler_params=pltpu.CompilerParams(vmem_limit_bytes=2**20),
    )(value, *after)


def pack_kernel(part_ref, q_ref, o_ref, *rest):
    *outs, q_scr, o_scr = rest
    layers, rows, width = q_ref.shape
    hd = o_ref.shape[1]
    q_scr[:, :, :width] = q_ref[...]
    if q_scr.shape[2] > width:
        q_scr[:, :, width:] = jnp.zeros((layers, rows, q_scr.shape[2] - width), q_scr.dtype)
    o_scr[:, :hd, :] = o_ref[...]
    if o_scr.shape[1] > hd:
        o_scr[:, hd:, :] = jnp.zeros((layers, o_scr.shape[1] - hd, o_scr.shape[2]), o_scr.dtype)
    rg, og = rows // ROWS, o_scr.shape[1] // ROWS
    n_q, n_o = rg * (q_scr.shape[2] // LANES), og * (o_scr.shape[2] // LANES)
    quarter = outs[0].shape[0]

    def block(scr, layer, index, groups):
        row = pl.multiple_of(lax.rem(index, groups) * ROWS, ROWS)
        lane = pl.multiple_of(lax.div(index, groups) * LANES, LANES)
        return scr[layer, pl.ds(row, ROWS), pl.ds(lane, LANES)]

    def body(i, carry):
        index = part_ref[0] * quarter + i
        in_q = jnp.minimum(index, n_q - 1)
        in_o = jnp.clip(index - n_q, 0, n_o - 1)
        for layer in range(layers):
            out = outs[min(layer, 1)]
            out[i + max(layer - 1, 0) * quarter] = jnp.where(index < n_q, block(q_scr, layer, in_q, rg), block(o_scr, layer, in_o, og))
        return carry

    lax.fori_loop(0, quarter, body, 0)


def own_quarters(part, w_qkv, w_out, quarter):
    layers, rows, width = w_qkv.shape
    vmem = pl.BlockSpec(memory_space=pltpu.VMEM)
    return pl.pallas_call(
        pack_kernel,
        out_shape=[
            jax.ShapeDtypeStruct((n * quarter, ROWS, LANES), w_qkv.dtype) for n in (1, layers - 1)
        ],
        in_specs=[pl.BlockSpec(memory_space=pltpu.SMEM), vmem, vmem],
        out_specs=[vmem] * 2,
        scratch_shapes=[
            pltpu.VMEM((layers, rows, ceil_to(width, LANES)), w_qkv.dtype),
            pltpu.VMEM((layers, ceil_to(w_out.shape[1], ROWS), w_out.shape[2]), w_out.dtype),
        ],
        compiler_params=pltpu.CompilerParams(vmem_limit_bytes=60 * 2**20),
    )(part, w_qkv, w_out)


class Routes:
    def __init__(self, n_ha, n_wa):
        self.n_ha, self.n_wa = n_ha, n_wa

    def send(self, value, ha_bits=0, wa_bits=0):
        pairs = [
            (a * self.n_wa + b, (a ^ ha_bits) * self.n_wa + (b ^ wa_bits))
            for a in range(self.n_ha)
            for b in range(self.n_wa)
        ]
        return lax.ppermute(value, AXES, pairs)

    def core(self, value):
        return self.send(value, ha_bits=1)

    def x(self, value):
        return self.send(value, ha_bits=2)

    def y(self, value):
        return self.send(value, wa_bits=1)

    def line(self, value):
        groups = [
            [a * self.n_wa + 2 * z + y for z in range(self.n_wa // 2)]
            for a in range(self.n_ha)
            for y in range(2)
        ]
        return lax.all_gather(value, AXES, axis=0, tiled=True, axis_index_groups=groups)


def over_square(routes, line, before, between):
    half = line.shape[0] // 2
    over_y, over_x = routes.y(line), routes.x(line)
    over_y, over_x = hand_on(over_y, *before), hand_on(over_x, *before)
    low, high = routes.y(over_x[:half]), routes.x(over_y[half:])
    there = between(over_y, over_x)
    if there:
        low, high = hand_on(low, *there), hand_on(high, *there)
    mine = [hand_on(line, over_y, over_x), over_y, over_x, low, high]
    return mine + [routes.core(piece) for piece in mine]


def stack_kernel(n, slot_ref, *refs):
    ins, outs, held, sems = refs[:n], refs[n:-2], refs[-2], refs[-1]
    rows = held.shape[2]
    reads, writes = [], []
    for j, out in enumerate(outs):
        for i in range(n):
            slot = pl.ds(slot_ref[i] * rows, rows)
            piece = ins[i].at[pl.ds(j * rows, rows)]
            reads.append(pltpu.make_async_copy(piece, held.at[j, i], sems.at[0, j, i]))
            writes.append(pltpu.make_async_copy(held.at[j, i], out.at[slot], sems.at[1, j, i]))
    for read in reads:
        read.start()
    for read, write in zip(reads, writes):
        read.wait()
        write.start()
    for write in writes:
        write.wait()


def stacked(slots, arrays, outs, after):
    n, rows = len(arrays), arrays[0].shape[0] // outs
    anywhere = pl.BlockSpec(memory_space=pl.ANY)
    line = jax.ShapeDtypeStruct((n * rows, ROWS, LANES), jnp.bfloat16)
    return pl.pallas_call(
        lambda *refs: stack_kernel(n, *refs[: n + 1], *refs[n + 1 + len(after) :]),
        out_shape=[line] * outs,
        in_specs=[pl.BlockSpec(memory_space=pltpu.SMEM)] + [anywhere] * (n + len(after)),
        out_specs=[anywhere] * outs,
        scratch_shapes=[
            pltpu.VMEM((outs, n, rows, ROWS, LANES), jnp.bfloat16),
            pltpu.SemaphoreType.DMA((2, outs, n)),
        ],
        compiler_params=pltpu.CompilerParams(vmem_limit_bytes=3 * 2**20),
    )(slots, *arrays, *after)


def w_tile(plan, ref, tile, first=0, count=None):
    count = plan["D"] // ROWS - first if count is None else count
    return jnp.concatenate([ref[plan["w_at"](g, tile)] for g in range(first, first + count)], axis=0)


def o_tile(plan, ref, tile, heads):
    return jnp.concatenate(
        [ref[plan["o_at"](h, g, tile)] for h in heads for g in range(plan["og"])], axis=0
    )


class Weights:
    def __init__(self, plan, place_ref, refs, w_scr, sems, order):
        self.plan, self.w_scr, self.sems, self.here = plan, w_scr, sems, set()
        n_parts = plan["n_parts"]
        self.rows = w_scr.shape[0] // n_parts
        if not plan["square"]:
            for part in order if n_parts > 1 else [0]:
                self.copy(refs[0].at[pl.ds(part * self.rows, self.rows)], part * self.rows, part)
            return
        pieces = []
        for c in range(2):
            for which, ref in enumerate(refs[5 * c : 5 * c + 5]):
                spot = place_ref[4 * c + min(which, 3)]
                to = spot * plan["n_line"] + (ref.shape[0] if which == 4 else 0)
                pieces.append((ref, to, spot // 2))
        for wanted in order:
            for ref, to, part in pieces:

                @pl.when(part == wanted)
                def _():
                    self.copy(ref, to, part)

    def copy(self, ref, to, part):
        dst = self.w_scr.at[pl.ds(to, ref.shape[0])]
        pltpu.make_async_copy(ref, dst, self.sems.at[part]).start()

    def need(self, kind, tiles):
        per_tile, first = self.plan[kind]
        quarter = self.plan["quarter"]
        for part in range(self.plan["n_parts"]):
            used = any(
                first + t * per_tile < (part + 1) * quarter and first + (t + 1) * per_tile > part * quarter
                for t in tiles
            )
            if used and part not in self.here:
                self.here.add(part)
                rows = self.w_scr.at[pl.ds(part * self.rows, self.rows)]
                pltpu.make_async_copy(rows, rows, self.sems.at[part]).wait()


def dims_of(plan):
    return plan["T"], plan["D"], plan["heads"], plan["hd"], plan["tiles"] * LANES


def norm(x, gain):
    xf = x.astype(jnp.float32)
    inverse = lax.rsqrt(jnp.mean(xf * xf, axis=-1, keepdims=True) + 1e-06)
    return inverse, (xf * inverse * gain).astype(jnp.bfloat16)


def project(plan, normed, weights, w_ref, proj_scr):
    for j in range(0, plan["tiles"], 2):
        js = range(j, min(j + 2, plan["tiles"]))
        weights.need("w_tiles", js)
        w = jnp.concatenate([w_tile(plan, w_ref, i) for i in js], axis=1)
        proj_scr[:, j * LANES : j * LANES + LANES * len(js)] = jnp.dot(
            normed, w, preferred_element_type=jnp.float32
        ).astype(jnp.bfloat16)


def qkv_of(plan, proj_ref, h):
    hd, hidden = plan["hd"], plan["heads"] * plan["hd"]
    return [proj_ref[:, m * hidden + h * hd : m * hidden + (h + 1) * hd] for m in range(3)]


def attend(plan, h, proj_ref, bias):
    q, k, v = qkv_of(plan, proj_ref, h)
    scores = lax.dot_general(q, k, NT, preferred_element_type=jnp.float32)
    raised = jnp.exp(scores * plan["hd"] ** (-0.5) + bias)
    probs = raised / jnp.sum(raised, axis=-1, keepdims=True)
    attended = jnp.dot(probs.astype(jnp.bfloat16), v, preferred_element_type=jnp.float32)
    return probs, attended.astype(jnp.bfloat16)


def rows_of(plan, ref, second=False):
    if not plan["pairs"]:
        return ref[...]
    n = plan["T"] // plan["pairs"]
    at = n if second else 0
    return jnp.concatenate([ref[2 * n * i + at : 2 * n * i + at + n, :] for i in range(plan["pairs"])], axis=0)


def fwd_kernel(plan, place_ref, gates_ref, x_ref, gain_ref, bias_ref, cot_ref, *rest):
    n = plan["n_refs"]
    refs, rest = rest[:n], rest[n:]
    y_ref, proj_out, probs_out, att_out, w_ref, sems, proj_ref, probs_ref, att_ref, gated_scr = rest
    T, D, heads, hd, wide = dims_of(plan)
    layer, stride = plan["layer"], plan["og"] * ROWS
    weights = Weights(plan, place_ref, refs, w_ref, sems, (0, 1, 2, 3))
    x = rows_of(plan, x_ref)
    inverse, normed = norm(x, gain_ref[layer : layer + 1, :])
    project(plan, normed, weights, w_ref, proj_ref)
    free = 4
    saves = [pltpu.make_async_copy(proj_ref, proj_out, sems.at[free])]
    saves[0].start()
    bias = bias_ref[...]
    gated_scr[...] = jnp.zeros_like(gated_scr)
    for h in range(heads):
        probs, attended = attend(plan, h, proj_ref, bias)
        probs_ref[h] = probs
        saves.append(pltpu.make_async_copy(probs_ref.at[h], probs_out.at[h], sems.at[free + 2 + h]))
        saves[-1].start()
        att_ref[:, h * hd : (h + 1) * hd] = attended
        gated = (attended.astype(jnp.float32) * gates_ref[layer, h]).astype(jnp.bfloat16)
        gated_scr[:, h * stride : h * stride + hd] = gated
    saves.append(pltpu.make_async_copy(att_ref, att_out, sems.at[free + 1]))
    saves[-1].start()
    gated = gated_scr[...]
    lane_tiles = D // LANES
    for j in range(0, lane_tiles, 2):
        js = range(j, min(j + 2, lane_tiles))
        weights.need("o_tiles", js)
        w = jnp.concatenate([o_tile(plan, w_ref, i, range(heads)) for i in js], axis=1)
        cols = slice(j * LANES, j * LANES + LANES * len(js))
        y = (
            x[:, cols].astype(jnp.float32) + jnp.dot(gated, w, preferred_element_type=jnp.float32)
        ).astype(jnp.bfloat16)
        n = T // plan["to"]
        for i in range(plan["to"]):
            y_ref[2 * n * i : 2 * n * i + n, cols] = y[n * i : n * i + n]
    cot = rows_of(plan, cot_ref, True)
    for i in range(plan["to"]):
        y_ref[2 * n * i + n : 2 * n * i + 2 * n, :] = cot[n * i : n * i + n]
    for copy in saves:
        copy.wait()


def backward(plan, gates_ref, outgrad, x, gain, inverse, proj_ref, probs_of, att_of, sens,
             weights, w_ref, dgated_scr, dproj_scr):
    T, D, heads, hd, wide = dims_of(plan)
    layer, stride, hidden = plan["layer"], plan["og"] * ROWS, heads * hd
    lane_tiles = D // LANES
    weights.need("o_tiles", range(lane_tiles))
    for r in range(0, heads, 2):
        hs = min(2, heads - r)
        w = jnp.concatenate(
            [o_tile(plan, w_ref, i, range(r, r + hs)) for i in range(lane_tiles)],
            axis=1,
        )
        out = lax.dot_general(outgrad, w, NT, preferred_element_type=jnp.float32)
        dgated_scr[:, r * stride : (r + hs) * stride] = out.astype(jnp.bfloat16)
    if wide > 3 * hidden:
        dproj_scr[:, wide - LANES :] = jnp.zeros((T, LANES), jnp.bfloat16)
    lane = lax.broadcasted_iota(jnp.int32, (T, LANES), 1)
    for h in range(heads):
        q, k, v = qkv_of(plan, proj_ref, h)
        probs = probs_of(h)
        dgated = dgated_scr[:, h * stride : h * stride + hd].astype(jnp.float32)
        own = jnp.sum(dgated * att_of(h).astype(jnp.float32), axis=-1, keepdims=True)
        sens = jnp.where(lane == layer * heads + h, own, sens)
        datt = (dgated * gates_ref[layer, h]).astype(jnp.bfloat16)
        dprobs = lax.dot_general(datt, v, NT, preferred_element_type=jnp.float32)
        dvalues = lax.dot_general(
            probs.astype(jnp.bfloat16), datt, TN, preferred_element_type=jnp.float32
        )
        inner = jnp.sum(dprobs * probs, axis=-1, keepdims=True)
        dscores = (probs * (dprobs - inner) * hd ** (-0.5)).astype(jnp.bfloat16)
        dqueries = jnp.dot(dscores, k, preferred_element_type=jnp.float32)
        dkeys = lax.dot_general(dscores, q, TN, preferred_element_type=jnp.float32)
        for m, d in enumerate((dqueries, dkeys, dvalues)):
            at = m * hidden + h * hd
            dproj_scr[:, at : at + hd] = d.astype(jnp.bfloat16)
    weights.need("w_tiles", range(plan["tiles"]))
    dproj = dproj_scr[...]
    step = 2 * LANES
    parts = []
    for r in range(0, D, step):
        rr = min(step, D - r)
        w = jnp.concatenate(
            [
                w_tile(plan, w_ref, i, r // ROWS, rr // ROWS)
                for i in range(plan["tiles"])
            ],
            axis=1,
        )
        parts.append(lax.dot_general(dproj, w, NT, preferred_element_type=jnp.float32))
    dnormed = jnp.concatenate(parts, axis=1) * gain
    xf = x.astype(jnp.float32)
    mean = jnp.mean(xf * dnormed, axis=-1, keepdims=True)
    ingrad = (
        outgrad.astype(jnp.float32)
        + inverse * dnormed
        - xf * (inverse * inverse * inverse) * mean
    )
    return ingrad, sens


def both_kernel(plan, place_ref, gates_ref, x_ref, gain_ref, bias_ref, *rest):
    n = plan["n_refs"]
    refs, rest = rest[:n], rest[n:]
    g_ref, w_ref, sems, proj_scr, probs_scr, att_scr, dgated_scr, dproj_scr = rest
    T, D, heads, hd, wide = dims_of(plan)
    layer = plan["layer"]
    weights = Weights(plan, place_ref, refs, w_ref, sems, (0, 1, 2, 3))
    gain = gain_ref[layer : layer + 1, :]
    x = rows_of(plan, x_ref)
    inverse, normed = norm(x, gain)
    project(plan, normed, weights, w_ref, proj_scr)
    bias = bias_ref[...]
    for h in range(heads):
        probs, attended = attend(plan, h, proj_scr, bias)
        probs_scr[h] = probs
        att_scr[:, h * hd : (h + 1) * hd] = attended
    ingrad, sens = backward(
        plan, gates_ref, rows_of(plan, x_ref, True), x, gain, inverse, proj_scr,
        lambda h: probs_scr[h], lambda h: att_scr[:, h * hd : (h + 1) * hd],
        jnp.zeros((T, LANES), jnp.float32), weights, w_ref, dgated_scr, dproj_scr,
    )
    g_ref[:, :D] = ingrad.astype(jnp.bfloat16)
    g_ref[:, D:] = sens.astype(jnp.bfloat16)


def bwd_kernel(plan, place_ref, gates_ref, x_ref, gain_ref, *rest):
    T, D, heads, hd, wide = dims_of(plan)
    n_in, n_out = plan["n_in"], plan["n_out"]
    outgrad_refs, rest = rest[:n_in], rest[n_in:]
    proj_in, probs_in, att_in, *rest = rest
    n = plan["n_refs"]
    refs, outs, rest = rest[:n], rest[n : n + n_out], rest[n + n_out :]
    w_ref, sems, proj_ref, probs_ref, att_ref, dgated_scr, dproj_scr, flow_scr = rest
    layer = plan["layer"]
    loads = []
    for src, dst in ((att_in, att_ref), (proj_in, proj_ref), (probs_in, probs_ref)):
        loads.append(pltpu.make_async_copy(src, dst, sems.at[4 + len(loads)]))
    for copy in loads:
        copy.start()
    weights = Weights(plan, place_ref, refs, w_ref, sems, (3, 2, 1, 0))
    gain = gain_ref[layer : layer + 1, :]
    x = rows_of(plan, x_ref)
    inverse, _ = norm(x, gain)

    def block(count, k):
        rows = T // count
        return pl.ds(pl.multiple_of(place_ref[8 + k] * rows, rows), rows)

    outgrad_ref = outgrad_refs[0]
    if n_in > 1:
        outgrad_ref = dproj_scr.at[:, : D + LANES]
        for k, ref in enumerate(outgrad_refs):
            outgrad_ref[block(n_in, k), :] = ref[...]
    outgrad, sens = outgrad_ref[:, :D], outgrad_ref[:, D : D + LANES].astype(jnp.float32)
    for copy in loads:
        copy.wait()
    ingrad, sens = backward(
        plan, gates_ref, outgrad, x, gain, inverse,
        proj_ref, lambda h: probs_ref[h], lambda h: att_ref[:, h * hd : (h + 1) * hd],
        sens, weights, w_ref, dgated_scr, dproj_scr,
    )
    if plan["last"]:
        g_ref, sens_ref = outs
        cols, n_tiles = g_ref.shape[1], D // LANES
        for t in range(n_tiles):
            flow_scr[t] = ingrad[:, t * LANES : (t + 1) * LANES]
        flow_scr[n_tiles] = sens
        for j in range(cols):
            rows = pl.ds(j, T // cols, stride=cols)
            for t in range(n_tiles):
                g_ref[:, j, t * LANES : (t + 1) * LANES] = flow_scr[t, rows, :].astype(jnp.bfloat16)
            own = flow_scr[n_tiles, rows, :].astype(jnp.bfloat16)
            for m in range(sens_ref.shape[0]):
                sens_ref[m, :, j, :] = own[:, m * heads : (m + 1) * heads]
    elif n_out > 1:
        flow_scr[:, :D] = ingrad
        flow_scr[:, D:] = sens
        for k, out in enumerate(outs):
            out[...] = flow_scr[block(n_out, k), :].astype(jnp.bfloat16)
    else:
        outs[0][:, :D] = ingrad.astype(jnp.bfloat16)
        outs[0][:, D:] = sens.astype(jnp.bfloat16)


def call(kernel, plan, place, gates, weights, arrays, saved, outs, saves, scratch, flops):
    vmem = pl.BlockSpec(memory_space=pltpu.VMEM)
    smem = pl.BlockSpec(memory_space=pltpu.SMEM)
    plan = dict(plan, n_refs=len(weights))
    n_sems = 4 + 2 + plan["heads"]
    return pl.pallas_call(
        functools.partial(kernel, plan),
        out_shape=list(outs) + list(saves),
        in_specs=[smem, smem]
        + [vmem] * len(arrays)
        + [pl.BlockSpec(memory_space=pl.ANY)] * (len(saved) + len(weights)),
        out_specs=[vmem] * len(outs) + [HBM] * len(saves),
        scratch_shapes=[
            pltpu.VMEM((plan["n_blocks"], ROWS, LANES), jnp.bfloat16),
            pltpu.SemaphoreType.DMA((n_sems,)),
        ]
        + scratch,
        compiler_params=pltpu.CompilerParams(vmem_limit_bytes=plan["vmem"] * 2**20),
        cost_estimate=pl.CostEstimate(flops=flops, bytes_accessed=12 * 2**20, transcendentals=0),
    )(place, gates, *arrays, *saved, *weights)


def per_device(n_ha, n_wa, tokens, cotangent, w_qkv, w_out, gains, gates):
    videos, frames, rows, cols, D = tokens.shape
    layers, heads = gates.shape
    T = videos * frames * rows * cols
    width = w_qkv.shape[2]
    hidden = width // 3
    hd = hidden // heads
    tiles = ceil_to(width, LANES) // LANES
    og = ceil_to(hd, ROWS) // ROWS
    lane_tiles = D // LANES
    wide = tiles * LANES

    def flat(value):
        return jnp.swapaxes(value, 0, 1).reshape(T, D)

    idx = jnp.arange(T)
    fl = frames // n_ha * videos
    lines = [
        idx % (videos * rows * cols),
        (idx // (rows * cols)) % fl * cols + idx % cols,
        (idx // cols) % (T // (n_wa * cols)),
    ]
    biases = [jnp.where(line[:, None] == line[None, :], 0.0, -1e30).astype(jnp.float32) for line in lines]

    def swap(value, axis):
        return lax.all_to_all(value, axis, split_axis=0, concat_axis=0, tiled=True)

    home, teacher = flat(tokens), flat(cotangent)

    shard = w_qkv.shape[1]
    base = dict(T=T, D=D, heads=heads, hd=hd, tiles=tiles, og=og, square=False, pairs=0, vmem=60,
                w_tiles=(shard // ROWS, 0), o_tiles=(og, shard // ROWS * tiles))
    weights = []
    fast = n_ha == 4 and n_wa % 4 == 0 and shard % ROWS == 0 and w_out.shape[1] == hd
    if fast:
        routes = Routes(n_ha, n_wa)
        ha, wa = lax.axis_index("ha"), lax.axis_index("wa")
        n_z = n_wa // 2
        spot = ha * 2 + wa % 2
        spots = [spot ^ k for k in (0, 1, 4, 5, 2, 3, 6, 7)]
        place = jnp.stack(spots + [ha ^ k for k in range(n_ha)]).astype(jnp.int32)
        rg = shard // ROWS
        quarter = -(-(rg * tiles + og * lane_tiles) // 4)

        def addresses(at):
            return dict(
                w_at=lambda g, t: at(g // rg, *divmod(t * rg + g % rg, quarter)),
                o_at=lambda h, g, t: at(h, *divmod(rg * tiles + t * og + g, quarter)),
            )

        squarewise = addresses(
            lambda slot, part, inner: ((part * 2 + slot % 2) * n_z + slot // 2) * quarter + inner
        )
        slots = jnp.stack([(wa // 2) ^ k for k in range(n_z)]).astype(jnp.int32)
        base.update(n_line=n_z * quarter, n_blocks=4 * quarter * n_wa, quarter=quarter, n_parts=4)
        plans = [dict(base, layer=layer, square=True, **squarewise) for layer in range(layers)]

        own, later = own_quarters(ha.astype(jnp.int32)[None], w_qkv, w_out, quarter)
        line = routes.line(own)
        later = hand_on(later, line)
        far = [routes.send(later, wa_bits=2 * k) for k in range(1, n_z)]
        lines = []

        def stack_later(*squares):
            lines.extend(stacked(slots, [later] + far, 2, squares))
            return lines

        weights = [over_square(routes, line, [home, teacher] + biases, stack_later)]

        def gather(which, before, there):
            line = hand_on(lines[which], *weights[which][3:5])
            weights.append(over_square(routes, line, before, lambda *squares: there))

    else:
        full_qkv = lax.all_gather(w_qkv, "wa", axis=1, tiled=True)
        full_out = lax.all_gather(w_out, "wa", axis=1, tiled=True)
        n_rows = D // ROWS
        n_w = n_rows * tiles
        base["w_at"] = lambda g, t: t * n_rows + g
        base["o_at"] = lambda h, g, t: n_w + (h * lane_tiles + t) * og + g
        for layer in range(layers):
            by_head = full_out[layer].reshape(heads, hd, D)
            weights.append(
                [flat_blocks(blocks_of(full_qkv[layer]), *[blocks_of(by_head[h]) for h in range(heads)])]
            )
        n_blocks = weights[0][0].shape[0]
        base.update(n_blocks=n_blocks, quarter=n_blocks, n_parts=1)
        place = jnp.zeros((1,), jnp.int32)
        plans = [dict(base, layer=layer) for layer in range(layers)]

    bf16, f32 = jnp.bfloat16, jnp.float32
    act = jax.ShapeDtypeStruct((T, D), bf16)
    loaded = jax.ShapeDtypeStruct((T, D + LANES), bf16)
    dense = 2 * T * D * (width + hidden)

    keep = [
        jax.ShapeDtypeStruct((T, wide), bf16),
        jax.ShapeDtypeStruct((heads, T, T), f32),
        jax.ShapeDtypeStruct((T, hidden), bf16),
    ]
    kept = [pltpu.VMEM(array.shape, array.dtype) for array in keep]
    grads = [pltpu.VMEM((T, heads * og * ROWS), bf16), pltpu.VMEM((T, wide), bf16)]

    def forward(layer, x, cot, pairs, to):
        return call(
            fwd_kernel, dict(plans[layer], pairs=pairs, to=to), place, gates, weights[layer],
            [x, gains, biases[layer], cot], [], [jax.ShapeDtypeStruct((2 * T, D), bf16)], keep,
            kept + grads[:1], dense,
        )

    def back(layer, x, outgrads, saved, pairs, outs, last=False):
        plan = dict(plans[layer], vmem=24, pairs=pairs, n_in=len(outgrads), n_out=len(outs), last=last)
        flow = pltpu.VMEM((D // LANES + 1, T, LANES) if last else (T, D + LANES), f32)
        return call(
            bwd_kernel, plan, place, gates, weights[layer], [x, gains] + outgrads, saved, outs, [],
            kept + grads + [flow], dense,
        )

    after_time, *saved_time = forward(0, home, teacher, 0, n_ha)
    tall = swap(after_time, "ha")
    if fast:
        gather(0, [after_time], [tall])
    after_height, *saved_height = forward(1, tall, tall, n_ha, n_wa)
    if fast:
        gather(1, [after_height], [])
    across = swap(after_height, "wa")
    (grad,) = call(
        both_kernel, dict(plans[2], pairs=n_wa, vmem=24), place, gates, weights[2],
        [across, gains, biases[2]], [], [loaded], [], kept + grads, 2 * dense,
    )
    grad = swap(grad, "wa")
    if fast:
        block = jax.ShapeDtypeStruct((T // n_ha, D + LANES), bf16)
        blocks = back(1, tall, [grad], saved_height, n_ha, [block] * n_ha)
        outgrads = [blocks[0]] + [routes.send(blocks[k], ha_bits=k) for k in range(1, n_ha)]
    else:
        (grad,) = back(1, tall, [grad], saved_height, n_ha, [loaded])
        outgrads = [swap(grad, "ha")]
    ends = [
        jax.ShapeDtypeStruct((T // cols, cols, D), bf16),
        jax.ShapeDtypeStruct((layers, T // cols, cols, heads), bf16),
    ]
    grad, sens = back(0, home, outgrads, saved_time, 0, ends, True)
    token_grad = jnp.swapaxes(grad.reshape(frames, videos, rows, cols, D), 0, 1)
    sens = sens.reshape(layers, frames, videos, rows, cols, heads)
    return (token_grad, jnp.moveaxis(sens, 2, 0))


def solution(mesh):
    spec = P(None, None, "ha", "wa", None)
    in_specs = (spec, spec, P(None, "wa", None), P(None, "wa", None), P(), P())
    out_specs = (spec, P(None, None, None, "ha", "wa", None))
    n_ha, n_wa = mesh.shape["ha"], mesh.shape["wa"]
    return jax.shard_map(
        functools.partial(per_device, n_ha, n_wa),
        mesh=mesh, in_specs=in_specs, out_specs=out_specs, check_vma=False,
    )
```

```python
import functools

import jax
import jax.numpy as jnp
from jax import lax
from jax.experimental import pallas as pl
from jax.experimental.pallas import tpu as pltpu
from jax.sharding import PartitionSpec as P

LANES = 128
ROWS = 16
AXES = ("ha", "wa")
NT = (((1,), (1,)), ((), ()))
TN = (((0,), (0,)), ((), ()))


def ceil_to(value, unit):
    return -(-value // unit) * unit


def blocks_of(w):
    rows, cols = w.shape
    tall, wide = ceil_to(rows, ROWS), ceil_to(cols, LANES)
    w = jnp.pad(w, [(0, tall - rows), (0, wide - cols)])
    return jnp.moveaxis(w.reshape(tall // ROWS, ROWS, wide // LANES, LANES), 2, 0)


def flat_blocks(*arrays):
    return jnp.concatenate([a.reshape(-1, ROWS, LANES) for a in arrays])


HBM = pl.BlockSpec(memory_space=pl.ANY)


def hand_on(value, *after):
    def nothing(*refs):
        del refs

    return pl.pallas_call(
        nothing,
        out_shape=jax.ShapeDtypeStruct(value.shape, value.dtype),
        in_specs=[HBM] * (1 + len(after)),
        out_specs=HBM,
        input_output_aliases={0: 0},
        compiler_params=pltpu.CompilerParams(vmem_limit_bytes=2**20),
    )(value, *after)


def pack_kernel(part_ref, q_ref, o_ref, *rest):
    *outs, q_scr, o_scr = rest
    layers, rows, width = q_ref.shape
    hd = o_ref.shape[1]
    q_scr[:, :, :width] = q_ref[...]
    if q_scr.shape[2] > width:
        q_scr[:, :, width:] = jnp.zeros((layers, rows, q_scr.shape[2] - width), q_scr.dtype)
    o_scr[:, :hd, :] = o_ref[...]
    if o_scr.shape[1] > hd:
        o_scr[:, hd:, :] = jnp.zeros((layers, o_scr.shape[1] - hd, o_scr.shape[2]), o_scr.dtype)
    rg, og = rows // ROWS, o_scr.shape[1] // ROWS
    n_q, n_o = rg * (q_scr.shape[2] // LANES), og * (o_scr.shape[2] // LANES)
    quarter = outs[0].shape[0]

    def block(scr, layer, index, groups):
        row = pl.multiple_of(lax.rem(index, groups) * ROWS, ROWS)
        lane = pl.multiple_of(lax.div(index, groups) * LANES, LANES)
        return scr[layer, pl.ds(row, ROWS), pl.ds(lane, LANES)]

    def body(i, carry):
        index = part_ref[0] * quarter + i
        in_q = jnp.minimum(index, n_q - 1)
        in_o = jnp.clip(index - n_q, 0, n_o - 1)
        for layer in range(layers):
            out = outs[min(layer, 1)]
            out[i + max(layer - 1, 0) * quarter] = jnp.where(index < n_q, block(q_scr, layer, in_q, rg), block(o_scr, layer, in_o, og))
        return carry

    lax.fori_loop(0, quarter, body, 0)


def own_quarters(part, w_qkv, w_out, quarter):
    layers, rows, width = w_qkv.shape
    vmem = pl.BlockSpec(memory_space=pltpu.VMEM)
    return pl.pallas_call(
        pack_kernel,
        out_shape=[
            jax.ShapeDtypeStruct((n * quarter, ROWS, LANES), w_qkv.dtype) for n in (1, layers - 1)
        ],
        in_specs=[pl.BlockSpec(memory_space=pltpu.SMEM), vmem, vmem],
        out_specs=[vmem] * 2,
        scratch_shapes=[
            pltpu.VMEM((layers, rows, ceil_to(width, LANES)), w_qkv.dtype),
            pltpu.VMEM((layers, ceil_to(w_out.shape[1], ROWS), w_out.shape[2]), w_out.dtype),
        ],
        compiler_params=pltpu.CompilerParams(vmem_limit_bytes=60 * 2**20),
    )(part, w_qkv, w_out)


class Routes:
    def __init__(self, n_ha, n_wa):
        self.n_ha, self.n_wa = n_ha, n_wa

    def send(self, value, ha_bits=0, wa_bits=0):
        pairs = [
            (a * self.n_wa + b, (a ^ ha_bits) * self.n_wa + (b ^ wa_bits))
            for a in range(self.n_ha)
            for b in range(self.n_wa)
        ]
        return lax.ppermute(value, AXES, pairs)

    def core(self, value):
        return self.send(value, ha_bits=1)

    def x(self, value):
        return self.send(value, ha_bits=2)

    def y(self, value):
        return self.send(value, wa_bits=1)

    def line(self, value):
        groups = [
            [a * self.n_wa + 2 * z + y for z in range(self.n_wa // 2)]
            for a in range(self.n_ha)
            for y in range(2)
        ]
        return lax.all_gather(value, AXES, axis=0, tiled=True, axis_index_groups=groups)


def over_square(routes, line, before, between):
    half = line.shape[0] // 2
    over_y, over_x = routes.y(line), routes.x(line)
    over_y, over_x = hand_on(over_y, *before), hand_on(over_x, *before)
    low, high = routes.y(over_x[:half]), routes.x(over_y[half:])
    there = between(over_y, over_x)
    if there:
        low, high = hand_on(low, *there), hand_on(high, *there)
    mine = [hand_on(line, over_y, over_x), over_y, over_x, low, high]
    return mine + [routes.core(piece) for piece in mine]


def stack_kernel(n, slot_ref, *refs):
    ins, outs = refs[:n], refs[n:]
    rows = ins[0].shape[0] // len(outs)
    for j, out in enumerate(outs):
        for i in range(n):
            out[pl.ds(slot_ref[i] * rows, rows)] = ins[i][j * rows : (j + 1) * rows]


def stacked(slots, arrays, outs, after):
    n, rows = len(arrays), arrays[0].shape[0] // outs
    vmem = pl.BlockSpec(memory_space=pltpu.VMEM)
    line = jax.ShapeDtypeStruct((n * rows, ROWS, LANES), jnp.bfloat16)
    return pl.pallas_call(
        lambda *refs: stack_kernel(n, *refs[: n + 1], *refs[n + 1 + len(after) :]),
        out_shape=[line] * outs,
        in_specs=[pl.BlockSpec(memory_space=pltpu.SMEM)] + [vmem] * n + [HBM] * len(after),
        out_specs=[vmem] * outs,
        compiler_params=pltpu.CompilerParams(vmem_limit_bytes=6 * 2**20),
    )(slots, *arrays, *after)


def w_tile(plan, ref, tile, first=0, count=None):
    count = plan["D"] // ROWS - first if count is None else count
    return jnp.concatenate([ref[plan["w_at"](g, tile)] for g in range(first, first + count)], axis=0)


def o_tile(plan, ref, tile, heads):
    return jnp.concatenate(
        [ref[plan["o_at"](h, g, tile)] for h in heads for g in range(plan["og"])], axis=0
    )


class Weights:
    def __init__(self, plan, place_ref, refs, w_scr, sems, order):
        self.plan, self.w_scr, self.sems, self.here = plan, w_scr, sems, set()
        n_parts = plan["n_parts"]
        self.rows = w_scr.shape[0] // n_parts
        if not plan["square"]:
            for part in order if n_parts > 1 else [0]:
                self.copy(refs[0].at[pl.ds(part * self.rows, self.rows)], part * self.rows, part)
            return
        pieces = []
        for c in range(2):
            for which, ref in enumerate(refs[5 * c : 5 * c + 5]):
                spot = place_ref[4 * c + min(which, 3)]
                to = spot * plan["n_line"] + (ref.shape[0] if which == 4 else 0)
                pieces.append((ref, to, spot // 2))
        for wanted in order:
            for ref, to, part in pieces:

                @pl.when(part == wanted)
                def _():
                    self.copy(ref, to, part)

    def copy(self, ref, to, part):
        dst = self.w_scr.at[pl.ds(to, ref.shape[0])]
        pltpu.make_async_copy(ref, dst, self.sems.at[part]).start()

    def need(self, kind, tiles):
        per_tile, first = self.plan[kind]
        quarter = self.plan["quarter"]
        for part in range(self.plan["n_parts"]):
            used = any(
                first + t * per_tile < (part + 1) * quarter and first + (t + 1) * per_tile > part * quarter
                for t in tiles
            )
            if used and part not in self.here:
                self.here.add(part)
                rows = self.w_scr.at[pl.ds(part * self.rows, self.rows)]
                pltpu.make_async_copy(rows, rows, self.sems.at[part]).wait()


def dims_of(plan):
    return plan["T"], plan["D"], plan["heads"], plan["hd"], plan["tiles"] * LANES


def norm(x, gain):
    xf = x.astype(jnp.float32)
    inverse = lax.rsqrt(jnp.mean(xf * xf, axis=-1, keepdims=True) + 1e-06)
    return inverse, (xf * inverse * gain).astype(jnp.bfloat16)


def project(plan, normed, weights, w_ref, proj_scr):
    for j in range(0, plan["tiles"], 2):
        js = range(j, min(j + 2, plan["tiles"]))
        weights.need("w_tiles", js)
        w = jnp.concatenate([w_tile(plan, w_ref, i) for i in js], axis=1)
        proj_scr[:, j * LANES : j * LANES + LANES * len(js)] = jnp.dot(
            normed, w, preferred_element_type=jnp.float32
        ).astype(jnp.bfloat16)


def qkv_of(plan, proj_ref, h):
    hd, hidden = plan["hd"], plan["heads"] * plan["hd"]
    return [proj_ref[:, m * hidden + h * hd : m * hidden + (h + 1) * hd] for m in range(3)]


def attend(plan, h, proj_ref, bias):
    q, k, v = qkv_of(plan, proj_ref, h)
    scores = lax.dot_general(q, k, NT, preferred_element_type=jnp.float32)
    raised = jnp.exp(scores * plan["hd"] ** (-0.5) + bias)
    probs = raised / jnp.sum(raised, axis=-1, keepdims=True)
    attended = jnp.dot(probs.astype(jnp.bfloat16), v, preferred_element_type=jnp.float32)
    return probs, attended.astype(jnp.bfloat16)


def rows_of(plan, ref, second=False):
    if not plan["pairs"]:
        return ref[...]
    n = plan["T"] // plan["pairs"]
    at = n if second else 0
    return jnp.concatenate([ref[2 * n * i + at : 2 * n * i + at + n, :] for i in range(plan["pairs"])], axis=0)


def fwd_kernel(plan, place_ref, gates_ref, x_ref, gain_ref, bias_ref, cot_ref, *rest):
    n = plan["n_refs"]
    refs, rest = rest[:n], rest[n:]
    y_ref, proj_out, probs_out, att_out, w_ref, sems, proj_ref, probs_ref, att_ref, gated_scr = rest
    T, D, heads, hd, wide = dims_of(plan)
    layer, stride = plan["layer"], plan["og"] * ROWS
    weights = Weights(plan, place_ref, refs, w_ref, sems, (0, 1, 2, 3))
    x = rows_of(plan, x_ref)
    inverse, normed = norm(x, gain_ref[layer : layer + 1, :])
    project(plan, normed, weights, w_ref, proj_ref)
    free = 4
    saves = [pltpu.make_async_copy(proj_ref, proj_out, sems.at[free])]
    saves[0].start()
    bias = bias_ref[...]
    gated_scr[...] = jnp.zeros_like(gated_scr)
    for h in range(heads):
        probs, attended = attend(plan, h, proj_ref, bias)
        probs_ref[h] = probs
        saves.append(pltpu.make_async_copy(probs_ref.at[h], probs_out.at[h], sems.at[free + 2 + h]))
        saves[-1].start()
        att_ref[:, h * hd : (h + 1) * hd] = attended
        gated = (attended.astype(jnp.float32) * gates_ref[layer, h]).astype(jnp.bfloat16)
        gated_scr[:, h * stride : h * stride + hd] = gated
    saves.append(pltpu.make_async_copy(att_ref, att_out, sems.at[free + 1]))
    saves[-1].start()
    gated = gated_scr[...]
    lane_tiles = D // LANES
    for j in range(0, lane_tiles, 2):
        js = range(j, min(j + 2, lane_tiles))
        weights.need("o_tiles", js)
        w = jnp.concatenate([o_tile(plan, w_ref, i, range(heads)) for i in js], axis=1)
        cols = slice(j * LANES, j * LANES + LANES * len(js))
        y = (
            x[:, cols].astype(jnp.float32) + jnp.dot(gated, w, preferred_element_type=jnp.float32)
        ).astype(jnp.bfloat16)
        n = T // plan["to"]
        for i in range(plan["to"]):
            y_ref[2 * n * i : 2 * n * i + n, cols] = y[n * i : n * i + n]
    cot = rows_of(plan, cot_ref, True)
    for i in range(plan["to"]):
        y_ref[2 * n * i + n : 2 * n * i + 2 * n, :] = cot[n * i : n * i + n]
    for copy in saves:
        copy.wait()


def backward(plan, gates_ref, outgrad, x, gain, inverse, proj_ref, probs_of, att_of, sens,
             weights, w_ref, dgated_scr, dproj_scr):
    T, D, heads, hd, wide = dims_of(plan)
    layer, stride, hidden = plan["layer"], plan["og"] * ROWS, heads * hd
    lane_tiles = D // LANES
    weights.need("o_tiles", range(lane_tiles))
    for r in range(0, heads, 2):
        hs = min(2, heads - r)
        w = jnp.concatenate(
            [o_tile(plan, w_ref, i, range(r, r + hs)) for i in range(lane_tiles)],
            axis=1,
        )
        out = lax.dot_general(outgrad, w, NT, preferred_element_type=jnp.float32)
        dgated_scr[:, r * stride : (r + hs) * stride] = out.astype(jnp.bfloat16)
    if wide > 3 * hidden:
        dproj_scr[:, wide - LANES :] = jnp.zeros((T, LANES), jnp.bfloat16)
    lane = lax.broadcasted_iota(jnp.int32, (T, LANES), 1)
    for h in range(heads):
        q, k, v = qkv_of(plan, proj_ref, h)
        probs = probs_of(h)
        dgated = dgated_scr[:, h * stride : h * stride + hd].astype(jnp.float32)
        own = jnp.sum(dgated * att_of(h).astype(jnp.float32), axis=-1, keepdims=True)
        sens = jnp.where(lane == layer * heads + h, own, sens)
        datt = (dgated * gates_ref[layer, h]).astype(jnp.bfloat16)
        dprobs = lax.dot_general(datt, v, NT, preferred_element_type=jnp.float32)
        dvalues = lax.dot_general(
            probs.astype(jnp.bfloat16), datt, TN, preferred_element_type=jnp.float32
        )
        inner = jnp.sum(dprobs * probs, axis=-1, keepdims=True)
        dscores = (probs * (dprobs - inner) * hd ** (-0.5)).astype(jnp.bfloat16)
        dqueries = jnp.dot(dscores, k, preferred_element_type=jnp.float32)
        dkeys = lax.dot_general(dscores, q, TN, preferred_element_type=jnp.float32)
        for m, d in enumerate((dqueries, dkeys, dvalues)):
            at = m * hidden + h * hd
            dproj_scr[:, at : at + hd] = d.astype(jnp.bfloat16)
    weights.need("w_tiles", range(plan["tiles"]))
    dproj = dproj_scr[...]
    step = 2 * LANES
    parts = []
    for r in range(0, D, step):
        rr = min(step, D - r)
        w = jnp.concatenate(
            [
                w_tile(plan, w_ref, i, r // ROWS, rr // ROWS)
                for i in range(plan["tiles"])
            ],
            axis=1,
        )
        parts.append(lax.dot_general(dproj, w, NT, preferred_element_type=jnp.float32))
    dnormed = jnp.concatenate(parts, axis=1) * gain
    xf = x.astype(jnp.float32)
    mean = jnp.mean(xf * dnormed, axis=-1, keepdims=True)
    ingrad = (
        outgrad.astype(jnp.float32)
        + inverse * dnormed
        - xf * (inverse * inverse * inverse) * mean
    )
    return ingrad, sens


def both_kernel(plan, place_ref, gates_ref, x_ref, gain_ref, bias_ref, *rest):
    n = plan["n_refs"]
    refs, rest = rest[:n], rest[n:]
    g_ref, w_ref, sems, proj_scr, probs_scr, att_scr, dgated_scr, dproj_scr = rest
    T, D, heads, hd, wide = dims_of(plan)
    layer = plan["layer"]
    weights = Weights(plan, place_ref, refs, w_ref, sems, (0, 1, 2, 3))
    gain = gain_ref[layer : layer + 1, :]
    x = rows_of(plan, x_ref)
    inverse, normed = norm(x, gain)
    project(plan, normed, weights, w_ref, proj_scr)
    bias = bias_ref[...]
    for h in range(heads):
        probs, attended = attend(plan, h, proj_scr, bias)
        probs_scr[h] = probs
        att_scr[:, h * hd : (h + 1) * hd] = attended
    ingrad, sens = backward(
        plan, gates_ref, rows_of(plan, x_ref, True), x, gain, inverse, proj_scr,
        lambda h: probs_scr[h], lambda h: att_scr[:, h * hd : (h + 1) * hd],
        jnp.zeros((T, LANES), jnp.float32), weights, w_ref, dgated_scr, dproj_scr,
    )
    g_ref[:, :D] = ingrad.astype(jnp.bfloat16)
    g_ref[:, D:] = sens.astype(jnp.bfloat16)


def bwd_kernel(plan, place_ref, gates_ref, x_ref, gain_ref, *rest):
    T, D, heads, hd, wide = dims_of(plan)
    n_in, n_out = plan["n_in"], plan["n_out"]
    outgrad_refs, rest = rest[:n_in], rest[n_in:]
    proj_in, probs_in, att_in, *rest = rest
    n = plan["n_refs"]
    refs, outs, rest = rest[:n], rest[n : n + n_out], rest[n + n_out :]
    w_ref, sems, proj_ref, probs_ref, att_ref, dgated_scr, dproj_scr, flow_scr = rest
    layer = plan["layer"]
    loads = []
    for src, dst in ((att_in, att_ref), (proj_in, proj_ref), (probs_in, probs_ref)):
        loads.append(pltpu.make_async_copy(src, dst, sems.at[4 + len(loads)]))
    for copy in loads:
        copy.start()
    weights = Weights(plan, place_ref, refs, w_ref, sems, (3, 2, 1, 0))
    gain = gain_ref[layer : layer + 1, :]
    x = rows_of(plan, x_ref)
    inverse, _ = norm(x, gain)

    def block(count, k):
        rows = T // count
        return pl.ds(pl.multiple_of(place_ref[8 + k] * rows, rows), rows)

    outgrad_ref = outgrad_refs[0]
    if n_in > 1:
        outgrad_ref = dproj_scr.at[:, : D + LANES]
        for k, ref in enumerate(outgrad_refs):
            outgrad_ref[block(n_in, k), :] = ref[...]
    outgrad, sens = outgrad_ref[:, :D], outgrad_ref[:, D : D + LANES].astype(jnp.float32)
    for copy in loads:
        copy.wait()
    ingrad, sens = backward(
        plan, gates_ref, outgrad, x, gain, inverse,
        proj_ref, lambda h: probs_ref[h], lambda h: att_ref[:, h * hd : (h + 1) * hd],
        sens, weights, w_ref, dgated_scr, dproj_scr,
    )
    if plan["last"]:
        g_ref, sens_ref = outs
        cols, n_tiles = g_ref.shape[1], D // LANES
        for t in range(n_tiles):
            flow_scr[t] = ingrad[:, t * LANES : (t + 1) * LANES]
        flow_scr[n_tiles] = sens
        for j in range(cols):
            rows = pl.ds(j, T // cols, stride=cols)
            for t in range(n_tiles):
                g_ref[:, j, t * LANES : (t + 1) * LANES] = flow_scr[t, rows, :].astype(jnp.bfloat16)
            own = flow_scr[n_tiles, rows, :].astype(jnp.bfloat16)
            for m in range(sens_ref.shape[0]):
                sens_ref[m, :, j, :] = own[:, m * heads : (m + 1) * heads]
    elif n_out > 1:
        flow_scr[:, :D] = ingrad
        flow_scr[:, D:] = sens
        for k, out in enumerate(outs):
            out[...] = flow_scr[block(n_out, k), :].astype(jnp.bfloat16)
    else:
        outs[0][:, :D] = ingrad.astype(jnp.bfloat16)
        outs[0][:, D:] = sens.astype(jnp.bfloat16)


def call(kernel, plan, place, gates, weights, arrays, saved, outs, saves, scratch, flops):
    vmem = pl.BlockSpec(memory_space=pltpu.VMEM)
    smem = pl.BlockSpec(memory_space=pltpu.SMEM)
    plan = dict(plan, n_refs=len(weights))
    n_sems = 4 + 2 + plan["heads"]
    return pl.pallas_call(
        functools.partial(kernel, plan),
        out_shape=list(outs) + list(saves),
        in_specs=[smem, smem]
        + [vmem] * len(arrays)
        + [pl.BlockSpec(memory_space=pl.ANY)] * (len(saved) + len(weights)),
        out_specs=[vmem] * len(outs) + [HBM] * len(saves),
        scratch_shapes=[
            pltpu.VMEM((plan["n_blocks"], ROWS, LANES), jnp.bfloat16),
            pltpu.SemaphoreType.DMA((n_sems,)),
        ]
        + scratch,
        compiler_params=pltpu.CompilerParams(vmem_limit_bytes=plan["vmem"] * 2**20),
        cost_estimate=pl.CostEstimate(flops=flops, bytes_accessed=12 * 2**20, transcendentals=0),
    )(place, gates, *arrays, *saved, *weights)


def per_device(n_ha, n_wa, tokens, cotangent, w_qkv, w_out, gains, gates):
    videos, frames, rows, cols, D = tokens.shape
    layers, heads = gates.shape
    T = videos * frames * rows * cols
    width = w_qkv.shape[2]
    hidden = width // 3
    hd = hidden // heads
    tiles = ceil_to(width, LANES) // LANES
    og = ceil_to(hd, ROWS) // ROWS
    lane_tiles = D // LANES
    wide = tiles * LANES

    def flat(value):
        return jnp.swapaxes(value, 0, 1).reshape(T, D)

    idx = jnp.arange(T)
    fl = frames // n_ha * videos
    lines = [
        idx % (videos * rows * cols),
        (idx // (rows * cols)) % fl * cols + idx % cols,
        (idx // cols) % (T // (n_wa * cols)),
    ]
    biases = [jnp.where(line[:, None] == line[None, :], 0.0, -1e30).astype(jnp.float32) for line in lines]

    def swap(value, axis):
        return lax.all_to_all(value, axis, split_axis=0, concat_axis=0, tiled=True)

    home, teacher = flat(tokens), flat(cotangent)

    shard = w_qkv.shape[1]
    base = dict(T=T, D=D, heads=heads, hd=hd, tiles=tiles, og=og, square=False, pairs=0, vmem=60,
                w_tiles=(shard // ROWS, 0), o_tiles=(og, shard // ROWS * tiles))
    weights = []
    fast = n_ha == 4 and n_wa % 4 == 0 and shard % ROWS == 0 and w_out.shape[1] == hd
    if fast:
        routes = Routes(n_ha, n_wa)
        ha, wa = lax.axis_index("ha"), lax.axis_index("wa")
        n_z = n_wa // 2
        spot = ha * 2 + wa % 2
        spots = [spot ^ k for k in (0, 1, 4, 5, 2, 3, 6, 7)]
        place = jnp.stack(spots + [ha ^ k for k in range(n_ha)]).astype(jnp.int32)
        rg = shard // ROWS
        quarter = -(-(rg * tiles + og * lane_tiles) // 4)

        def addresses(at):
            return dict(
                w_at=lambda g, t: at(g // rg, *divmod(t * rg + g % rg, quarter)),
                o_at=lambda h, g, t: at(h, *divmod(rg * tiles + t * og + g, quarter)),
            )

        squarewise = addresses(
            lambda slot, part, inner: ((part * 2 + slot % 2) * n_z + slot // 2) * quarter + inner
        )
        slots = jnp.stack([(wa // 2) ^ k for k in range(n_z)]).astype(jnp.int32)
        base.update(n_line=n_z * quarter, n_blocks=4 * quarter * n_wa, quarter=quarter, n_parts=4)
        plans = [dict(base, layer=layer, square=True, **squarewise) for layer in range(layers)]

        own, later = own_quarters(ha.astype(jnp.int32)[None], w_qkv, w_out, quarter)
        line = routes.line(own)
        later = hand_on(later, line)
        far = [routes.send(later, wa_bits=2 * k) for k in range(1, n_z)]
        lines = []

        def stack_later(*squares):
            lines.extend(stacked(slots, [later] + far, 2, squares))
            return lines

        weights = [over_square(routes, line, [home, teacher] + biases, stack_later)]

        def gather(which, before, there):
            line = hand_on(lines[which], *weights[which][3:5])
            weights.append(over_square(routes, line, before, lambda *squares: there))

    else:
        full_qkv = lax.all_gather(w_qkv, "wa", axis=1, tiled=True)
        full_out = lax.all_gather(w_out, "wa", axis=1, tiled=True)
        n_rows = D // ROWS
        n_w = n_rows * tiles
        base["w_at"] = lambda g, t: t * n_rows + g
        base["o_at"] = lambda h, g, t: n_w + (h * lane_tiles + t) * og + g
        for layer in range(layers):
            by_head = full_out[layer].reshape(heads, hd, D)
            weights.append(
                [flat_blocks(blocks_of(full_qkv[layer]), *[blocks_of(by_head[h]) for h in range(heads)])]
            )
        n_blocks = weights[0][0].shape[0]
        base.update(n_blocks=n_blocks, quarter=n_blocks, n_parts=1)
        place = jnp.zeros((1,), jnp.int32)
        plans = [dict(base, layer=layer) for layer in range(layers)]

    bf16, f32 = jnp.bfloat16, jnp.float32
    act = jax.ShapeDtypeStruct((T, D), bf16)
    loaded = jax.ShapeDtypeStruct((T, D + LANES), bf16)
    dense = 2 * T * D * (width + hidden)

    keep = [
        jax.ShapeDtypeStruct((T, wide), bf16),
        jax.ShapeDtypeStruct((heads, T, T), f32),
        jax.ShapeDtypeStruct((T, hidden), bf16),
    ]
    kept = [pltpu.VMEM(array.shape, array.dtype) for array in keep]
    grads = [pltpu.VMEM((T, heads * og * ROWS), bf16), pltpu.VMEM((T, wide), bf16)]

    def forward(layer, x, cot, pairs, to):
        return call(
            fwd_kernel, dict(plans[layer], pairs=pairs, to=to), place, gates, weights[layer],
            [x, gains, biases[layer], cot], [], [jax.ShapeDtypeStruct((2 * T, D), bf16)], keep,
            kept + grads[:1], dense,
        )

    def back(layer, x, outgrads, saved, pairs, outs, last=False):
        plan = dict(plans[layer], vmem=24, pairs=pairs, n_in=len(outgrads), n_out=len(outs), last=last)
        flow = pltpu.VMEM((D // LANES + 1, T, LANES) if last else (T, D + LANES), f32)
        return call(
            bwd_kernel, plan, place, gates, weights[layer], [x, gains] + outgrads, saved, outs, [],
            kept + grads + [flow], dense,
        )

    after_time, *saved_time = forward(0, home, teacher, 0, n_ha)
    tall = swap(after_time, "ha")
    if fast:
        gather(0, [after_time], [tall])
    after_height, *saved_height = forward(1, tall, tall, n_ha, n_wa)
    if fast:
        gather(1, [after_height], [])
    across = swap(after_height, "wa")
    (grad,) = call(
        both_kernel, dict(plans[2], pairs=n_wa, vmem=24), place, gates, weights[2],
        [across, gains, biases[2]], [], [loaded], [], kept + grads, 2 * dense,
    )
    grad = swap(grad, "wa")
    if fast:
        block = jax.ShapeDtypeStruct((T // n_ha, D + LANES), bf16)
        blocks = back(1, tall, [grad], saved_height, n_ha, [block] * n_ha)
        outgrads = [blocks[0]] + [routes.send(blocks[k], ha_bits=k) for k in range(1, n_ha)]
    else:
        (grad,) = back(1, tall, [grad], saved_height, n_ha, [loaded])
        outgrads = [swap(grad, "ha")]
    ends = [
        jax.ShapeDtypeStruct((T // cols, cols, D), bf16),
        jax.ShapeDtypeStruct((layers, T // cols, cols, heads), bf16),
    ]
    grad, sens = back(0, home, outgrads, saved_time, 0, ends, True)
    token_grad = jnp.swapaxes(grad.reshape(frames, videos, rows, cols, D), 0, 1)
    sens = sens.reshape(layers, frames, videos, rows, cols, heads)
    return (token_grad, jnp.moveaxis(sens, 2, 0))


def solution(mesh):
    spec = P(None, None, "ha", "wa", None)
    in_specs = (spec, spec, P(None, "wa", None), P(None, "wa", None), P(), P())
    out_specs = (spec, P(None, None, None, "ha", "wa", None))
    n_ha, n_wa = mesh.shape["ha"], mesh.shape["wa"]
    return jax.shard_map(
        functools.partial(per_device, n_ha, n_wa),
        mesh=mesh, in_specs=in_specs, out_specs=out_specs, check_vma=False,
    )
```

```python
import functools

import jax
import jax.numpy as jnp
from jax import lax
from jax.experimental import pallas as pl
from jax.experimental.pallas import tpu as pltpu
from jax.sharding import PartitionSpec as P

LANES = 128
ROWS = 16
AXES = ("ha", "wa")
NT = (((1,), (1,)), ((), ()))
TN = (((0,), (0,)), ((), ()))


def ceil_to(value, unit):
    return -(-value // unit) * unit


def blocks_of(w):
    rows, cols = w.shape
    tall, wide = ceil_to(rows, ROWS), ceil_to(cols, LANES)
    w = jnp.pad(w, [(0, tall - rows), (0, wide - cols)])
    return jnp.moveaxis(w.reshape(tall // ROWS, ROWS, wide // LANES, LANES), 2, 0)


def flat_blocks(*arrays):
    return jnp.concatenate([a.reshape(-1, ROWS, LANES) for a in arrays])


HBM = pl.BlockSpec(memory_space=pl.ANY)


def hand_on(value, *after):
    def nothing(*refs):
        del refs

    return pl.pallas_call(
        nothing,
        out_shape=jax.ShapeDtypeStruct(value.shape, value.dtype),
        in_specs=[HBM] * (1 + len(after)),
        out_specs=HBM,
        input_output_aliases={0: 0},
        compiler_params=pltpu.CompilerParams(vmem_limit_bytes=2**20),
    )(value, *after)


def pack_kernel(part_ref, q_ref, o_ref, *rest):
    *outs, q_scr, o_scr = rest
    layers, rows, width = q_ref.shape
    hd = o_ref.shape[1]
    q_scr[:, :, :width] = q_ref[...]
    if q_scr.shape[2] > width:
        q_scr[:, :, width:] = jnp.zeros((layers, rows, q_scr.shape[2] - width), q_scr.dtype)
    o_scr[:, :hd, :] = o_ref[...]
    if o_scr.shape[1] > hd:
        o_scr[:, hd:, :] = jnp.zeros((layers, o_scr.shape[1] - hd, o_scr.shape[2]), o_scr.dtype)
    rg, og = rows // ROWS, o_scr.shape[1] // ROWS
    n_q, n_o = rg * (q_scr.shape[2] // LANES), og * (o_scr.shape[2] // LANES)
    quarter = outs[0].shape[0]

    def block(scr, layer, index, groups):
        row = pl.multiple_of(lax.rem(index, groups) * ROWS, ROWS)
        lane = pl.multiple_of(lax.div(index, groups) * LANES, LANES)
        return scr[layer, pl.ds(row, ROWS), pl.ds(lane, LANES)]

    def body(i, carry):
        index = part_ref[0] * quarter + i
        in_q = jnp.minimum(index, n_q - 1)
        in_o = jnp.clip(index - n_q, 0, n_o - 1)
        for layer in range(layers):
            out = outs[min(layer, 1)]
            out[i + max(layer - 1, 0) * quarter] = jnp.where(index < n_q, block(q_scr, layer, in_q, rg), block(o_scr, layer, in_o, og))
        return carry

    lax.fori_loop(0, quarter, body, 0)


def own_quarters(part, w_qkv, w_out, quarter):
    layers, rows, width = w_qkv.shape
    vmem = pl.BlockSpec(memory_space=pltpu.VMEM)
    return pl.pallas_call(
        pack_kernel,
        out_shape=[
            jax.ShapeDtypeStruct((n * quarter, ROWS, LANES), w_qkv.dtype) for n in (1, layers - 1)
        ],
        in_specs=[pl.BlockSpec(memory_space=pltpu.SMEM), vmem, vmem],
        out_specs=[vmem] * 2,
        scratch_shapes=[
            pltpu.VMEM((layers, rows, ceil_to(width, LANES)), w_qkv.dtype),
            pltpu.VMEM((layers, ceil_to(w_out.shape[1], ROWS), w_out.shape[2]), w_out.dtype),
        ],
        compiler_params=pltpu.CompilerParams(vmem_limit_bytes=60 * 2**20),
    )(part, w_qkv, w_out)


class Routes:
    def __init__(self, n_ha, n_wa):
        self.n_ha, self.n_wa = n_ha, n_wa

    def send(self, value, ha_bits=0, wa_bits=0):
        pairs = [
            (a * self.n_wa + b, (a ^ ha_bits) * self.n_wa + (b ^ wa_bits))
            for a in range(self.n_ha)
            for b in range(self.n_wa)
        ]
        return lax.ppermute(value, AXES, pairs)

    def core(self, value):
        return self.send(value, ha_bits=1)

    def x(self, value):
        return self.send(value, ha_bits=2)

    def y(self, value):
        return self.send(value, wa_bits=1)

    def line(self, value):
        groups = [
            [a * self.n_wa + 2 * z + y for z in range(self.n_wa // 2)]
            for a in range(self.n_ha)
            for y in range(2)
        ]
        return lax.all_gather(value, AXES, axis=0, tiled=True, axis_index_groups=groups)


def over_square(routes, line, before, between):
    half = line.shape[0] // 2
    over_y, over_x = routes.y(line), routes.x(line)
    over_y, over_x = hand_on(over_y, *before), hand_on(over_x, *before)
    low, high = routes.y(over_x[:half]), routes.x(over_y[half:])
    there = between(over_y, over_x)
    if there:
        low, high = hand_on(low, *there), hand_on(high, *there)
    mine = [hand_on(line, over_y, over_x), over_y, over_x, low, high]
    return mine + [routes.core(piece) for piece in mine]


def stack_kernel(n, slot_ref, *refs):
    ins, outs = refs[:n], refs[n:]
    rows = ins[0].shape[0] // len(outs)
    for j, out in enumerate(outs):
        for i in range(n):
            out[pl.ds(slot_ref[i] * rows, rows)] = ins[i][j * rows : (j + 1) * rows]


def stacked(slots, arrays, outs, after):
    n, rows = len(arrays), arrays[0].shape[0] // outs
    vmem = pl.BlockSpec(memory_space=pltpu.VMEM)
    line = jax.ShapeDtypeStruct((n * rows, ROWS, LANES), jnp.bfloat16)
    return pl.pallas_call(
        lambda *refs: stack_kernel(n, *refs[: n + 1], *refs[n + 1 + len(after) :]),
        out_shape=[line] * outs,
        in_specs=[pl.BlockSpec(memory_space=pltpu.SMEM)] + [vmem] * n + [HBM] * len(after),
        out_specs=[vmem] * outs,
        compiler_params=pltpu.CompilerParams(vmem_limit_bytes=6 * 2**20),
    )(slots, *arrays, *after)


def w_tile(plan, ref, tile, first=0, count=None):
    count = plan["D"] // ROWS - first if count is None else count
    return jnp.concatenate([ref[plan["w_at"](g, tile)] for g in range(first, first + count)], axis=0)


def o_tile(plan, ref, tile, heads):
    return jnp.concatenate(
        [ref[plan["o_at"](h, g, tile)] for h in heads for g in range(plan["og"])], axis=0
    )


class Weights:
    def __init__(self, plan, place_ref, refs, w_scr, sems, order):
        self.plan, self.w_scr, self.sems, self.here = plan, w_scr, sems, set()
        n_parts = plan["n_parts"]
        self.rows = w_scr.shape[0] // n_parts
        if not plan["square"]:
            for part in order if n_parts > 1 else [0]:
                self.copy(refs[0].at[pl.ds(part * self.rows, self.rows)], part * self.rows, part)
            return
        pieces = []
        for c in range(2):
            for which, ref in enumerate(refs[5 * c : 5 * c + 5]):
                spot = place_ref[4 * c + min(which, 3)]
                to = spot * plan["n_line"] + (ref.shape[0] if which == 4 else 0)
                pieces.append((ref, to, spot // 2))
        for wanted in order:
            for ref, to, part in pieces:

                @pl.when(part == wanted)
                def _():
                    self.copy(ref, to, part)

    def copy(self, ref, to, part):
        dst = self.w_scr.at[pl.ds(to, ref.shape[0])]
        pltpu.make_async_copy(ref, dst, self.sems.at[part]).start()

    def need(self, kind, tiles):
        per_tile, first = self.plan[kind]
        quarter = self.plan["quarter"]
        for part in range(self.plan["n_parts"]):
            used = any(
                first + t * per_tile < (part + 1) * quarter and first + (t + 1) * per_tile > part * quarter
                for t in tiles
            )
            if used and part not in self.here:
                self.here.add(part)
                rows = self.w_scr.at[pl.ds(part * self.rows, self.rows)]
                pltpu.make_async_copy(rows, rows, self.sems.at[part]).wait()


def dims_of(plan):
    return plan["T"], plan["D"], plan["heads"], plan["hd"], plan["tiles"] * LANES


def norm(x, gain):
    xf = x.astype(jnp.float32)
    inverse = lax.rsqrt(jnp.mean(xf * xf, axis=-1, keepdims=True) + 1e-06)
    return inverse, (xf * inverse * gain).astype(jnp.bfloat16)


def project(plan, normed, weights, w_ref, proj_scr):
    for j in range(0, plan["tiles"], 2):
        js = range(j, min(j + 2, plan["tiles"]))
        weights.need("w_tiles", js)
        w = jnp.concatenate([w_tile(plan, w_ref, i) for i in js], axis=1)
        proj_scr[:, j * LANES : j * LANES + LANES * len(js)] = jnp.dot(
            normed, w, preferred_element_type=jnp.float32
        ).astype(jnp.bfloat16)


def qkv_of(plan, proj_ref, h):
    hd, hidden = plan["hd"], plan["heads"] * plan["hd"]
    return [proj_ref[:, m * hidden + h * hd : m * hidden + (h + 1) * hd] for m in range(3)]


def attend(plan, h, proj_ref, bias):
    q, k, v = qkv_of(plan, proj_ref, h)
    scores = lax.dot_general(q, k, NT, preferred_element_type=jnp.float32)
    raised = jnp.exp(scores * plan["hd"] ** (-0.5) + bias)
    probs = raised / jnp.sum(raised, axis=-1, keepdims=True)
    attended = jnp.dot(probs.astype(jnp.bfloat16), v, preferred_element_type=jnp.float32)
    return probs, attended.astype(jnp.bfloat16)


def rows_of(plan, ref, second=False):
    if not plan["pairs"]:
        return ref[...]
    n = plan["T"] // plan["pairs"]
    at = n if second else 0
    return jnp.concatenate([ref[2 * n * i + at : 2 * n * i + at + n, :] for i in range(plan["pairs"])], axis=0)


def fwd_kernel(plan, place_ref, gates_ref, x_ref, gain_ref, bias_ref, cot_ref, *rest):
    n = plan["n_refs"]
    refs, rest = rest[:n], rest[n:]
    y_ref, proj_out, probs_out, att_out, w_ref, sems, proj_ref, probs_ref, att_ref, gated_scr = rest
    T, D, heads, hd, wide = dims_of(plan)
    layer, stride = plan["layer"], plan["og"] * ROWS
    weights = Weights(plan, place_ref, refs, w_ref, sems, (0, 1, 2, 3))
    x = rows_of(plan, x_ref)
    inverse, normed = norm(x, gain_ref[layer : layer + 1, :])
    project(plan, normed, weights, w_ref, proj_ref)
    free = 4
    saves = [pltpu.make_async_copy(proj_ref, proj_out, sems.at[free])]
    saves[0].start()
    bias = bias_ref[...]
    gated_scr[...] = jnp.zeros_like(gated_scr)
    for h in range(heads):
        probs, attended = attend(plan, h, proj_ref, bias)
        probs_ref[h] = probs
        saves.append(pltpu.make_async_copy(probs_ref.at[h], probs_out.at[h], sems.at[free + 2 + h]))
        saves[-1].start()
        att_ref[:, h * hd : (h + 1) * hd] = attended
        gated = (attended.astype(jnp.float32) * gates_ref[layer, h]).astype(jnp.bfloat16)
        gated_scr[:, h * stride : h * stride + hd] = gated
    saves.append(pltpu.make_async_copy(att_ref, att_out, sems.at[free + 1]))
    saves[-1].start()
    gated = gated_scr[...]
    lane_tiles = D // LANES
    for j in range(0, lane_tiles, 2):
        js = range(j, min(j + 2, lane_tiles))
        weights.need("o_tiles", js)
        w = jnp.concatenate([o_tile(plan, w_ref, i, range(heads)) for i in js], axis=1)
        cols = slice(j * LANES, j * LANES + LANES * len(js))
        y = (
            x[:, cols].astype(jnp.float32) + jnp.dot(gated, w, preferred_element_type=jnp.float32)
        ).astype(jnp.bfloat16)
        n = T // plan["to"]
        for i in range(plan["to"]):
            y_ref[2 * n * i : 2 * n * i + n, cols] = y[n * i : n * i + n]
    cot = rows_of(plan, cot_ref, True)
    for i in range(plan["to"]):
        y_ref[2 * n * i + n : 2 * n * i + 2 * n, :] = cot[n * i : n * i + n]
    for copy in saves:
        copy.wait()


def backward(plan, gates_ref, outgrad, x, gain, inverse, proj_ref, probs_of, att_of, sens,
             weights, w_ref, dgated_scr, dproj_scr):
    T, D, heads, hd, wide = dims_of(plan)
    layer, stride, hidden = plan["layer"], plan["og"] * ROWS, heads * hd
    lane_tiles = D // LANES
    weights.need("o_tiles", range(lane_tiles))
    for r in range(0, heads, 2):
        hs = min(2, heads - r)
        w = jnp.concatenate(
            [o_tile(plan, w_ref, i, range(r, r + hs)) for i in range(lane_tiles)],
            axis=1,
        )
        out = lax.dot_general(outgrad, w, NT, preferred_element_type=jnp.float32)
        dgated_scr[:, r * stride : (r + hs) * stride] = out.astype(jnp.bfloat16)
    if wide > 3 * hidden:
        dproj_scr[:, wide - LANES :] = jnp.zeros((T, LANES), jnp.bfloat16)
    lane = lax.broadcasted_iota(jnp.int32, (T, LANES), 1)
    for h in range(heads):
        q, k, v = qkv_of(plan, proj_ref, h)
        probs = probs_of(h)
        dgated = dgated_scr[:, h * stride : h * stride + hd].astype(jnp.float32)
        own = jnp.sum(dgated * att_of(h).astype(jnp.float32), axis=-1, keepdims=True)
        sens = jnp.where(lane == layer * heads + h, own, sens)
        datt = (dgated * gates_ref[layer, h]).astype(jnp.bfloat16)
        dprobs = lax.dot_general(datt, v, NT, preferred_element_type=jnp.float32)
        dvalues = lax.dot_general(
            probs.astype(jnp.bfloat16), datt, TN, preferred_element_type=jnp.float32
        )
        inner = jnp.sum(dprobs * probs, axis=-1, keepdims=True)
        dscores = (probs * (dprobs - inner) * hd ** (-0.5)).astype(jnp.bfloat16)
        dqueries = jnp.dot(dscores, k, preferred_element_type=jnp.float32)
        dkeys = lax.dot_general(dscores, q, TN, preferred_element_type=jnp.float32)
        for m, d in enumerate((dqueries, dkeys, dvalues)):
            at = m * hidden + h * hd
            dproj_scr[:, at : at + hd] = d.astype(jnp.bfloat16)
    weights.need("w_tiles", range(plan["tiles"]))
    dproj = dproj_scr[...]
    step = 2 * LANES
    parts = []
    for r in range(0, D, step):
        rr = min(step, D - r)
        w = jnp.concatenate(
            [
                w_tile(plan, w_ref, i, r // ROWS, rr // ROWS)
                for i in range(plan["tiles"])
            ],
            axis=1,
        )
        parts.append(lax.dot_general(dproj, w, NT, preferred_element_type=jnp.float32))
    dnormed = jnp.concatenate(parts, axis=1) * gain
    xf = x.astype(jnp.float32)
    mean = jnp.mean(xf * dnormed, axis=-1, keepdims=True)
    ingrad = (
        outgrad.astype(jnp.float32)
        + inverse * dnormed
        - xf * (inverse * inverse * inverse) * mean
    )
    return ingrad, sens


def both_kernel(plan, place_ref, gates_ref, x_ref, gain_ref, bias_ref, *rest):
    n = plan["n_refs"]
    refs, rest = rest[:n], rest[n:]
    g_ref, w_ref, sems, proj_scr, probs_scr, att_scr, dgated_scr, dproj_scr = rest
    T, D, heads, hd, wide = dims_of(plan)
    layer = plan["layer"]
    weights = Weights(plan, place_ref, refs, w_ref, sems, (0, 1, 2, 3))
    gain = gain_ref[layer : layer + 1, :]
    x = rows_of(plan, x_ref)
    inverse, normed = norm(x, gain)
    project(plan, normed, weights, w_ref, proj_scr)
    bias = bias_ref[...]
    for h in range(heads):
        probs, attended = attend(plan, h, proj_scr, bias)
        probs_scr[h] = probs
        att_scr[:, h * hd : (h + 1) * hd] = attended
    ingrad, sens = backward(
        plan, gates_ref, rows_of(plan, x_ref, True), x, gain, inverse, proj_scr,
        lambda h: probs_scr[h], lambda h: att_scr[:, h * hd : (h + 1) * hd],
        jnp.zeros((T, LANES), jnp.float32), weights, w_ref, dgated_scr, dproj_scr,
    )
    g_ref[:, :D] = ingrad.astype(jnp.bfloat16)
    g_ref[:, D:] = sens.astype(jnp.bfloat16)


def bwd_kernel(plan, place_ref, gates_ref, x_ref, gain_ref, *rest):
    T, D, heads, hd, wide = dims_of(plan)
    n_in, n_out = plan["n_in"], plan["n_out"]
    outgrad_refs, rest = rest[:n_in], rest[n_in:]
    proj_in, probs_in, att_in, *rest = rest
    n = plan["n_refs"]
    refs, outs, rest = rest[:n], rest[n : n + n_out], rest[n + n_out :]
    w_ref, sems, proj_ref, probs_ref, att_ref, dgated_scr, dproj_scr, flow_scr = rest
    layer = plan["layer"]
    loads = []
    for src, dst in ((att_in, att_ref), (proj_in, proj_ref), (probs_in, probs_ref)):
        loads.append(pltpu.make_async_copy(src, dst, sems.at[4 + len(loads)]))
    for copy in loads:
        copy.start()
    weights = Weights(plan, place_ref, refs, w_ref, sems, (3, 2, 1, 0))
    gain = gain_ref[layer : layer + 1, :]
    x = rows_of(plan, x_ref)
    inverse, _ = norm(x, gain)

    def block(count, k):
        rows = T // count
        return pl.ds(pl.multiple_of(place_ref[8 + k] * rows, rows), rows)

    outgrad_ref = outgrad_refs[0]
    if n_in > 1:
        outgrad_ref = dproj_scr.at[:, : D + LANES]
        for k, ref in enumerate(outgrad_refs):
            outgrad_ref[block(n_in, k), :] = ref[...]
    outgrad, sens = outgrad_ref[:, :D], outgrad_ref[:, D : D + LANES].astype(jnp.float32)
    for copy in loads:
        copy.wait()
    ingrad, sens = backward(
        plan, gates_ref, outgrad, x, gain, inverse,
        proj_ref, lambda h: probs_ref[h], lambda h: att_ref[:, h * hd : (h + 1) * hd],
        sens, weights, w_ref, dgated_scr, dproj_scr,
    )
    if plan["last"]:
        g_ref, sens_ref = outs
        cols, n_tiles = g_ref.shape[1], D // LANES
        for t in range(n_tiles):
            flow_scr[t] = ingrad[:, t * LANES : (t + 1) * LANES]
        flow_scr[n_tiles] = sens
        for j in range(cols):
            rows = pl.ds(j, T // cols, stride=cols)
            for t in range(n_tiles):
                g_ref[:, j, t * LANES : (t + 1) * LANES] = flow_scr[t, rows, :].astype(jnp.bfloat16)
            own = flow_scr[n_tiles, rows, :].astype(jnp.bfloat16)
            for m in range(sens_ref.shape[0]):
                sens_ref[m, :, j, :] = own[:, m * heads : (m + 1) * heads]
    elif n_out > 1:
        flow_scr[:, :D] = ingrad
        flow_scr[:, D:] = sens
        for k, out in enumerate(outs):
            out[...] = flow_scr[block(n_out, k), :].astype(jnp.bfloat16)
    else:
        outs[0][:, :D] = ingrad.astype(jnp.bfloat16)
        outs[0][:, D:] = sens.astype(jnp.bfloat16)


def call(kernel, plan, place, gates, weights, arrays, saved, outs, saves, scratch, flops):
    vmem = pl.BlockSpec(memory_space=pltpu.VMEM)
    smem = pl.BlockSpec(memory_space=pltpu.SMEM)
    plan = dict(plan, n_refs=len(weights))
    n_sems = 4 + 2 + plan["heads"]
    return pl.pallas_call(
        functools.partial(kernel, plan),
        out_shape=list(outs) + list(saves),
        in_specs=[smem, smem]
        + [vmem] * len(arrays)
        + [pl.BlockSpec(memory_space=pl.ANY)] * (len(saved) + len(weights)),
        out_specs=[vmem] * len(outs) + [HBM] * len(saves),
        scratch_shapes=[
            pltpu.VMEM((plan["n_blocks"], ROWS, LANES), jnp.bfloat16),
            pltpu.SemaphoreType.DMA((n_sems,)),
        ]
        + scratch,
        compiler_params=pltpu.CompilerParams(vmem_limit_bytes=plan["vmem"] * 2**20),
        cost_estimate=pl.CostEstimate(flops=flops, bytes_accessed=12 * 2**20, transcendentals=0),
    )(place, gates, *arrays, *saved, *weights)


def per_device(n_ha, n_wa, tokens, cotangent, w_qkv, w_out, gains, gates):
    videos, frames, rows, cols, D = tokens.shape
    layers, heads = gates.shape
    T = videos * frames * rows * cols
    width = w_qkv.shape[2]
    hidden = width // 3
    hd = hidden // heads
    tiles = ceil_to(width, LANES) // LANES
    og = ceil_to(hd, ROWS) // ROWS
    lane_tiles = D // LANES
    wide = tiles * LANES

    def flat(value):
        return jnp.swapaxes(value, 0, 1).reshape(T, D)

    idx = jnp.arange(T)
    fl = frames // n_ha * videos
    lines = [
        idx % (videos * rows * cols),
        (idx // (rows * cols)) % fl * cols + idx % cols,
        (idx // cols) % (T // (n_wa * cols)),
    ]
    biases = [jnp.where(line[:, None] == line[None, :], 0.0, -1e30).astype(jnp.float32) for line in lines]

    def swap(value, axis):
        return lax.all_to_all(value, axis, split_axis=0, concat_axis=0, tiled=True)

    home, teacher = flat(tokens), flat(cotangent)

    shard = w_qkv.shape[1]
    base = dict(T=T, D=D, heads=heads, hd=hd, tiles=tiles, og=og, square=False, pairs=0, vmem=60,
                w_tiles=(shard // ROWS, 0), o_tiles=(og, shard // ROWS * tiles))
    weights = []
    fast = n_ha == 4 and n_wa % 4 == 0 and n_wa & (n_wa - 1) == 0 and shard % ROWS == 0 and w_out.shape[1] == hd
    if fast:
        routes = Routes(n_ha, n_wa)
        ha, wa = lax.axis_index("ha"), lax.axis_index("wa")
        n_z = n_wa // 2
        spot = ha * 2 + wa % 2
        spots = [spot ^ k for k in (0, 1, 4, 5, 2, 3, 6, 7)]
        place = jnp.stack(spots + [ha ^ k for k in range(n_ha)]).astype(jnp.int32)
        rg = shard // ROWS
        quarter = -(-(rg * tiles + og * lane_tiles) // 4)

        def addresses(at):
            return dict(
                w_at=lambda g, t: at(g // rg, *divmod(t * rg + g % rg, quarter)),
                o_at=lambda h, g, t: at(h, *divmod(rg * tiles + t * og + g, quarter)),
            )

        squarewise = addresses(
            lambda slot, part, inner: ((part * 2 + slot % 2) * n_z + slot // 2) * quarter + inner
        )
        slots = jnp.stack([(wa // 2) ^ k for k in range(n_z)]).astype(jnp.int32)
        base.update(n_line=n_z * quarter, n_blocks=4 * quarter * n_wa, quarter=quarter, n_parts=4)
        plans = [dict(base, layer=layer, square=True, **squarewise) for layer in range(layers)]

        own, later = own_quarters(ha.astype(jnp.int32)[None], w_qkv, w_out, quarter)
        line = routes.line(own)
        later = hand_on(later, line)
        got, bit = {0: later}, n_z // 2
        while bit:
            got.update({k ^ bit: routes.send(got[k], wa_bits=2 * bit) for k in list(got)})
            bit //= 2
        far = [got[k] for k in range(1, n_z)]
        lines = []

        def stack_later(*squares):
            lines.extend(stacked(slots, [later] + far, 2, squares))
            return lines

        weights = [over_square(routes, line, [home, teacher] + biases + far[:1], stack_later)]

        def gather(which, before, there):
            line = hand_on(lines[which], *weights[which][3:5])
            weights.append(over_square(routes, line, before, lambda *squares: there))

    else:
        full_qkv = lax.all_gather(w_qkv, "wa", axis=1, tiled=True)
        full_out = lax.all_gather(w_out, "wa", axis=1, tiled=True)
        n_rows = D // ROWS
        n_w = n_rows * tiles
        base["w_at"] = lambda g, t: t * n_rows + g
        base["o_at"] = lambda h, g, t: n_w + (h * lane_tiles + t) * og + g
        for layer in range(layers):
            by_head = full_out[layer].reshape(heads, hd, D)
            weights.append(
                [flat_blocks(blocks_of(full_qkv[layer]), *[blocks_of(by_head[h]) for h in range(heads)])]
            )
        n_blocks = weights[0][0].shape[0]
        base.update(n_blocks=n_blocks, quarter=n_blocks, n_parts=1)
        place = jnp.zeros((1,), jnp.int32)
        plans = [dict(base, layer=layer) for layer in range(layers)]

    bf16, f32 = jnp.bfloat16, jnp.float32
    act = jax.ShapeDtypeStruct((T, D), bf16)
    loaded = jax.ShapeDtypeStruct((T, D + LANES), bf16)
    dense = 2 * T * D * (width + hidden)

    keep = [
        jax.ShapeDtypeStruct((T, wide), bf16),
        jax.ShapeDtypeStruct((heads, T, T), f32),
        jax.ShapeDtypeStruct((T, hidden), bf16),
    ]
    kept = [pltpu.VMEM(array.shape, array.dtype) for array in keep]
    grads = [pltpu.VMEM((T, heads * og * ROWS), bf16), pltpu.VMEM((T, wide), bf16)]

    def forward(layer, x, cot, pairs, to):
        return call(
            fwd_kernel, dict(plans[layer], pairs=pairs, to=to), place, gates, weights[layer],
            [x, gains, biases[layer], cot], [], [jax.ShapeDtypeStruct((2 * T, D), bf16)], keep,
            kept + grads[:1], dense,
        )

    def back(layer, x, outgrads, saved, pairs, outs, last=False):
        plan = dict(plans[layer], vmem=24, pairs=pairs, n_in=len(outgrads), n_out=len(outs), last=last)
        flow = pltpu.VMEM((D // LANES + 1, T, LANES) if last else (T, D + LANES), f32)
        return call(
            bwd_kernel, plan, place, gates, weights[layer], [x, gains] + outgrads, saved, outs, [],
            kept + grads + [flow], dense,
        )

    after_time, *saved_time = forward(0, home, teacher, 0, n_ha)
    tall = swap(after_time, "ha")
    if fast:
        gather(0, [after_time], [tall])
    after_height, *saved_height = forward(1, tall, tall, n_ha, n_wa)
    if fast:
        gather(1, [after_height], [])
    across = swap(after_height, "wa")
    (grad,) = call(
        both_kernel, dict(plans[2], pairs=n_wa, vmem=24), place, gates, weights[2],
        [across, gains, biases[2]], [], [loaded], [], kept + grads, 2 * dense,
    )
    grad = swap(grad, "wa")
    if fast:
        block = jax.ShapeDtypeStruct((T // n_ha, D + LANES), bf16)
        blocks = back(1, tall, [grad], saved_height, n_ha, [block] * n_ha)
        outgrads = [blocks[0]] + [routes.send(blocks[k], ha_bits=k) for k in range(1, n_ha)]
    else:
        (grad,) = back(1, tall, [grad], saved_height, n_ha, [loaded])
        outgrads = [swap(grad, "ha")]
    ends = [
        jax.ShapeDtypeStruct((T // cols, cols, D), bf16),
        jax.ShapeDtypeStruct((layers, T // cols, cols, heads), bf16),
    ]
    grad, sens = back(0, home, outgrads, saved_time, 0, ends, True)
    token_grad = jnp.swapaxes(grad.reshape(frames, videos, rows, cols, D), 0, 1)
    sens = sens.reshape(layers, frames, videos, rows, cols, heads)
    return (token_grad, jnp.moveaxis(sens, 2, 0))


def solution(mesh):
    spec = P(None, None, "ha", "wa", None)
    in_specs = (spec, spec, P(None, "wa", None), P(None, "wa", None), P(), P())
    out_specs = (spec, P(None, None, None, "ha", "wa", None))
    n_ha, n_wa = mesh.shape["ha"], mesh.shape["wa"]
    return jax.shard_map(
        functools.partial(per_device, n_ha, n_wa),
        mesh=mesh, in_specs=in_specs, out_specs=out_specs, check_vma=False,
    )
```

```python
import functools

import jax
import jax.numpy as jnp
from jax import lax
from jax.experimental import pallas as pl
from jax.experimental.pallas import tpu as pltpu
from jax.sharding import PartitionSpec as P

LANES = 128
ROWS = 16
AXES = ("ha", "wa")
NT = (((1,), (1,)), ((), ()))
TN = (((0,), (0,)), ((), ()))


def ceil_to(value, unit):
    return -(-value // unit) * unit


def blocks_of(w):
    rows, cols = w.shape
    tall, wide = ceil_to(rows, ROWS), ceil_to(cols, LANES)
    w = jnp.pad(w, [(0, tall - rows), (0, wide - cols)])
    return jnp.moveaxis(w.reshape(tall // ROWS, ROWS, wide // LANES, LANES), 2, 0)


def flat_blocks(*arrays):
    return jnp.concatenate([a.reshape(-1, ROWS, LANES) for a in arrays])


HBM = pl.BlockSpec(memory_space=pl.ANY)


def hand_on(value, *after):
    def nothing(*refs):
        del refs

    return pl.pallas_call(
        nothing,
        out_shape=jax.ShapeDtypeStruct(value.shape, value.dtype),
        in_specs=[HBM] * (1 + len(after)),
        out_specs=HBM,
        input_output_aliases={0: 0},
        compiler_params=pltpu.CompilerParams(vmem_limit_bytes=2**20),
    )(value, *after)


def pack_kernel(part_ref, q_ref, o_ref, *rest):
    *outs, q_scr, o_scr = rest
    layers, rows, width = q_ref.shape
    hd = o_ref.shape[1]
    q_scr[:, :, :width] = q_ref[...]
    if q_scr.shape[2] > width:
        q_scr[:, :, width:] = jnp.zeros((layers, rows, q_scr.shape[2] - width), q_scr.dtype)
    o_scr[:, :hd, :] = o_ref[...]
    if o_scr.shape[1] > hd:
        o_scr[:, hd:, :] = jnp.zeros((layers, o_scr.shape[1] - hd, o_scr.shape[2]), o_scr.dtype)
    rg, og = rows // ROWS, o_scr.shape[1] // ROWS
    n_q, n_o = rg * (q_scr.shape[2] // LANES), og * (o_scr.shape[2] // LANES)
    quarter = outs[0].shape[0]

    def block(scr, layer, index, groups):
        row = pl.multiple_of(lax.rem(index, groups) * ROWS, ROWS)
        lane = pl.multiple_of(lax.div(index, groups) * LANES, LANES)
        return scr[layer, pl.ds(row, ROWS), pl.ds(lane, LANES)]

    def body(i, carry):
        index = part_ref[0] * quarter + i
        in_q = jnp.minimum(index, n_q - 1)
        in_o = jnp.clip(index - n_q, 0, n_o - 1)
        for layer in range(layers):
            out = outs[min(layer, 1)]
            out[i + max(layer - 1, 0) * quarter] = jnp.where(index < n_q, block(q_scr, layer, in_q, rg), block(o_scr, layer, in_o, og))
        return carry

    lax.fori_loop(0, quarter, body, 0)


def own_quarters(part, w_qkv, w_out, quarter):
    layers, rows, width = w_qkv.shape
    vmem = pl.BlockSpec(memory_space=pltpu.VMEM)
    return pl.pallas_call(
        pack_kernel,
        out_shape=[
            jax.ShapeDtypeStruct((n * quarter, ROWS, LANES), w_qkv.dtype) for n in (1, layers - 1)
        ],
        in_specs=[pl.BlockSpec(memory_space=pltpu.SMEM), vmem, vmem],
        out_specs=[vmem] * 2,
        scratch_shapes=[
            pltpu.VMEM((layers, rows, ceil_to(width, LANES)), w_qkv.dtype),
            pltpu.VMEM((layers, ceil_to(w_out.shape[1], ROWS), w_out.shape[2]), w_out.dtype),
        ],
        compiler_params=pltpu.CompilerParams(vmem_limit_bytes=60 * 2**20),
    )(part, w_qkv, w_out)


class Routes:
    def __init__(self, n_ha, n_wa):
        self.n_ha, self.n_wa = n_ha, n_wa

    def send(self, value, ha_bits=0, wa_bits=0):
        pairs = [
            (a * self.n_wa + b, (a ^ ha_bits) * self.n_wa + (b ^ wa_bits))
            for a in range(self.n_ha)
            for b in range(self.n_wa)
        ]
        return lax.ppermute(value, AXES, pairs)

    def core(self, value):
        return self.send(value, ha_bits=1)

    def x(self, value):
        return self.send(value, ha_bits=2)

    def y(self, value):
        return self.send(value, wa_bits=1)

    def line(self, value):
        groups = [
            [a * self.n_wa + 2 * z + y for z in range(self.n_wa // 2)]
            for a in range(self.n_ha)
            for y in range(2)
        ]
        return lax.all_gather(value, AXES, axis=0, tiled=True, axis_index_groups=groups)


def half_of(value, second):
    n = value.shape[0] // 2
    first = n if second else 0

    def kernel(source, out):
        out[...] = source[first : first + n]

    vmem = pl.BlockSpec(memory_space=pltpu.VMEM)
    return pl.pallas_call(
        kernel,
        out_shape=jax.ShapeDtypeStruct((n,) + value.shape[1:], value.dtype),
        in_specs=[vmem],
        out_specs=vmem,
        compiler_params=pltpu.CompilerParams(vmem_limit_bytes=3 * 2**20),
    )(value)


def over_square(routes, line, before, between):
    over_y, over_x = routes.y(line), routes.x(line)
    over_y, over_x = hand_on(over_y, *before), hand_on(over_x, *before)
    low, high = routes.y(half_of(over_x, False)), routes.x(half_of(over_y, True))
    there = between(over_y, over_x)
    if there:
        low, high = hand_on(low, *there), hand_on(high, *there)
    mine = [hand_on(line, over_y, over_x), over_y, over_x, low, high]
    return mine + [routes.core(piece) for piece in mine]


def stack_kernel(n, slot_ref, *refs):
    ins, outs = refs[:n], refs[n:]
    rows = ins[0].shape[0] // len(outs)
    for j, out in enumerate(outs):
        for i in range(n):
            out[pl.ds(slot_ref[i] * rows, rows)] = ins[i][j * rows : (j + 1) * rows]


def stacked(slots, arrays, outs, after):
    n, rows = len(arrays), arrays[0].shape[0] // outs
    vmem = pl.BlockSpec(memory_space=pltpu.VMEM)
    line = jax.ShapeDtypeStruct((n * rows, ROWS, LANES), jnp.bfloat16)
    return pl.pallas_call(
        lambda *refs: stack_kernel(n, *refs[: n + 1], *refs[n + 1 + len(after) :]),
        out_shape=[line] * outs,
        in_specs=[pl.BlockSpec(memory_space=pltpu.SMEM)] + [vmem] * n + [HBM] * len(after),
        out_specs=[vmem] * outs,
        compiler_params=pltpu.CompilerParams(vmem_limit_bytes=6 * 2**20),
    )(slots, *arrays, *after)


def w_tile(plan, ref, tile, first=0, count=None):
    count = plan["D"] // ROWS - first if count is None else count
    return jnp.concatenate([ref[plan["w_at"](g, tile)] for g in range(first, first + count)], axis=0)


def o_tile(plan, ref, tile, heads):
    return jnp.concatenate(
        [ref[plan["o_at"](h, g, tile)] for h in heads for g in range(plan["og"])], axis=0
    )


class Weights:
    def __init__(self, plan, place_ref, refs, w_scr, sems, order):
        self.plan, self.w_scr, self.sems, self.here = plan, w_scr, sems, set()
        n_parts = plan["n_parts"]
        self.rows = w_scr.shape[0] // n_parts
        if not plan["square"]:
            for part in order if n_parts > 1 else [0]:
                self.copy(refs[0].at[pl.ds(part * self.rows, self.rows)], part * self.rows, part)
            return
        pieces = []
        for c in range(2):
            for which, ref in enumerate(refs[5 * c : 5 * c + 5]):
                spot = place_ref[4 * c + min(which, 3)]
                to = spot * plan["n_line"] + (ref.shape[0] if which == 4 else 0)
                pieces.append((ref, to, spot // 2))
        for wanted in order:
            for ref, to, part in pieces:

                @pl.when(part == wanted)
                def _():
                    self.copy(ref, to, part)

    def copy(self, ref, to, part):
        dst = self.w_scr.at[pl.ds(to, ref.shape[0])]
        pltpu.make_async_copy(ref, dst, self.sems.at[part]).start()

    def need(self, kind, tiles):
        per_tile, first = self.plan[kind]
        quarter = self.plan["quarter"]
        for part in range(self.plan["n_parts"]):
            used = any(
                first + t * per_tile < (part + 1) * quarter and first + (t + 1) * per_tile > part * quarter
                for t in tiles
            )
            if used and part not in self.here:
                self.here.add(part)
                rows = self.w_scr.at[pl.ds(part * self.rows, self.rows)]
                pltpu.make_async_copy(rows, rows, self.sems.at[part]).wait()


def dims_of(plan):
    return plan["T"], plan["D"], plan["heads"], plan["hd"], plan["tiles"] * LANES


def norm(x, gain):
    xf = x.astype(jnp.float32)
    inverse = lax.rsqrt(jnp.mean(xf * xf, axis=-1, keepdims=True) + 1e-06)
    return inverse, (xf * inverse * gain).astype(jnp.bfloat16)


def project(plan, normed, weights, w_ref, proj_scr):
    for j in range(0, plan["tiles"], 2):
        js = range(j, min(j + 2, plan["tiles"]))
        weights.need("w_tiles", js)
        w = jnp.concatenate([w_tile(plan, w_ref, i) for i in js], axis=1)
        proj_scr[:, j * LANES : j * LANES + LANES * len(js)] = jnp.dot(
            normed, w, preferred_element_type=jnp.float32
        ).astype(jnp.bfloat16)


def qkv_of(plan, proj_ref, h):
    hd, hidden = plan["hd"], plan["heads"] * plan["hd"]
    return [proj_ref[:, m * hidden + h * hd : m * hidden + (h + 1) * hd] for m in range(3)]


def attend(plan, h, proj_ref, bias):
    q, k, v = qkv_of(plan, proj_ref, h)
    scores = lax.dot_general(q, k, NT, preferred_element_type=jnp.float32)
    raised = jnp.exp(scores * plan["hd"] ** (-0.5) + bias)
    probs = raised / jnp.sum(raised, axis=-1, keepdims=True)
    attended = jnp.dot(probs.astype(jnp.bfloat16), v, preferred_element_type=jnp.float32)
    return probs, attended.astype(jnp.bfloat16)


def rows_of(plan, ref, second=False):
    if not plan["pairs"]:
        return ref[...]
    n = plan["T"] // plan["pairs"]
    at = n if second else 0
    return jnp.concatenate([ref[2 * n * i + at : 2 * n * i + at + n, :] for i in range(plan["pairs"])], axis=0)


def fwd_kernel(plan, place_ref, gates_ref, x_ref, gain_ref, bias_ref, cot_ref, *rest):
    n = plan["n_refs"]
    refs, rest = rest[:n], rest[n:]
    y_ref, proj_out, probs_out, att_out, w_ref, sems, proj_ref, probs_ref, att_ref, gated_scr = rest
    T, D, heads, hd, wide = dims_of(plan)
    layer, stride = plan["layer"], plan["og"] * ROWS
    weights = Weights(plan, place_ref, refs, w_ref, sems, (0, 1, 2, 3))
    x = rows_of(plan, x_ref)
    inverse, normed = norm(x, gain_ref[layer : layer + 1, :])
    project(plan, normed, weights, w_ref, proj_ref)
    free = 4
    saves = [pltpu.make_async_copy(proj_ref, proj_out, sems.at[free])]
    saves[0].start()
    bias = bias_ref[...]
    gated_scr[...] = jnp.zeros_like(gated_scr)
    for h in range(heads):
        probs, attended = attend(plan, h, proj_ref, bias)
        probs_ref[h] = probs
        saves.append(pltpu.make_async_copy(probs_ref.at[h], probs_out.at[h], sems.at[free + 2 + h]))
        saves[-1].start()
        att_ref[:, h * hd : (h + 1) * hd] = attended
        gated = (attended.astype(jnp.float32) * gates_ref[layer, h]).astype(jnp.bfloat16)
        gated_scr[:, h * stride : h * stride + hd] = gated
    saves.append(pltpu.make_async_copy(att_ref, att_out, sems.at[free + 1]))
    saves[-1].start()
    gated = gated_scr[...]
    lane_tiles = D // LANES
    for j in range(0, lane_tiles, 2):
        js = range(j, min(j + 2, lane_tiles))
        weights.need("o_tiles", js)
        w = jnp.concatenate([o_tile(plan, w_ref, i, range(heads)) for i in js], axis=1)
        cols = slice(j * LANES, j * LANES + LANES * len(js))
        y = (
            x[:, cols].astype(jnp.float32) + jnp.dot(gated, w, preferred_element_type=jnp.float32)
        ).astype(jnp.bfloat16)
        n = T // plan["to"]
        for i in range(plan["to"]):
            y_ref[2 * n * i : 2 * n * i + n, cols] = y[n * i : n * i + n]
    cot = rows_of(plan, cot_ref, True)
    for i in range(plan["to"]):
        y_ref[2 * n * i + n : 2 * n * i + 2 * n, :] = cot[n * i : n * i + n]
    for copy in saves:
        copy.wait()


def backward(plan, gates_ref, outgrad, x, gain, inverse, proj_ref, probs_of, att_of, sens,
             weights, w_ref, dgated_scr, dproj_scr):
    T, D, heads, hd, wide = dims_of(plan)
    layer, stride, hidden = plan["layer"], plan["og"] * ROWS, heads * hd
    lane_tiles = D // LANES
    weights.need("o_tiles", range(lane_tiles))
    for r in range(0, heads, 2):
        hs = min(2, heads - r)
        w = jnp.concatenate(
            [o_tile(plan, w_ref, i, range(r, r + hs)) for i in range(lane_tiles)],
            axis=1,
        )
        out = lax.dot_general(outgrad, w, NT, preferred_element_type=jnp.float32)
        dgated_scr[:, r * stride : (r + hs) * stride] = out.astype(jnp.bfloat16)
    if wide > 3 * hidden:
        dproj_scr[:, wide - LANES :] = jnp.zeros((T, LANES), jnp.bfloat16)
    lane = lax.broadcasted_iota(jnp.int32, (T, LANES), 1)
    for h in range(heads):
        q, k, v = qkv_of(plan, proj_ref, h)
        probs = probs_of(h)
        dgated = dgated_scr[:, h * stride : h * stride + hd].astype(jnp.float32)
        own = jnp.sum(dgated * att_of(h).astype(jnp.float32), axis=-1, keepdims=True)
        sens = jnp.where(lane == layer * heads + h, own, sens)
        datt = (dgated * gates_ref[layer, h]).astype(jnp.bfloat16)
        dprobs = lax.dot_general(datt, v, NT, preferred_element_type=jnp.float32)
        dvalues = lax.dot_general(
            probs.astype(jnp.bfloat16), datt, TN, preferred_element_type=jnp.float32
        )
        inner = jnp.sum(dprobs * probs, axis=-1, keepdims=True)
        dscores = (probs * (dprobs - inner) * hd ** (-0.5)).astype(jnp.bfloat16)
        dqueries = jnp.dot(dscores, k, preferred_element_type=jnp.float32)
        dkeys = lax.dot_general(dscores, q, TN, preferred_element_type=jnp.float32)
        for m, d in enumerate((dqueries, dkeys, dvalues)):
            at = m * hidden + h * hd
            dproj_scr[:, at : at + hd] = d.astype(jnp.bfloat16)
    weights.need("w_tiles", range(plan["tiles"]))
    dproj = dproj_scr[...]
    step = 2 * LANES
    parts = []
    for r in range(0, D, step):
        rr = min(step, D - r)
        w = jnp.concatenate(
            [
                w_tile(plan, w_ref, i, r // ROWS, rr // ROWS)
                for i in range(plan["tiles"])
            ],
            axis=1,
        )
        parts.append(lax.dot_general(dproj, w, NT, preferred_element_type=jnp.float32))
    dnormed = jnp.concatenate(parts, axis=1) * gain
    xf = x.astype(jnp.float32)
    mean = jnp.mean(xf * dnormed, axis=-1, keepdims=True)
    ingrad = (
        outgrad.astype(jnp.float32)
        + inverse * dnormed
        - xf * (inverse * inverse * inverse) * mean
    )
    return ingrad, sens


def both_kernel(plan, place_ref, gates_ref, x_ref, gain_ref, bias_ref, *rest):
    n = plan["n_refs"]
    refs, rest = rest[:n], rest[n:]
    g_ref, w_ref, sems, proj_scr, probs_scr, att_scr, dgated_scr, dproj_scr = rest
    T, D, heads, hd, wide = dims_of(plan)
    layer = plan["layer"]
    weights = Weights(plan, place_ref, refs, w_ref, sems, (0, 1, 2, 3))
    gain = gain_ref[layer : layer + 1, :]
    x = rows_of(plan, x_ref)
    inverse, normed = norm(x, gain)
    project(plan, normed, weights, w_ref, proj_scr)
    bias = bias_ref[...]
    for h in range(heads):
        probs, attended = attend(plan, h, proj_scr, bias)
        probs_scr[h] = probs
        att_scr[:, h * hd : (h + 1) * hd] = attended
    ingrad, sens = backward(
        plan, gates_ref, rows_of(plan, x_ref, True), x, gain, inverse, proj_scr,
        lambda h: probs_scr[h], lambda h: att_scr[:, h * hd : (h + 1) * hd],
        jnp.zeros((T, LANES), jnp.float32), weights, w_ref, dgated_scr, dproj_scr,
    )
    g_ref[:, :D] = ingrad.astype(jnp.bfloat16)
    g_ref[:, D:] = sens.astype(jnp.bfloat16)


def bwd_kernel(plan, place_ref, gates_ref, x_ref, gain_ref, *rest):
    T, D, heads, hd, wide = dims_of(plan)
    n_in, n_out = plan["n_in"], plan["n_out"]
    outgrad_refs, rest = rest[:n_in], rest[n_in:]
    proj_in, probs_in, att_in, *rest = rest
    n = plan["n_refs"]
    refs, outs, rest = rest[:n], rest[n : n + n_out], rest[n + n_out :]
    w_ref, sems, proj_ref, probs_ref, att_ref, dgated_scr, dproj_scr, flow_scr = rest
    layer = plan["layer"]
    loads = []
    for src, dst in ((att_in, att_ref), (proj_in, proj_ref), (probs_in, probs_ref)):
        loads.append(pltpu.make_async_copy(src, dst, sems.at[4 + len(loads)]))
    for copy in loads:
        copy.start()
    weights = Weights(plan, place_ref, refs, w_ref, sems, (3, 2, 1, 0))
    gain = gain_ref[layer : layer + 1, :]
    x = rows_of(plan, x_ref)
    inverse, _ = norm(x, gain)

    def block(count, k):
        rows = T // count
        return pl.ds(pl.multiple_of(place_ref[8 + k] * rows, rows), rows)

    outgrad_ref = outgrad_refs[0]
    if n_in > 1:
        outgrad_ref = dproj_scr.at[:, : D + LANES]
        for k, ref in enumerate(outgrad_refs):
            outgrad_ref[block(n_in, k), :] = ref[...]
    outgrad, sens = outgrad_ref[:, :D], outgrad_ref[:, D : D + LANES].astype(jnp.float32)
    for copy in loads:
        copy.wait()
    ingrad, sens = backward(
        plan, gates_ref, outgrad, x, gain, inverse,
        proj_ref, lambda h: probs_ref[h], lambda h: att_ref[:, h * hd : (h + 1) * hd],
        sens, weights, w_ref, dgated_scr, dproj_scr,
    )
    if plan["last"]:
        g_ref, sens_ref = outs
        cols, n_tiles = g_ref.shape[1], D // LANES
        for t in range(n_tiles):
            flow_scr[t] = ingrad[:, t * LANES : (t + 1) * LANES]
        flow_scr[n_tiles] = sens
        for j in range(cols):
            rows = pl.ds(j, T // cols, stride=cols)
            for t in range(n_tiles):
                g_ref[:, j, t * LANES : (t + 1) * LANES] = flow_scr[t, rows, :].astype(jnp.bfloat16)
            own = flow_scr[n_tiles, rows, :].astype(jnp.bfloat16)
            for m in range(sens_ref.shape[0]):
                sens_ref[m, :, j, :] = own[:, m * heads : (m + 1) * heads]
    elif n_out > 1:
        flow_scr[:, :D] = ingrad
        flow_scr[:, D:] = sens
        for k, out in enumerate(outs):
            out[...] = flow_scr[block(n_out, k), :].astype(jnp.bfloat16)
    else:
        outs[0][:, :D] = ingrad.astype(jnp.bfloat16)
        outs[0][:, D:] = sens.astype(jnp.bfloat16)


def call(kernel, plan, place, gates, weights, arrays, saved, outs, saves, scratch, flops):
    vmem = pl.BlockSpec(memory_space=pltpu.VMEM)
    smem = pl.BlockSpec(memory_space=pltpu.SMEM)
    plan = dict(plan, n_refs=len(weights))
    n_sems = 4 + 2 + plan["heads"]
    return pl.pallas_call(
        functools.partial(kernel, plan),
        out_shape=list(outs) + list(saves),
        in_specs=[smem, smem]
        + [vmem] * len(arrays)
        + [pl.BlockSpec(memory_space=pl.ANY)] * (len(saved) + len(weights)),
        out_specs=[vmem] * len(outs) + [HBM] * len(saves),
        scratch_shapes=[
            pltpu.VMEM((plan["n_blocks"], ROWS, LANES), jnp.bfloat16),
            pltpu.SemaphoreType.DMA((n_sems,)),
        ]
        + scratch,
        compiler_params=pltpu.CompilerParams(vmem_limit_bytes=plan["vmem"] * 2**20),
        cost_estimate=pl.CostEstimate(flops=flops, bytes_accessed=12 * 2**20, transcendentals=0),
    )(place, gates, *arrays, *saved, *weights)


def per_device(n_ha, n_wa, tokens, cotangent, w_qkv, w_out, gains, gates):
    videos, frames, rows, cols, D = tokens.shape
    layers, heads = gates.shape
    T = videos * frames * rows * cols
    width = w_qkv.shape[2]
    hidden = width // 3
    hd = hidden // heads
    tiles = ceil_to(width, LANES) // LANES
    og = ceil_to(hd, ROWS) // ROWS
    lane_tiles = D // LANES
    wide = tiles * LANES

    def flat(value):
        return jnp.swapaxes(value, 0, 1).reshape(T, D)

    idx = jnp.arange(T)
    fl = frames // n_ha * videos
    lines = [
        idx % (videos * rows * cols),
        (idx // (rows * cols)) % fl * cols + idx % cols,
        (idx // cols) % (T // (n_wa * cols)),
    ]
    biases = [jnp.where(line[:, None] == line[None, :], 0.0, -1e30).astype(jnp.float32) for line in lines]

    def swap(value, axis):
        return lax.all_to_all(value, axis, split_axis=0, concat_axis=0, tiled=True)

    home, teacher = flat(tokens), flat(cotangent)

    shard = w_qkv.shape[1]
    base = dict(T=T, D=D, heads=heads, hd=hd, tiles=tiles, og=og, square=False, pairs=0, vmem=60,
                w_tiles=(shard // ROWS, 0), o_tiles=(og, shard // ROWS * tiles))
    weights = []
    fast = n_ha == 4 and n_wa % 4 == 0 and n_wa & (n_wa - 1) == 0 and shard % ROWS == 0 and w_out.shape[1] == hd
    if fast:
        routes = Routes(n_ha, n_wa)
        ha, wa = lax.axis_index("ha"), lax.axis_index("wa")
        n_z = n_wa // 2
        spot = ha * 2 + wa % 2
        spots = [spot ^ k for k in (0, 1, 4, 5, 2, 3, 6, 7)]
        place = jnp.stack(spots + [ha ^ k for k in range(n_ha)]).astype(jnp.int32)
        rg = shard // ROWS
        quarter = -(-(rg * tiles + og * lane_tiles) // 4)

        def addresses(at):
            return dict(
                w_at=lambda g, t: at(g // rg, *divmod(t * rg + g % rg, quarter)),
                o_at=lambda h, g, t: at(h, *divmod(rg * tiles + t * og + g, quarter)),
            )

        squarewise = addresses(
            lambda slot, part, inner: ((part * 2 + slot % 2) * n_z + slot // 2) * quarter + inner
        )
        slots = jnp.stack([(wa // 2) ^ k for k in range(n_z)]).astype(jnp.int32)
        base.update(n_line=n_z * quarter, n_blocks=4 * quarter * n_wa, quarter=quarter, n_parts=4)
        plans = [dict(base, layer=layer, square=True, **squarewise) for layer in range(layers)]

        own, later = own_quarters(ha.astype(jnp.int32)[None], w_qkv, w_out, quarter)
        line = routes.line(own)
        later = hand_on(later, line)
        got, bit = {0: later}, n_z // 2
        while bit:
            got.update({k ^ bit: routes.send(got[k], wa_bits=2 * bit) for k in list(got)})
            bit //= 2
        far = [got[k] for k in range(1, n_z)]
        lines = []

        def stack_later(*squares):
            lines.extend(stacked(slots, [later] + far, 2, squares))
            return lines

        weights = [over_square(routes, line, [home, teacher] + biases + far[:1], stack_later)]

        def gather(which, before, there):
            line = hand_on(lines[which], *weights[which][3:5])
            weights.append(over_square(routes, line, before, lambda *squares: there))

    else:
        full_qkv = lax.all_gather(w_qkv, "wa", axis=1, tiled=True)
        full_out = lax.all_gather(w_out, "wa", axis=1, tiled=True)
        n_rows = D // ROWS
        n_w = n_rows * tiles
        base["w_at"] = lambda g, t: t * n_rows + g
        base["o_at"] = lambda h, g, t: n_w + (h * lane_tiles + t) * og + g
        for layer in range(layers):
            by_head = full_out[layer].reshape(heads, hd, D)
            weights.append(
                [flat_blocks(blocks_of(full_qkv[layer]), *[blocks_of(by_head[h]) for h in range(heads)])]
            )
        n_blocks = weights[0][0].shape[0]
        base.update(n_blocks=n_blocks, quarter=n_blocks, n_parts=1)
        place = jnp.zeros((1,), jnp.int32)
        plans = [dict(base, layer=layer) for layer in range(layers)]

    bf16, f32 = jnp.bfloat16, jnp.float32
    act = jax.ShapeDtypeStruct((T, D), bf16)
    loaded = jax.ShapeDtypeStruct((T, D + LANES), bf16)
    dense = 2 * T * D * (width + hidden)

    keep = [
        jax.ShapeDtypeStruct((T, wide), bf16),
        jax.ShapeDtypeStruct((heads, T, T), f32),
        jax.ShapeDtypeStruct((T, hidden), bf16),
    ]
    kept = [pltpu.VMEM(array.shape, array.dtype) for array in keep]
    grads = [pltpu.VMEM((T, heads * og * ROWS), bf16), pltpu.VMEM((T, wide), bf16)]

    def forward(layer, x, cot, pairs, to):
        return call(
            fwd_kernel, dict(plans[layer], pairs=pairs, to=to), place, gates, weights[layer],
            [x, gains, biases[layer], cot], [], [jax.ShapeDtypeStruct((2 * T, D), bf16)], keep,
            kept + grads[:1], dense,
        )

    def back(layer, x, outgrads, saved, pairs, outs, last=False):
        plan = dict(plans[layer], vmem=24, pairs=pairs, n_in=len(outgrads), n_out=len(outs), last=last)
        flow = pltpu.VMEM((D // LANES + 1, T, LANES) if last else (T, D + LANES), f32)
        return call(
            bwd_kernel, plan, place, gates, weights[layer], [x, gains] + outgrads, saved, outs, [],
            kept + grads + [flow], dense,
        )

    after_time, *saved_time = forward(0, home, teacher, 0, n_ha)
    tall = swap(after_time, "ha")
    if fast:
        gather(0, [after_time], [tall])
    after_height, *saved_height = forward(1, tall, tall, n_ha, n_wa)
    if fast:
        gather(1, [after_height], [])
    across = swap(after_height, "wa")
    (grad,) = call(
        both_kernel, dict(plans[2], pairs=n_wa, vmem=24), place, gates, weights[2],
        [across, gains, biases[2]], [], [loaded], [], kept + grads, 2 * dense,
    )
    grad = swap(grad, "wa")
    if fast:
        block = jax.ShapeDtypeStruct((T // n_ha, D + LANES), bf16)
        blocks = back(1, tall, [grad], saved_height, n_ha, [block] * n_ha)
        outgrads = [blocks[0]] + [routes.send(blocks[k], ha_bits=k) for k in range(1, n_ha)]
    else:
        (grad,) = back(1, tall, [grad], saved_height, n_ha, [loaded])
        outgrads = [swap(grad, "ha")]
    ends = [
        jax.ShapeDtypeStruct((T // cols, cols, D), bf16),
        jax.ShapeDtypeStruct((layers, T // cols, cols, heads), bf16),
    ]
    grad, sens = back(0, home, outgrads, saved_time, 0, ends, True)
    token_grad = jnp.swapaxes(grad.reshape(frames, videos, rows, cols, D), 0, 1)
    sens = sens.reshape(layers, frames, videos, rows, cols, heads)
    return (token_grad, jnp.moveaxis(sens, 2, 0))


def solution(mesh):
    spec = P(None, None, "ha", "wa", None)
    in_specs = (spec, spec, P(None, "wa", None), P(None, "wa", None), P(), P())
    out_specs = (spec, P(None, None, None, "ha", "wa", None))
    n_ha, n_wa = mesh.shape["ha"], mesh.shape["wa"]
    return jax.shard_map(
        functools.partial(per_device, n_ha, n_wa),
        mesh=mesh, in_specs=in_specs, out_specs=out_specs, check_vma=False,
    )
```
